128 devices in a mesh: dp: 16 (over x, y), tp: 8 (over z, core).
Axes of the slice: x: 4, y: 4, z: 4, core: 2. Of those that a mesh axis runs over, the one named last changes fastest.
Arguments:
- tokens: bfloat16 [2, 8192, 2048], P(None, ('dp', 'tp')), may hold values from -6 to 6
- cotangent: bfloat16 [2, 8192, 2048], P(None, ('dp', 'tp')), may hold values from -6 to 6
- mixer_gain: bfloat16 [2048], replicated, may hold values from 0.5 to 1.5
- feedforward_gain: bfloat16 [2048], replicated, may hold values from 0.5 to 1.5
- branch_weight: bfloat16 [2048, 2816], P('dp', 'tp'), may hold values from -0.125 to 0.125
- input_weight: bfloat16 [2048, 2816], P('dp', 'tp'), may hold values from -0.125 to 0.125
- output_weight: bfloat16 [2816, 2048], P('tp', 'dp'), may hold values from -0.3125 to 0.3125
- recurrence_gate: bfloat16 [176, 2816], P(None, ('tp', 'dp')), may hold values from -0.4375 to 0.4375
- input_gate: bfloat16 [176, 2816], P(None, ('tp', 'dp')), may hold values from -0.4375 to 0.4375
- conv_kernel: bfloat16 [4, 2816], P(None, ('tp', 'dp')), may hold values from -3 to 3
- conv_bias: bfloat16 [2816], P(('tp', 'dp')), may hold values from -2 to 2
- recurrence_bias: bfloat16 [2816], P(('tp', 'dp')), may hold values from -3 to 3
- input_bias: bfloat16 [2816], P(('tp', 'dp')), may hold values from -3 to 3
- decay_param: bfloat16 [2816], P(('tp', 'dp')), may hold values from 3.4 to 11.6, as said below
- gate_weight: bfloat16 [2048, 6144], P('dp', 'tp'), may hold values from -0.125 to 0.125
- up_weight: bfloat16 [2048, 6144], P('dp', 'tp'), may hold values from -0.125 to 0.125
- down_weight: bfloat16 [6144, 2048], P('tp', 'dp'), may hold values from -0.15625 to 0.15625
- doc_starts: int32 [2, 128], replicated, may hold values from 0 to 8192, as said below
Outputs:
- layer_output: bfloat16 [2, 8192, 2048], P(None, ('dp', 'tp'))
- tokens_grad: float32 [2, 8192, 2048], P(None, ('dp', 'tp'))
- mixer_gain_grad: float32 [2048], P(('tp', 'dp'))
- feedforward_gain_grad: float32 [2048], P(('tp', 'dp'))
- branch_weight_grad: float32 [2048, 2816], P('dp', 'tp')
- input_weight_grad: float32 [2048, 2816], P('dp', 'tp')
- output_weight_grad: float32 [2816, 2048], P('tp', 'dp')
- recurrence_gate_grad: float32 [176, 2816], P(None, ('tp', 'dp'))
- input_gate_grad: float32 [176, 2816], P(None, ('tp', 'dp'))
- conv_kernel_grad: float32 [4, 2816], P(None, ('tp', 'dp'))
- conv_bias_grad: float32 [2816], P(('tp', 'dp'))
- recurrence_bias_grad: float32 [2816], P(('tp', 'dp'))
- input_bias_grad: float32 [2816], P(('tp', 'dp'))
- decay_param_grad: float32 [2816], P(('tp', 'dp'))
- gate_weight_grad: float32 [2048, 6144], P('dp', 'tp')
- up_weight_grad: float32 [2048, 6144], P('dp', 'tp')
- down_weight_grad: float32 [6144, 2048], P('tp', 'dp')
The draws below stay inside these ranges and needn't reach their ends.
Inputs may be any that keep to these rules, and one draw needn't show every extreme that they name: `doc_starts`: each row lists 0, then the row's further document starts in increasing order, then entries equal to 8192 that mark unused slots; a row holds 1 to 128 documents. softplus(-decay_param) lies between 1e-5 and 0.03.
All inputs are finite; a program needn't handle non-finite values.
Results may differ from the reference program's by a relative error of at most 0.0088.
Values may be sent and summed in bfloat16 or wider, within the bound.
No kernel may reach another device: no remote copies, remote signals or barrier semaphores. Data moves between devices by JAX's collectives and lax.ppermute only.
A program may use at most 256 MiB of HBM per device.

```python
from functools import partial
import jax
import jax.numpy as jnp
from jax import lax

D = 2048
R = 2816
FF = 6144
CONV = 4
ROWS = 2
NDOC = 128
SEG = 512
BS = 176
LENGTH = 8192


def draw_decay_param(key, part):
    key = jax.random.fold_in(key, 7)
    rates = jnp.exp(jax.random.uniform(key, (R,), jnp.float32, jnp.log(1e-05), jnp.log(0.03)))
    return (-jnp.log(jnp.expm1(rates))).astype(jnp.bfloat16)


def draw_doc_starts(key, part):
    key = jax.random.fold_in(key, 3)
    subkeys = jax.random.split(key, 6)
    half_count = (NDOC - 1) // 2

    def general_row(row_key):
        count_key, pick_key = jax.random.split(row_key)
        doc_count = jax.random.randint(count_key, (), 1, NDOC + 1)
        picks = jax.random.permutation(pick_key, LENGTH - 1)[:NDOC - 1] + 1
        chosen = jnp.where(jnp.arange(NDOC - 1) < doc_count - 1, picks, LENGTH)
        return jnp.concatenate([jnp.zeros((1,), jnp.int32), jnp.sort(chosen).astype(jnp.int32)])
    rows_all = jax.vmap(general_row)(jax.random.split(subkeys[0], ROWS))
    first_count = jax.random.randint(subkeys[1], (), 0, half_count)
    last_count = jax.random.randint(subkeys[2], (), 0, half_count)
    first_picks = jax.random.permutation(subkeys[3], SEG - 1)[:half_count] + 1
    last_picks = jax.random.permutation(subkeys[4], SEG - 1)[:half_count] + (LENGTH - SEG + 1)
    rank = jnp.arange(half_count)
    later_starts = jnp.concatenate([jnp.where(rank < first_count, first_picks, LENGTH).astype(jnp.int32), jnp.where(rank < last_count, last_picks, LENGTH).astype(jnp.int32), jnp.full((NDOC - 1 - 2 * half_count,), LENGTH, jnp.int32)])
    long_row = jnp.concatenate([jnp.zeros((1,), jnp.int32), jnp.sort(later_starts)])
    chosen_row = jax.random.randint(subkeys[5], (), 0, ROWS)
    return jnp.where((jnp.arange(ROWS) == chosen_row)[:, None], long_row[None, :], rows_all).astype(jnp.int32)


def levels(key, dims, cuts, low, top_value):
    def one(axis_at, parts):
        draws = jax.random.uniform(jax.random.fold_in(jax.random.fold_in(key, 6), axis_at), (parts,), jnp.float32, low / len(cuts), top_value / len(cuts))
        return jnp.repeat(jnp.exp(draws), dims[axis_at] // parts).reshape((-1,) + (1,) * (len(dims) - axis_at - 1))

    loudness = one(*cuts[0])
    for cut in cuts[1:]:
        loudness = loudness * one(*cut)
    return loudness


def normal_values(rng, dims, scale, limit, shards=(), kind=jnp.bfloat16):
    values = jax.random.normal(rng, dims, jnp.float32) * scale
    if len(shards) > 0:
        values = levels(rng, dims, shards, -0.22, 0.18) * values
    return jnp.clip(values, min=-limit, max=limit).astype(kind)


def setup_inputs(seed: int = 0) -> dict:
    arg_keys = jax.random.split(jax.random.key(seed), 19)
    tokens = normal_values(arg_keys[0], (ROWS, LENGTH, D), 1.0, 6.0, ((1, 128),))
    cotangent = normal_values(arg_keys[1], (ROWS, LENGTH, D), 1.0, 6.0, ((1, 128),))
    mixer_gain = jnp.clip(1.0 + 0.1 * jax.random.normal(arg_keys[2], (D,), jnp.float32), 0.5, 1.5).astype(jnp.bfloat16)
    feedforward_gain = jnp.clip(1.0 + 0.1 * jax.random.normal(arg_keys[3], (D,), jnp.float32), 0.5, 1.5).astype(jnp.bfloat16)
    branch_weight = normal_values(arg_keys[4], (D, R), D ** -0.5, 0.125, ((0, 16), (1, 8)))
    input_weight = normal_values(arg_keys[5], (D, R), D ** -0.5, 0.125, ((0, 16), (1, 8)))
    output_weight = normal_values(arg_keys[6], (R, D), (R // 8) ** -0.5, 0.3125, ((0, 8), (1, 16)))
    recurrence_gate = normal_values(arg_keys[7], (BS, R), BS ** -0.5, 0.4375, ((1, 128),))
    input_gate = normal_values(arg_keys[8], (BS, R), BS ** -0.5, 0.4375, ((1, 128),))
    conv_kernel = normal_values(arg_keys[9], (CONV, R), CONV ** -0.5, 3.0, ((1, 128),))
    conv_bias = normal_values(arg_keys[10], (R,), 0.3, 2.0, ((0, 128),))
    recurrence_bias = normal_values(arg_keys[11], (R,), 0.5, 3.0, ((0, 128),))
    input_bias = normal_values(arg_keys[12], (R,), 0.5, 3.0, ((0, 128),))
    decay_param = draw_decay_param(jax.random.fold_in(arg_keys[18], 71), 0)
    gate_weight = normal_values(arg_keys[14], (D, FF), D ** -0.5, 0.125, ((0, 16), (1, 8)))
    up_weight = normal_values(arg_keys[15], (D, FF), D ** -0.5, 0.125, ((0, 16), (1, 8)))
    down_weight = normal_values(arg_keys[16], (FF, D), (FF // 4) ** -0.5, 0.15625, ((0, 8), (1, 16)))
    doc_starts = draw_doc_starts(jax.random.fold_in(arg_keys[18], 71), 0)
    return {"tokens": tokens, "cotangent": cotangent, "mixer_gain": mixer_gain, "feedforward_gain": feedforward_gain, "branch_weight": branch_weight, "input_weight": input_weight, "output_weight": output_weight, "recurrence_gate": recurrence_gate, "input_gate": input_gate, "conv_kernel": conv_kernel, "conv_bias": conv_bias, "recurrence_bias": recurrence_bias, "input_bias": input_bias, "decay_param": decay_param, "gate_weight": gate_weight, "up_weight": up_weight, "down_weight": down_weight, "doc_starts": doc_starts}


@jax.custom_vjp
def low(v):
    return lax.optimization_barrier(v.astype(jnp.bfloat16)).astype(jnp.float32)

@jax.custom_vjp
def low_back(v):
    return v

def low_keep(v):
    return (low(v), None)

def low_pass(kept, grad):
    return (grad,)

def back_keep(v):
    return (v, None)

def back_low(kept, grad):
    return (low(grad),)
low.defvjp(low_keep, low_pass)
low_back.defvjp(back_keep, back_low)
eps_norm = 1e-06
decay_power = 8.0
mult_eps = 0.001
highest = lax.Precision.HIGHEST

def matmul(left, right):
    return jnp.dot(left, right, precision=highest)

def rms_normal(values):
    return values * lax.rsqrt(lax.optimization_barrier(jnp.mean(values * values, axis=-1, keepdims=True)) + eps_norm)

def block_mix(values, weight):
    block_size = weight.shape[0]
    block_count = weight.shape[1] // block_size
    mixed_blocks = jnp.einsum('thk,khj->thj', values.reshape(-1, block_count, block_size), weight.reshape(block_size, block_count, block_size), precision=highest)
    return mixed_blocks.reshape(values.shape)

def gate_terms(conv_out, recur_pre, entry_pre, decay_param, starting):
    rate = jax.nn.softplus(-decay_param)
    decay_now = jnp.where(starting, 0.0, jnp.exp(-decay_power * rate * jax.nn.sigmoid(recur_pre)))
    scale = jnp.where(starting, 1.0, jnp.sqrt(1.0 - decay_now * decay_now + mult_eps))
    return (decay_now, scale * jax.nn.sigmoid(entry_pre) * conv_out)

def linear_pair(earlier, latter):
    return (earlier[0] * latter[0], latter[0] * earlier[1] + latter[1])

def recur_block(carry_state, pieces):
    cum_decay, cum_update = lax.associative_scan(linear_pair, pieces, axis=0)
    states = cum_update + cum_decay * carry_state[None, :]
    return (states[-1], states)

def row_forward(params, row_tokens, row_starts):
    mixer_gain, feedforward_gain, branch_weight, input_weight, output_weight, recurrence_gate, input_gate, conv_kernel, conv_bias, recurrence_bias, input_bias, decay_param, gate_weight, up_weight, down_weight = params
    gelu_tanh = partial(jax.nn.gelu, approximate=True)
    row_length = row_tokens.shape[0]
    normed_one = low(rms_normal(row_tokens) * mixer_gain)
    branch_pre = low_back(matmul(normed_one, branch_weight))
    conv_in = low_back(matmul(normed_one, input_weight))
    keep = 1.0 - row_starts
    keep_padded = jnp.concatenate([jnp.ones((CONV - 1,), jnp.float32), keep])
    extended = jnp.concatenate([jnp.zeros((CONV - 1, conv_in.shape[1]), jnp.float32), conv_in], axis=0)
    valid_mask = jnp.ones((row_length,), jnp.float32)
    conv_out = jnp.zeros_like(conv_in) + conv_bias
    for tap_index in range(CONV):
        if tap_index > 0:
            valid_mask = valid_mask * keep_padded[CONV - tap_index:CONV - tap_index + row_length]
        conv_out = conv_out + conv_kernel[tap_index] * extended[CONV - 1 - tap_index:CONV - 1 - tap_index + row_length] * valid_mask[:, None]
    conv_low = low(conv_out)
    recur_pre = low_back(block_mix(conv_low, recurrence_gate) + recurrence_bias)
    entry_pre = low_back(block_mix(conv_low, input_gate) + input_bias)
    decay_now, update = gate_terms(conv_out, recur_pre, entry_pre, decay_param, row_starts[:, None] > 0.5)
    block_total = row_length // SEG
    unit_count = conv_in.shape[1]
    last_state, states = lax.scan(jax.checkpoint(recur_block), jnp.zeros((unit_count,), jnp.float32), (decay_now.reshape(block_total, SEG, unit_count), update.reshape(block_total, SEG, unit_count)))
    states = states.reshape(row_length, unit_count)
    mixer_in = low(states * gelu_tanh(branch_pre))
    residual = row_tokens + low_back(matmul(mixer_in, output_weight))
    normed_two = low(rms_normal(residual) * feedforward_gain)
    gate_pre = low_back(matmul(normed_two, gate_weight))
    up_pre = low_back(matmul(normed_two, up_weight))
    hidden = low(gelu_tanh(gate_pre) * up_pre)
    return residual + low_back(matmul(hidden, down_weight))

def reference(tokens, cotangent, mixer_gain, feedforward_gain, branch_weight, input_weight, output_weight, recurrence_gate, input_gate, conv_kernel, conv_bias, recurrence_bias, input_bias, decay_param, gate_weight, up_weight, down_weight, doc_starts):
    positions = jnp.arange(LENGTH, dtype=jnp.int32)
    row_starts = jnp.any(doc_starts[:, :, None] == positions[None, None, :], axis=1).astype(jnp.float32)
    params = tuple((weight_item.astype(jnp.float32) for weight_item in (mixer_gain, feedforward_gain, branch_weight, input_weight, output_weight, recurrence_gate, input_gate, conv_kernel, conv_bias, recurrence_bias, input_bias, decay_param, gate_weight, up_weight, down_weight)))

    def forward(token_values, *weights):

        def one_row(row_pair):
            return row_forward(weights, row_pair[0], row_pair[1])
        return lax.map(jax.checkpoint(one_row), (token_values, row_starts))
    outputs, pullback = jax.vjp(forward, tokens.astype(jnp.float32), *params)
    grads = pullback(cotangent.astype(jnp.float32))
    return (outputs.astype(jnp.bfloat16), grads[0], grads[1], grads[2], grads[3], grads[4], grads[5], grads[6], grads[7], grads[8], grads[9], grads[10], grads[11], grads[12], grads[13], grads[14], grads[15])
```

```python
from functools import partial

import jax
import jax.numpy as jnp
from jax import lax
from jax.experimental import pallas as pl
from jax.experimental.pallas import tpu as pltpu
from jax.sharding import Mesh
from jax.sharding import PartitionSpec as P

eps_norm = 1e-06
decay_power = 8.0
mult_eps = 0.001
gelu_scale = 0.7978845608028654
gelu_cubic = 0.044715
lanes = 128
f32 = jnp.float32
bf16 = jnp.bfloat16


no_cost = pl.CostEstimate(flops=0, bytes_accessed=0, transcendentals=0)


def up_to(count, step):
    return -(-count // step) * step


def widen(values, width, axis):
    pads = [(0, 0)] * values.ndim
    pads[axis] = (0, width - values.shape[axis])
    return jnp.pad(values, pads)


def rms_unit(values):
    inverse = lax.rsqrt(jnp.mean(values * values, axis=-1, keepdims=True) + eps_norm)
    return (values * inverse, inverse)


def norm_back(grad_normed, unit_values, inverse, gain):
    scaled = grad_normed * gain
    return inverse * (scaled - unit_values * jnp.mean(scaled * unit_values, axis=-1, keepdims=True))


def gelu_parts(values):
    squared = values * values
    tanh_value = jnp.tanh(gelu_scale * values * (1.0 + gelu_cubic * squared))
    half = 0.5 * (1.0 + tanh_value)
    slope = half + 0.5 * values * (1.0 - tanh_value * tanh_value) * gelu_scale * (
        1.0 + 3.0 * gelu_cubic * squared
    )
    return (values * half, slope)


def dot(left, right, left_axis=1, right_axis=0):
    return lax.dot_general(
        left, right, (((left_axis,), (right_axis,)), ((), ())), preferred_element_type=f32
    )


def gather_small(value, axis):
    peers = lax.axis_size(axis)
    return lax.all_to_all(jnp.broadcast_to(value[None], (peers,) + value.shape), axis, 0, 0)


def scatter_sum(value, axis):
    return jnp.sum(lax.all_to_all(value, axis, 0, 0).astype(f32), axis=0)


def tie(value, *before):
    return lax.optimization_barrier((value,) + before)[0]


def tie_all(values, *before):
    return lax.optimization_barrier((values,) + before)[0]


def swap_cores(value):
    return lax.ppermute(value, "core", [(0, 1), (1, 0)])


def turn(value, by):
    count = lax.axis_size("z")
    return lax.ppermute(value, "z", [(i, (i + by) % count) for i in range(count)])


def ring_near(value):
    return (value, turn(value, 1), turn(value, -1), swap_cores(value))


def ring_far(near):
    value, below, above, other = near
    half = value.shape[0] // 2
    far_low, far_high = turn(below[:half], 1), turn(above[half:], -1)
    swapped = [swap_cores(part) for part in (above, below, far_low, far_high)]
    return [value, above, below, far_low, far_high, other] + swapped


def ring_places(rows):
    half = rows // 2
    places = [(0, 0, rows), (1, 0, rows), (3, 0, rows), (2, 0, half), (2, half, half)]
    return [(by, side, at, size) for side in range(2) for by, at, size in places]


def ring_whole(pieces):
    count = lax.axis_size("z")
    z, core = lax.axis_index("z"), lax.axis_index("core")
    rows, columns = pieces[0].shape
    whole = jnp.zeros((2 * count * rows, columns), pieces[0].dtype)
    for piece, (by, side, first, _) in zip(pieces, ring_places(rows)):
        span = lax.rem(z + by, count) * 2 + (1 - core if side else core)
        whole = lax.dynamic_update_slice(whole, piece, (span * rows + first, 0))
    return whole


def ring_scatter(part, kind, first=None, second=None):
    count = lax.axis_size("z")
    z = lax.axis_index("z")
    half = part.shape[1] // 2

    def piece(by):
        return lax.dynamic_index_in_dim(part, lax.rem(z + by, count), 0, keepdims=False)

    def step(low, high, work):
        if work is None:
            return turn(low, 1), turn(high, -1)
        operand, function = work
        low, high, operand = lax.optimization_barrier((low, high, operand))
        below, above = turn(low, 1), turn(high, -1)
        below, above, _ = lax.optimization_barrier((below, above, function(operand)))
        return below, above

    far = piece(2).astype(kind)
    from_below, from_above = step(far[:half], far[half:], first)
    ahead, behind = piece(1), piece(3)
    ahead = jnp.concatenate([ahead[:half] + from_below.astype(f32), ahead[half:]], axis=0)
    behind = jnp.concatenate([behind[:half], behind[half:] + from_above.astype(f32)], axis=0)
    below, above = step(ahead.astype(kind), behind.astype(kind), second)
    return piece(0) + below.astype(f32) + above.astype(f32)


def sum_cores(send, keep):
    part = keep.astype(f32) + swap_cores(send.astype(bf16)).astype(f32)
    return part.reshape(lax.axis_size("z"), -1, part.shape[-1])


class Sizes:
    def __init__(self, rows, seg, spans, width, conv_width):
        self.rows, self.seg, self.spans = rows, seg, spans
        self.width, self.conv_width = width, conv_width
        self.length = seg * spans
        self.tokens = rows * self.length
        self.tiles = seg // 8

    def chunk(self, span, row):
        return pl.ds(pl.multiple_of(span * (self.rows * self.seg) + row * self.seg, self.seg), self.seg)

    def tile(self, span, row, tile):
        start = span * (self.rows * self.seg) + row * self.seg + tile * 8
        return pl.ds(pl.multiple_of(start, 8), 8)


def tile_scan(decay, value, backward):
    place = lax.broadcasted_iota(jnp.int32, decay.shape, 0)
    for step in (1, 2, 4):
        if backward:
            fits, turn = (place < 8 - step, 8 - step)
        else:
            fits, turn = (place >= step, step)
        other_decay = jnp.where(fits, pltpu.roll(decay, turn, 0), 1.0)
        other_value = jnp.where(fits, pltpu.roll(value, turn, 0), 0.0)
        value = value + decay * other_value
        decay = decay * other_decay
    return (decay, value)


def run_scan(sizes, decay_ref, value_ref, product_ref, total_ref, last_ref, backward):
    edge = 0 if backward else 7
    shape = (8, sizes.width)

    def span_step(index, carried):
        span = sizes.spans - 1 - index if backward else index
        carried = list(carried)
        for step in range(sizes.tiles):
            tile = sizes.tiles - 1 - step if backward else step
            for row in range(sizes.rows):
                at = sizes.tile(span, row, tile)
                decay, value = tile_scan(decay_ref[at, :], value_ref[at, :], backward)
                product, total = carried[2 * row], carried[2 * row + 1]
                total = value + decay * total
                product = decay * product
                product_ref[at, :] = product
                total_ref[at, :] = total
                carried[2 * row] = jnp.broadcast_to(product[edge : edge + 1], shape)
                carried[2 * row + 1] = jnp.broadcast_to(total[edge : edge + 1], shape)
        return tuple(carried)

    first = (jnp.ones(shape, f32), jnp.zeros(shape, f32)) * sizes.rows
    carried = lax.fori_loop(0, sizes.spans, span_step, first)
    last_ref[...] = jnp.zeros(last_ref.shape, f32)
    for row in range(sizes.rows):
        last_ref[row : row + 1, :] = carried[2 * row][:1]
        last_ref[sizes.rows + row : sizes.rows + row + 1, :] = carried[2 * row + 1][:1]


def from_others(sizes, index_ref, all_ref, peers, backward):
    mine = index_ref[0]
    entering = [jnp.zeros((1, sizes.width), f32) for _ in range(sizes.rows)]
    for step in range(peers - 1):
        peer = peers - 1 - step if backward else step
        ahead = peer > mine if backward else peer < mine
        for row in range(sizes.rows):
            product = all_ref[peer, row : row + 1, :]
            total = all_ref[peer, sizes.rows + row : sizes.rows + row + 1, :]
            entering[row] = jnp.where(ahead, total + product * entering[row], entering[row])
    return entering


def gates_kernel(
    sizes,
    conv_in,
    tail,
    masks,
    table,
    params,
    conv_out,
    conv_low,
    decay,
    recur,
    entry,
    product,
    total,
    last,
    extended,
    mixed,
    update,
):
    seg, taps, width = sizes.seg, sizes.conv_width, sizes.width
    for row in range(sizes.rows):
        extended[row, 0:8, :] = tail[row * 8 : row * 8 + 8, :]

    def conv_step(span, carried):
        for row in range(sizes.rows):
            at = sizes.chunk(span, row)
            start = pl.multiple_of(span * seg, seg)
            extended[row, pl.ds(start + 8, seg), :] = conv_in[at, :]
            window = extended[row, pl.ds(start, seg + 8), :]
            valid = masks[at, :]
            value = params[taps : taps + 1, :] + params[0:1, :] * window[8:]
            for tap in range(1, taps):
                value = value + params[tap : tap + 1, :] * window[8 - tap : 8 - tap + seg] * (
                    valid[:, tap : tap + 1]
                )
            conv_out[at, :] = value
            conv_low[at, :] = value.astype(bf16)
        return carried

    lax.fori_loop(0, sizes.spans, conv_step, 0)
    part = 256

    def mix_step(index, carried):
        at = pl.ds(pl.multiple_of(index * part, part), part)
        mixed[at, :] = dot(conv_low[at, :], table[...], 1, 1)
        return carried

    lax.fori_loop(0, sizes.tokens // part, mix_step, 0)
    step_rows = 32
    recur_bias = params[taps + 1 : taps + 2, :]
    entry_bias = params[taps + 2 : taps + 3, :]
    rate = params[taps + 3 : taps + 4, :] * (-decay_power)

    def gate_step(index, carried):
        at = pl.ds(pl.multiple_of(index * step_rows, step_rows), step_rows)
        starting = jnp.broadcast_to(masks[at, :][:, 0:1], (step_rows, width)) > 0.5
        recur_now = jax.nn.sigmoid(mixed[at, :width] + recur_bias)
        entry_now = jax.nn.sigmoid(mixed[at, width:] + entry_bias)
        decay_now = jnp.where(starting, 0.0, jnp.exp(rate * recur_now))
        scale = jnp.where(starting, 1.0, jnp.sqrt(1.0 - decay_now * decay_now + mult_eps))
        recur[at, :] = recur_now
        entry[at, :] = entry_now
        decay[at, :] = decay_now
        update[at, :] = scale * entry_now * conv_out[at, :]
        return carried

    lax.fori_loop(0, sizes.tokens // step_rows, gate_step, 0)
    run_scan(sizes, decay, update, product, total, last, False)


def states_kernel(
    sizes, peers, index, gathered, product, total, branch_pre, mixer_in, states, entered
):
    entering = from_others(sizes, index, gathered, peers, False)
    entered[...] = jnp.zeros(entered.shape, f32)
    for row in range(sizes.rows):
        entered[row : row + 1, :] = entering[row]

    def state_step(span, carried):
        for row in range(sizes.rows):
            at = sizes.chunk(span, row)
            state = total[at, :] + product[at, :] * entering[row]
            states[at, :] = state
            mixer_in[at, :] = (state * gelu_parts(branch_pre[at, :])[0]).astype(bf16)
        return carried

    lax.fori_loop(0, sizes.spans, state_step, 0)


def reverse_kernel(
    sizes,
    out_at,
    place,
    branch_pre,
    states,
    decay,
    weights_hbm,
    *refs,
):
    places = ring_places(sizes.rows * sizes.seg)
    pieces, refs = refs[: len(places)], refs[len(places) :]
    grad_branch, grad_branch_pre, grad_states, product, total, last = refs[:6]
    scaled, grad_mixer, weights, sem = refs[6:]
    width = sizes.width
    copy = pltpu.make_async_copy(
        weights_hbm.at[:, out_at * width : (out_at + 1) * width], weights, sem
    )
    copy.start()
    z, core = place[0], place[1]
    rows = sizes.rows * sizes.seg
    for piece, (by, side, first, count) in zip(pieces, places):
        span = lax.rem(z + by, sizes.spans // 2) * 2 + (1 - core if side else core)
        at = pl.ds(pl.multiple_of(span * rows + first, sizes.seg), count)
        grad_branch[at, :] = piece[...]
    copy.wait()
    part = 256

    def mix_step(index, carried):
        at = pl.ds(pl.multiple_of(index * part, part), part)
        grad_mixer[at, :] = dot(grad_branch[at, :], weights[...])
        return carried

    lax.fori_loop(0, sizes.tokens // part, mix_step, 0)

    def gelu_step(span, carried):
        for row in range(sizes.rows):
            at = sizes.chunk(span, row)
            grad = grad_mixer[at, :]
            act, slope = gelu_parts(branch_pre[at, :])
            grad_state = grad * act
            grad_states[at, :] = grad_state
            scaled[at, :] = decay[at, :] * grad_state
            grad_branch_pre[at, :] = (grad * states[at, :] * slope).astype(bf16)
        return carried

    lax.fori_loop(0, sizes.spans, gelu_step, 0)
    run_scan(sizes, decay, scaled, product, total, last, True)


def gates_back_kernel(
    sizes,
    peers,
    index,
    gathered,
    product,
    total,
    grad_states,
    states,
    entered,
    decay,
    recur,
    entry,
    conv_out,
    conv_in,
    tail,
    masks,
    table,
    params,
    grad_branch_pre,
    grad_gates,
    grad_front,
    ends,
    head,
    sums,
    later,
    before,
    grad_conv,
    extended,
    masks_ext,
):
    seg, taps, width = sizes.seg, sizes.conv_width, sizes.width
    length = sizes.length
    entering = from_others(sizes, index, gathered, peers, True)
    for row in range(sizes.rows):
        later[row, length : length + 8, :] = jnp.broadcast_to(entering[row], (8, width))
        before[row, 0:8, :] = jnp.broadcast_to(entered[row : row + 1, :], (8, width))
        extended[row, 0:8, :] = tail[row * 8 : row * 8 + 8, :]
        for edge in (0, length + 8):
            grad_conv[row, edge : edge + 8, :] = jnp.zeros((8, width), f32)
            masks_ext[row, edge : edge + 8, :] = jnp.zeros((8, masks_ext.shape[2]), f32)

    def place_step(span, carried):
        start = pl.multiple_of(span * seg, seg)
        for row in range(sizes.rows):
            at = sizes.chunk(span, row)
            later[row, pl.ds(start, seg), :] = total[at, :] + product[at, :] * entering[row]
            before[row, pl.ds(start + 8, seg), :] = states[at, :]
            extended[row, pl.ds(start + 8, seg), :] = conv_in[at, :]
            masks_ext[row, pl.ds(start + 8, seg), :] = masks[at, :]
        return carried

    lax.fori_loop(0, sizes.spans, place_step, 0)
    rate = params[taps + 3 : taps + 4, :] * (-decay_power)

    def fold(values):
        return jnp.sum(values.reshape(seg // 8, 8, width), axis=0)

    def gate_step(span, carried):
        start = pl.multiple_of(span * seg, seg)
        rate_sum, recur_sum, entry_sum = carried
        for row in range(sizes.rows):
            at = sizes.chunk(span, row)
            starting = jnp.broadcast_to(masks[at, :][:, 0:1], (seg, width)) > 0.5
            carried_now = grad_states[at, :] + later[row, pl.ds(start, seg + 8), :][1 : seg + 1]
            state_before = before[row, pl.ds(start, seg + 8), :][7 : seg + 7]
            decay_now, recur_now, entry_now = (decay[at, :], recur[at, :], entry[at, :])
            conv_now = conv_out[at, :]
            scale = jnp.where(starting, 1.0, jnp.sqrt(1.0 - decay_now * decay_now + mult_eps))
            grad_direct = carried_now * scale * entry_now
            grad_entry = carried_now * scale * conv_now * entry_now * (1.0 - entry_now)
            grad_scale = carried_now * entry_now * conv_now
            grad_decay = carried_now * state_before - grad_scale * decay_now / scale
            grad_power = jnp.where(starting, 0.0, grad_decay * decay_now)
            grad_recur = grad_power * rate * recur_now * (1.0 - recur_now)
            recur_low = grad_recur.astype(bf16)
            entry_low = grad_entry.astype(bf16)
            grad_gates[at, :width] = recur_low
            grad_gates[at, width:] = entry_low
            grad_conv[row, pl.ds(start + 8, seg), :] = grad_direct
            rate_sum = rate_sum + fold(grad_power * recur_now)
            recur_sum = recur_sum + fold(recur_low.astype(f32))
            entry_sum = entry_sum + fold(entry_low.astype(f32))
        return (rate_sum, recur_sum, entry_sum)

    empty = jnp.zeros((8, width), f32)
    rate_sum, recur_sum, entry_sum = lax.fori_loop(
        0, sizes.spans, gate_step, (empty, empty, empty)
    )

    def mix_step(span, carried):
        start = pl.multiple_of(span * seg, seg)
        whole = pl.ds(pl.multiple_of(span * (sizes.rows * seg), seg), sizes.rows * seg)
        mixed = dot(grad_gates[whole, :], table[...], 1, 0)
        for row in range(sizes.rows):
            place = pl.ds(start + 8, seg)
            grad_conv[row, place, :] = (
                grad_conv[row, place, :] + mixed[row * seg : (row + 1) * seg]
            )
        return carried

    lax.fori_loop(0, sizes.spans, mix_step, 0)

    def conv_step(span, carried):
        start = pl.multiple_of(span * seg, seg)
        carried = list(carried)
        for row in range(sizes.rows):
            at = sizes.chunk(span, row)
            grad_window = grad_conv[row, pl.ds(start + 8, seg + 8), :]
            mask_window = masks_ext[row, pl.ds(start + 8, seg + 8), :]
            conv_window = extended[row, pl.ds(start, seg + 8), :]
            value = params[0:1, :] * grad_window[:seg]
            carried[0] = carried[0] + fold(grad_window[:seg] * conv_window[8:])
            carried[taps] = carried[taps] + fold(grad_window[:seg])
            for tap in range(1, taps):
                weighted = grad_window * mask_window[:, tap : tap + 1]
                value = value + params[tap : tap + 1, :] * weighted[tap : tap + seg]
                carried[tap] = carried[tap] + fold(
                    weighted[:seg] * conv_window[8 - tap : 8 - tap + seg]
                )
            grad_front[at, :width] = value.astype(bf16)
            grad_front[at, width:] = grad_branch_pre[at, :]

            @pl.when(span == sizes.spans - 1)
            def _():
                ends[row * 8 : row * 8 + 8, :] = value[seg - 8 :]

        return tuple(carried)

    folded = lax.fori_loop(0, sizes.spans, conv_step, (empty,) * (taps + 1))
    for row in range(sizes.rows):
        grad_window = grad_conv[row, 0:16, :]
        mask_window = masks_ext[row, 0:16, :]
        value = jnp.zeros((8, width), f32)
        for tap in range(1, taps):
            weighted = grad_window * mask_window[:, tap : tap + 1]
            value = value + params[tap : tap + 1, :] * weighted[tap : tap + 8]
        head[row * 8 : row * 8 + 8, :] = value
    for place, part in enumerate(folded + (recur_sum, entry_sum, rate_sum)):
        sums[place : place + 1, :] = jnp.sum(part, axis=0, keepdims=True)


def call(kernel, outs, scratch, *operands, scalars=0, anywhere=(), sems=()):
    vmem = pl.BlockSpec(memory_space=pltpu.VMEM)
    in_specs = [pl.BlockSpec(memory_space=pltpu.SMEM)] * scalars
    in_specs += [vmem] * (len(operands) - scalars)
    for index in anywhere:
        in_specs[index] = pl.BlockSpec(memory_space=pl.ANY)
    return pl.pallas_call(
        kernel,
        out_shape=[jax.ShapeDtypeStruct(shape, kind) for shape, kind in outs],
        in_specs=in_specs,
        out_specs=[vmem] * len(outs),
        scratch_shapes=[pltpu.VMEM(shape, kind) for shape, kind in scratch] + list(sems),
        cost_estimate=no_cost,
        compiler_params=pltpu.CompilerParams(vmem_limit_bytes=48 * 1024 * 1024),
    )(*operands)


def product_kernel(at, core, x_hbm, weights_hbm, out_hbm, x, weights, out, in_sem, out_sem):
    mine = core[0]
    spans, span, depth = x.shape
    slots, rows, columns = out.shape
    steps = weights.shape[0] // columns

    def weight_copy(index):
        place = pl.ds(pl.multiple_of(index * columns, columns), columns)
        return pltpu.make_async_copy(
            weights_hbm.at[place, at * depth : (at + 1) * depth],
            weights.at[place],
            in_sem.at[index + 1],
        )

    def out_copy(index):
        place = pl.ds(pl.multiple_of(index * columns, columns), columns)
        return pltpu.make_async_copy(
            out.at[index % slots], out_hbm.at[:, place], out_sem.at[index % slots]
        )

    x_copy = pltpu.make_async_copy(x_hbm.at[:, mine], x, in_sem.at[0])
    x_copy.start()
    for index in range(steps):
        weight_copy(index).start()
    x_copy.wait()

    def step(index, carried):
        weight_copy(index).wait()

        @pl.when(index >= slots)
        def _():
            out_copy(index - slots).wait()

        place = pl.ds(pl.multiple_of(index * columns, columns), columns)
        value = dot(x[...].reshape(rows, depth), weights[place, :], 1, 1)
        out[index % slots] = value.astype(out.dtype)
        out_copy(index).start()
        return carried

    lax.fori_loop(0, steps, step, 0)
    for index in range(steps - slots, steps):
        out_copy(index).wait()


def core_product(core, values, weights, at, kind):
    spans = lax.axis_size("z")
    depth, model = values.shape[1], weights.shape[0]
    span = values.shape[0] // (2 * spans)
    columns = 512
    anywhere = pl.BlockSpec(memory_space=pl.ANY)
    return pl.pallas_call(
        partial(product_kernel, at),
        out_shape=jax.ShapeDtypeStruct((spans * span, model), kind),
        in_specs=[pl.BlockSpec(memory_space=pltpu.SMEM), anywhere, anywhere],
        out_specs=anywhere,
        scratch_shapes=[
            pltpu.VMEM((spans, span, depth), bf16),
            pltpu.VMEM((model, depth), bf16),
            pltpu.VMEM((2, spans * span, columns), kind),
            pltpu.SemaphoreType.DMA((model // columns + 1,)),
            pltpu.SemaphoreType.DMA((2,)),
        ],
        cost_estimate=no_cost,
        compiler_params=pltpu.CompilerParams(vmem_limit_bytes=60 * 1024 * 1024),
    )(
        jnp.reshape(core, (1,)).astype(jnp.int32),
        values.reshape(spans, 2, span, depth),
        weights,
    )


def core_products(values, weights, at):
    core = lax.axis_index("core")
    return (
        core_product(1 - core, values, weights, at, bf16),
        core_product(core, values, weights, at, f32),
    )


def feed_kernel(
    spans, aliased, core, x_hbm, grad_hbm, weights_hbm, *refs
):
    refs = refs[aliased:]
    (part_hbm, hidden_hbm, both_hbm, x, grad, weights, pre, hidden, both, part) = refs[:10]
    in_sem, weight_sem, out_sem, part_sem = refs[10:]
    mine = core[0]
    rows, model = spans * x.shape[1], x.shape[2]
    inner = grad.shape[2]
    span = x.shape[1]
    copies = [
        pltpu.make_async_copy(x_hbm.at[:, mine], x, in_sem.at[0]),
        pltpu.make_async_copy(grad_hbm.at[:, mine], grad, in_sem.at[1]),
    ]
    columns = weights.shape[2]
    count = 2 * inner // columns

    def weight_copy(index):
        at = pl.ds(pl.multiple_of(index * columns, columns), columns)
        return pltpu.make_async_copy(
            weights_hbm.at[:, at], weights.at[index], weight_sem.at[index]
        )

    copies[0].start()
    for index in range(count):
        weight_copy(index).start()
    copies[1].start()
    copies[0].wait()

    def forward_step(index, carried):
        weight_copy(index).wait()
        at = pl.ds(pl.multiple_of(index * columns, columns), columns)
        pre[:, at] = dot(x[...].reshape(rows, model), weights[index])
        return carried

    lax.fori_loop(0, count, forward_step, 0)
    copies[1].wait()
    step_rows = 32
    steps = span // step_rows

    def act_step(index, carried):
        at = pl.ds(pl.multiple_of(index * step_rows, step_rows), step_rows)
        z = index // steps
        inside = pl.ds(pl.multiple_of((index % steps) * step_rows, step_rows), step_rows)
        act, slope = gelu_parts(pre[at, :inner])
        up = pre[at, inner:]
        grad_now = grad[z, inside, :]
        hidden[z, inside, :] = (act * up).astype(bf16)
        both[z, inside, :inner] = (grad_now * up * slope).astype(bf16)
        both[z, inside, inner:] = (grad_now * act).astype(bf16)
        return carried

    lax.fori_loop(0, spans * steps, act_step, 0)
    outs = [
        pltpu.make_async_copy(hidden, hidden_hbm.at[:, mine], out_sem.at[0]),
        pltpu.make_async_copy(both, both_hbm.at[:, mine], out_sem.at[1]),
    ]
    for out in outs:
        out.start()
    width = part.shape[2]

    def part_copy(index, slot):
        at = pl.ds(pl.multiple_of(index * width, width), width)
        return pltpu.make_async_copy(part.at[slot], part_hbm.at[:, at], part_sem.at[slot])

    def back_step(index, carried):
        slot = index % 2

        @pl.when(index >= 2)
        def _():
            part_copy(index - 2, slot).wait()

        at = pl.ds(pl.multiple_of(index * width, width), width)
        total = jnp.zeros((rows, width), f32)
        for piece in range(count):
            total = total + dot(
                both[:, :, piece * columns : (piece + 1) * columns].reshape(rows, columns),
                weights[piece, at, :],
                1,
                1,
            )
        part[slot] = total.astype(part.dtype)
        part_copy(index, slot).start()
        return carried

    last = model // width
    lax.fori_loop(0, last, back_step, 0)
    for index in (last - 2, last - 1):
        part_copy(index, index % 2).wait()
    for out in outs:
        out.wait()


def feed_forward(core, flat, grad_hidden, weights, part_kind, given):
    spans = lax.axis_size("z")
    model, inner = flat.shape[1], grad_hidden.shape[1]
    span = flat.shape[0] // (2 * spans)
    rows = spans * span
    columns, width = 512, 512
    anywhere = pl.BlockSpec(memory_space=pl.ANY)
    return pl.pallas_call(
        partial(feed_kernel, spans, len(given)),
        out_shape=[
            jax.ShapeDtypeStruct((rows, model), part_kind),
            jax.ShapeDtypeStruct((spans, 2, span, inner), bf16),
            jax.ShapeDtypeStruct((spans, 2, span, 2 * inner), bf16),
        ],
        in_specs=[pl.BlockSpec(memory_space=pltpu.SMEM)] + [anywhere] * (3 + len(given)),
        out_specs=[anywhere] * 3,
        scratch_shapes=[
            pltpu.VMEM((spans, span, model), bf16),
            pltpu.VMEM((spans, span, inner), f32),
            pltpu.VMEM((2 * inner // columns, model, columns), bf16),
            pltpu.VMEM((rows, 2 * inner), f32),
            pltpu.VMEM((spans, span, inner), bf16),
            pltpu.VMEM((spans, span, 2 * inner), bf16),
            pltpu.VMEM((2, rows, width), part_kind),
            pltpu.SemaphoreType.DMA((2,)),
            pltpu.SemaphoreType.DMA((2 * inner // columns,)),
            pltpu.SemaphoreType.DMA((2,)),
            pltpu.SemaphoreType.DMA((2,)),
        ],
        input_output_aliases={4: 1, 5: 2} if given else {},
        cost_estimate=no_cost,
        compiler_params=pltpu.CompilerParams(vmem_limit_bytes=60 * 1024 * 1024),
    )(
        jnp.reshape(core, (1,)).astype(jnp.int32),
        flat.reshape(spans, 2, span, model),
        grad_hidden.reshape(spans, 2, span, inner),
        weights,
        *given,
    )


def weight_kernel(with_sums, filled, left, right, *refs):
    value = dot(left[...], right[...], 0, 0)
    if with_sums:
        weight, (out, sums) = refs[0], refs[1 + filled :]
        product = value * weight[...].astype(f32)
        sums[...] = sum(
            product[:, start : start + lanes] for start in range(0, product.shape[1], lanes)
        )
    else:
        out = refs[filled]
    out[...] = value.astype(bf16)


def weight_grad(left, right, width, total, place=0, given=None, weight=None, weight_at=0, blocks=0):
    depth, rows = left.shape
    block = 512 if width > 1024 else 1024
    blocks = blocks or right.shape[1] // width
    in_specs = [
        pl.BlockSpec((depth, block), lambda j, i: (0, i)),
        pl.BlockSpec((depth, width), lambda j, i: (0, j)),
    ]
    operands = [left, right]
    out_shape = [jax.ShapeDtypeStruct((rows, total), bf16)]
    out_specs = [pl.BlockSpec((block, width), lambda j, i: (i, j + place))]
    if weight is not None:
        in_specs.append(pl.BlockSpec((block, width), lambda j, i: (i, weight_at)))
        operands.append(weight)
        out_shape.append(jax.ShapeDtypeStruct((rows, lanes), f32))
        out_specs.append(pl.BlockSpec((block, lanes), lambda j, i: (i, 0)))
    aliases = {}
    if given is not None:
        aliases = {len(operands): 0}
        in_specs.append(pl.BlockSpec(memory_space=pl.ANY))
        operands.append(given)
    found = pl.pallas_call(
        partial(weight_kernel, weight is not None, given is not None),
        grid=(blocks, rows // block),
        out_shape=out_shape,
        in_specs=in_specs,
        out_specs=out_specs,
        input_output_aliases=aliases,
        cost_estimate=no_cost,
        compiler_params=pltpu.CompilerParams(vmem_limit_bytes=40 * 1024 * 1024),
    )(*operands)
    return found if weight is not None else found[0]


def shards(
    tokens,
    cotangent,
    mixer_gain,
    feedforward_gain,
    branch_weight,
    input_weight,
    output_weight,
    recurrence_gate,
    input_gate,
    conv_kernel,
    conv_bias,
    recurrence_bias,
    input_bias,
    decay_param,
    gate_weight,
    up_weight,
    down_weight,
    doc_starts,
):
    spans = lax.axis_size("z") * 2
    core = lax.axis_index("core")
    dp_index = lax.axis_index("dp")
    peers = lax.axis_size("dp")
    rows, seg, model = tokens.shape
    units = branch_weight.shape[1]
    width = up_to(units, lanes)
    hidden_width = gate_weight.shape[1]
    taps = conv_kernel.shape[0]
    block = recurrence_gate.shape[0]
    blocks = units // block
    share = units // peers
    sizes = Sizes(rows, seg, spans, width, taps)
    own, length, block_tokens = rows * seg, sizes.length, sizes.tokens
    depth = model // peers

    mine = jnp.reshape(dp_index, (1,)).astype(jnp.int32)

    x_own = tokens.reshape(own, model).astype(f32)
    unit_one, inverse_one = rms_unit(x_own)
    gain_one = mixer_gain.astype(f32)
    gain_two = feedforward_gain.astype(f32)
    normed_one = (unit_one * gain_one).astype(bf16)
    one_near = ring_near(normed_one)
    one_far = ring_far(one_near)

    small = jnp.concatenate(
        [
            recurrence_gate,
            input_gate,
            conv_kernel,
            conv_bias[None],
            recurrence_bias[None],
            input_bias[None],
            decay_param[None],
        ],
        axis=0,
    ).T
    small_width = up_to(small.shape[1], lanes)
    small_rows = up_to(share, 8)
    small_all = gather_small(widen(widen(small, small_width, 1), small_rows, 0), "dp")
    small_all = small_all[:, :share].reshape(units, small_width)
    front_weights = lax.all_gather(
        jnp.concatenate(
            [
                widen(input_weight, width, 1),
                widen(branch_weight, width, 1),
                widen(output_weight.T, width, 1),
            ],
            axis=1,
        ),
        "dp",
        axis=0,
        tiled=True,
    )
    flat_one = ring_whole(one_far)
    cot_near = ring_near(tie(cotangent.reshape(own, model), flat_one))
    back_weights = lax.all_gather(
        jnp.concatenate(tie_all((gate_weight, up_weight, down_weight.T), one_near), axis=1),
        "dp",
        axis=0,
        tiled=True,
    )
    input_matrix = front_weights[:, :width]
    branch_matrix = front_weights[:, width : 2 * width]
    gate_up = back_weights[:, : 2 * hidden_width]
    down_turned = back_weights[:, 2 * hidden_width :]
    def diagonal(turned):
        lines = [
            jnp.pad(
                turned[h * block : (h + 1) * block],
                ((0, 0), (h * block, width - (h + 1) * block)),
            )
            for h in range(blocks)
        ]
        return widen(jnp.concatenate(lines, axis=0), width, 0)

    table = jnp.concatenate(
        [diagonal(small_all[:, :block]), diagonal(small_all[:, block : 2 * block])], axis=0
    )
    vectors = widen(small_all[:, 2 * block : 2 * block + taps + 4].astype(f32).T, width, 1)
    decay_values = vectors[taps + 3]
    params = widen(
        jnp.concatenate([vectors[: taps + 3], jax.nn.softplus(-decay_values)[None]], axis=0),
        up_to(taps + 4, 8),
        0,
    )

    positions = dp_index * length - (taps - 1) + jnp.arange(length + taps - 1, dtype=jnp.int32)
    starts = jnp.any(doc_starts[:, :, None] == positions[None, None, :], axis=1).astype(f32)
    columns = [starts[:, taps - 1 :]]
    valid = jnp.ones((rows, length), f32)
    for tap in range(1, taps):
        valid = valid * (1.0 - starts[:, taps - tap : taps - tap + length])
        columns.append(valid)
    masks = jnp.stack(columns + [valid] * (8 - taps), axis=-1)
    masks = masks.reshape(rows, spans, seg, 8).transpose(1, 0, 2, 3).reshape(block_tokens, 8)

    conv_in = dot(flat_one, input_matrix)
    conv_ends = conv_in.reshape(spans, rows, seg, width)[spans - 1, :, seg - 8 :, :]
    tail = lax.ppermute(
        conv_ends.reshape(rows * 8, width), "dp", [(i, i + 1) for i in range(peers - 1)]
    )
    flat = (block_tokens, width)
    conv_out, conv_low, decay, recur, entry, product, total, last = call(
        partial(gates_kernel, sizes),
        [(flat, f32), (flat, bf16)] + [(flat, f32)] * 5 + [((8, width), f32)],
        [
            ((rows, length + 8, width), f32),
            ((block_tokens, 2 * width), f32),
            (flat, f32),
        ],
        conv_in,
        tail,
        masks,
        table,
        params,
    )
    branch_pre = dot(tie(flat_one, last), branch_matrix)
    cot_far = ring_far(tie_all(cot_near, branch_pre))
    mixer_in, states, entered = call(
        partial(states_kernel, sizes, peers),
        [(flat, bf16), (flat, f32), ((8, width), f32)],
        [],
        mine,
        gather_small(tie(last, cot_near), "dp"),
        product,
        total,
        branch_pre,
        scalars=1,
    )
    branch_out = ring_scatter(
        sum_cores(*core_products(mixer_in, front_weights, 2)), bf16
    )

    residual = x_own + branch_out
    unit_two, inverse_two = rms_unit(residual)
    normed_two = (unit_two * gain_two).astype(bf16)
    flat_two = lax.all_gather(normed_two, ("z", "core"), axis=0, tiled=True)
    cotangent_flat = ring_whole(tie_all(cot_far, normed_two))
    grad_hidden = dot(cotangent_flat, down_turned)
    send, hidden, grad_gate_up = feed_forward(
        1 - core, flat_two, grad_hidden, back_weights, bf16, ()
    )
    keep, hidden, grad_gate_up = feed_forward(
        core, flat_two, grad_hidden, back_weights, f32, (hidden, grad_gate_up)
    )
    hidden = hidden.reshape(block_tokens, hidden_width)
    grad_gate_up = grad_gate_up.reshape(block_tokens, 2 * hidden_width)
    feed_width = 3 * hidden_width
    kept = {}

    def gate_up_part(operand):
        kept["feed"] = weight_grad(flat_two, operand, 2 * hidden_width, feed_width)
        return kept["feed"]

    def down_part(operand):
        kept["feed"] = weight_grad(
            cotangent_flat, operand, hidden_width, feed_width, 2, kept["feed"]
        )
        return kept["feed"]

    grad_normed_two = ring_scatter(
        sum_cores(send, keep), bf16, (grad_gate_up, gate_up_part), (hidden, down_part)
    )
    feed_grads = lax.psum_scatter(kept["feed"], "dp", scatter_dimension=0, tiled=True)
    grad_residual = cotangent.reshape(own, model).astype(f32) + norm_back(
        grad_normed_two, unit_two, inverse_two, gain_two
    )
    gain_two_part = jnp.sum(grad_normed_two * unit_two, axis=0)
    near = ring_near(grad_residual.astype(bf16))
    feed_hidden = tie(hidden, near[0])
    feed_send, feed_keep = core_products(feed_hidden, back_weights, 2)
    far = ring_far(tie_all(near, feed_send, feed_keep))

    places = jnp.stack([lax.axis_index("z"), core]).astype(jnp.int32)
    grad_branch, grad_branch_pre, grad_states, back_product, back_total, back_last = call(
        partial(reverse_kernel, sizes, 2),
        [((block_tokens, model), bf16), (flat, bf16)]
        + [(flat, f32)] * 3
        + [((8, width), f32)],
        [(flat, f32), (flat, f32), ((model, width), bf16)],
        places,
        branch_pre,
        states,
        decay,
        front_weights,
        *far,
        scalars=1,
        anywhere=(4,),
        sems=(pltpu.SemaphoreType.DMA,),
    )
    back_gathered = gather_small(back_last, "dp")
    feed_out = ring_scatter(sum_cores(tie(feed_send, back_last), feed_keep), bf16)
    layer_output = (residual + feed_out).astype(bf16)
    middle_part = weight_grad(tie(grad_branch, back_last), mixer_in, width, 2 * width)
    middle_part, branch_sums = weight_grad(
        flat_one, grad_branch_pre, width, 2 * width, 1, middle_part, front_weights, 1
    )
    sum_rows = up_to(taps + 4, 8)
    grad_gates, grad_front, ends, head, sums = call(
        partial(gates_back_kernel, sizes, peers),
        [
            ((block_tokens, 2 * width), bf16),
            ((block_tokens, 2 * width), bf16),
            ((rows * 8, width), f32),
            ((rows * 8, width), f32),
            ((sum_rows, width), f32),
        ],
        [
            ((rows, length + 8, width), f32),
            ((rows, length + 8, width), f32),
            ((rows, length + 16, width), f32),
            ((rows, length + 8, width), f32),
            ((rows, length + 16, 8), f32),
        ],
        mine,
        tie(back_gathered, middle_part, feed_grads),
        back_product,
        back_total,
        grad_states,
        states,
        entered,
        decay,
        recur,
        entry,
        conv_out,
        conv_in,
        tail,
        masks,
        table,
        params,
        grad_branch_pre,
        scalars=1,
    )
    middle_grad = lax.psum_scatter(
        tie(middle_part, feed_grads), "dp", scatter_dimension=0, tiled=True
    )
    from_next = lax.ppermute(head, "dp", [(i + 1, i) for i in range(peers - 1)])
    grad_front = lax.dynamic_update_slice(
        grad_front.reshape(spans, rows, seg, 2 * width),
        (ends + from_next).astype(bf16).reshape(1, rows, 8, width),
        (spans - 1, 0, seg - 8, 0),
    ).reshape(block_tokens, 2 * width)
    def input_part(operand):
        part, sums = weight_grad(
            flat_one, operand, width, width, 0, None, front_weights, 0, 1
        )
        kept["sums"] = sums
        kept["sent"] = lax.all_to_all(part.reshape(peers, depth, width), "dp", 0, 0)
        return sums

    grad_normed_one = ring_scatter(
        sum_cores(*core_products(grad_front, front_weights, 0)), bf16, (grad_front, input_part)
    )
    tokens_grad = grad_residual + norm_back(grad_normed_one, unit_one, inverse_one, gain_one)
    feed_grads = tie(feed_grads, grad_normed_one).astype(f32)
    middle_grad = tie(middle_grad, grad_normed_one).astype(f32)
    input_grad = jnp.sum(tie(kept["sent"], grad_normed_one).astype(f32), axis=0)
    gain_one_part = jnp.sum(branch_sums + kept["sums"], axis=1) / gain_one
    gain_parts = jnp.stack([gain_one_part, gain_two_part]).reshape(2, spans // 2, 2, -1)
    gain_parts = gain_parts.transpose(2, 1, 0, 3)
    gain_keep = lax.dynamic_index_in_dim(gain_parts, core, 0, keepdims=False)
    gain_send = lax.dynamic_index_in_dim(gain_parts, 1 - core, 0, keepdims=False)
    gain_parts = ring_scatter(gain_keep + swap_cores(gain_send), f32)
    gain_share = model // spans // peers
    gain_parts = gain_parts.reshape(2, peers, gain_share).transpose(1, 0, 2)

    table_grads = dot(grad_gates, conv_low, 0, 0)

    def diagonal_back(turned):
        block_of = (jnp.arange(units) // block)[:, None]
        kept = turned[:units, :block]
        for h in range(1, blocks):
            kept = jnp.where(block_of == h, turned[:units, h * block : (h + 1) * block], kept)
        return kept

    small_grads = jnp.concatenate(
        [
            diagonal_back(table_grads[:width]),
            diagonal_back(table_grads[width:]),
            sums[:, :units].T,
        ],
        axis=1,
    )
    small_grads = widen(small_grads, small_width, 1).reshape(peers, share, small_width)
    small_grads = jnp.concatenate([small_grads, widen(gain_parts, small_width, 2)], axis=1)
    small_grads = scatter_sum(tie(small_grads, kept["sent"]), "dp")
    gain_grads = small_grads[share : share + 2, :gain_share]
    small_grads = small_grads[:share].T
    rate_slope = jax.nn.sigmoid(-decay_param.astype(f32)) * decay_power
    at = 2 * block
    return (
        layer_output.reshape(rows, seg, model),
        tokens_grad.reshape(rows, seg, model),
        gain_grads[0],
        gain_grads[1],
        middle_grad[:, width : width + units],
        input_grad[:, :units],
        middle_grad[:, :units].T,
        small_grads[:block],
        small_grads[block:at],
        small_grads[at : at + taps],
        small_grads[at + taps],
        small_grads[at + taps + 1],
        small_grads[at + taps + 2],
        small_grads[at + taps + 3] * rate_slope,
        feed_grads[:, :hidden_width],
        feed_grads[:, hidden_width : 2 * hidden_width],
        feed_grads[:, 2 * hidden_width :].T,
    )


def solution(mesh):
    peers, group = mesh.devices.shape
    split = Mesh(mesh.devices.reshape(peers, group // 2, 2), ("dp", "z", "core"))
    tokens_spec = P(None, ("dp", "z", "core"), None)
    split_units = P(None, ("z", "core", "dp"))
    split_vector = P(("z", "core", "dp"))
    rows_first, units_first = P("dp", ("z", "core")), P(("z", "core"), "dp")
    return jax.shard_map(
        shards,
        mesh=split,
        in_specs=(tokens_spec, tokens_spec, P(), P(), rows_first, rows_first, units_first)
        + (split_units,) * 3
        + (split_vector,) * 4
        + (rows_first, rows_first, units_first, P()),
        out_specs=(tokens_spec, tokens_spec, split_vector, split_vector)
        + (rows_first, rows_first, units_first)
        + (split_units,) * 3
        + (split_vector,) * 4
        + (rows_first, rows_first, units_first),
        check_vma=False,
    )
```

```python
from functools import partial

import jax
import jax.numpy as jnp
from jax import lax
from jax.experimental import pallas as pl
from jax.experimental.pallas import tpu as pltpu
from jax.sharding import Mesh
from jax.sharding import PartitionSpec as P

eps_norm = 1e-06
decay_power = 8.0
mult_eps = 0.001
gelu_scale = 0.7978845608028654
gelu_cubic = 0.044715
lanes = 128
f32 = jnp.float32
bf16 = jnp.bfloat16


def cost(microseconds):
    return pl.CostEstimate(
        flops=microseconds * 1_100_000_000, bytes_accessed=0, transcendentals=0
    )


no_cost = cost(0)


def up_to(count, step):
    return -(-count // step) * step


def widen(values, width, axis):
    pads = [(0, 0)] * values.ndim
    pads[axis] = (0, width - values.shape[axis])
    return jnp.pad(values, pads)


def rms_unit(values):
    inverse = lax.rsqrt(jnp.mean(values * values, axis=-1, keepdims=True) + eps_norm)
    return (values * inverse, inverse)


def norm_back(grad_normed, unit_values, inverse, gain):
    scaled = grad_normed * gain
    return inverse * (scaled - unit_values * jnp.mean(scaled * unit_values, axis=-1, keepdims=True))


def gelu_parts(values):
    squared = values * values
    tanh_value = jnp.tanh(gelu_scale * values * (1.0 + gelu_cubic * squared))
    half = 0.5 * (1.0 + tanh_value)
    slope = half + 0.5 * values * (1.0 - tanh_value * tanh_value) * gelu_scale * (
        1.0 + 3.0 * gelu_cubic * squared
    )
    return (values * half, slope)


def dot(left, right, left_axis=1, right_axis=0):
    return lax.dot_general(
        left, right, (((left_axis,), (right_axis,)), ((), ())), preferred_element_type=f32
    )


def gather_small(value, axis):
    peers = lax.axis_size(axis)
    return lax.all_to_all(jnp.broadcast_to(value[None], (peers,) + value.shape), axis, 0, 0)


def scatter_sum(value, axis):
    return jnp.sum(lax.all_to_all(value, axis, 0, 0).astype(f32), axis=0)


def tie(value, *before):
    return lax.optimization_barrier((value,) + before)[0]


def tie_all(values, *before):
    return lax.optimization_barrier((values,) + before)[0]


def swap_cores(value):
    return lax.ppermute(value, "core", [(0, 1), (1, 0)])


def turn(value, by):
    count = lax.axis_size("z")
    return lax.ppermute(value, "z", [(i, (i + by) % count) for i in range(count)])


def ring_near(value):
    return (value, turn(value, 1), turn(value, -1), swap_cores(value))


def ring_far(near, work=None):
    value, below, above, other = near
    half = value.shape[0] // 2
    far_low, far_high = ring_step(below[:half], above[half:], work)
    swapped = [swap_cores(part) for part in (above, below, far_low, far_high)]
    return [value, above, below, far_low, far_high, other] + swapped


def ring_places(rows):
    half = rows // 2
    places = [(0, 0, rows), (1, 0, rows), (3, 0, rows), (2, 0, half), (2, half, half)]
    return [(by, side, at, size) for side in range(2) for by, at, size in places]


def ring_whole(pieces):
    count = lax.axis_size("z")
    z, core = lax.axis_index("z"), lax.axis_index("core")
    rows, columns = pieces[0].shape
    whole = jnp.zeros((2 * count * rows, columns), pieces[0].dtype)
    for piece, (by, side, first, _) in zip(pieces, ring_places(rows)):
        span = (1 - core if side else core) * count + lax.rem(z + by, count)
        whole = lax.dynamic_update_slice(whole, piece, (span * rows + first, 0))
    return whole


def scatter_direct(part, axis):
    count = lax.axis_size(axis)
    index = lax.axis_index(axis)

    def piece(by):
        return lax.dynamic_index_in_dim(part, lax.rem(index + by, count), 0, keepdims=False)

    found = piece(0).astype(f32)
    for by in range(1, count):
        pairs = [(i, (i + by) % count) for i in range(count)]
        found = found + lax.ppermute(piece(by), axis, pairs).astype(f32)
    return found


def ring_step(low, high, work):
    if work is None:
        return turn(low, 1), turn(high, -1)
    operand, function = work
    low, high, operand = lax.optimization_barrier((low, high, operand))
    below, above = turn(low, 1), turn(high, -1)
    below, above, _ = lax.optimization_barrier((below, above, function(operand)))
    return below, above


def far_pieces(operands, takes=0):
    model = operands[2].shape[0]
    half = operands[1].shape[0] // lax.axis_size("z") // 2
    return product_pieces((2,), *operands, [((half, model), bf16)] * 2, takes)


def near_pieces(operands, takes=0):
    model = operands[2].shape[0]
    rows = operands[1].shape[0] // lax.axis_size("z")
    return product_pieces((1, 3, 0), *operands, [((rows, model), f32)] * 3, takes)


def all_pieces(operands, takes=0):
    model = operands[2].shape[0]
    rows = operands[1].shape[0] // lax.axis_size("z")
    outs = [((rows // 2, model), bf16)] * 2 + [((rows, model), f32)] * 3
    return product_pieces((2, 1, 3, 0), *operands, outs, takes)


def near_sums(ahead, behind, from_below, from_above):
    return rows_call(near_body, (ahead, behind, from_below, from_above), [(ahead.shape, bf16)] * 2)


def ring_scatter(x, got, weights, others, at, body, extra, outs, first=None, second=None):
    operands = (x, got, weights, others, at)
    if first is not None:
        low, high, ahead, behind, mine = all_pieces(operands, 9)
        below, above = ring_step(low, high, first)
    else:
        low, high = far_pieces(operands, 5)
        found = []

        def near_work(operand):
            found.extend(near_pieces(operand + operands[2:], 6))
            return found

        below, above = ring_step(low, high, ((x, got), near_work))
        ahead, behind, mine = found
    below, above = ring_step(*near_sums(ahead, behind, below, above), second)
    return rows_call(body, (mine, below, above) + extra, outs)


class Sizes:
    def __init__(self, rows, seg, spans, width, conv_width):
        self.rows, self.seg, self.spans = rows, seg, spans
        self.width, self.conv_width = width, conv_width
        self.stride = rows * seg
        self.tokens = spans * self.stride
    def pair(self, position):
        count = self.rows * self.spans
        return pl.ds(pl.multiple_of(position * count, count), count)


def weave(sizes, source, target, back=False):
    blocks = sizes.seg // 8

    def step(index, carried):
        row, block = index // blocks, index % blocks
        natural = [
            pl.ds(
                pl.multiple_of(
                    (span % 2 * (sizes.spans // 2) + span // 2) * sizes.stride
                    + row * sizes.seg
                    + block * 8,
                    8,
                ),
                8,
            )
            for span in range(sizes.spans)
        ]
        woven = [
            pl.ds(pl.multiple_of(((block * 8 + place) * sizes.rows + row) * sizes.spans, 8), 8)
            for place in range(8)
        ]
        reads, writes = (woven, natural) if back else (natural, woven)
        for start in range(0, sizes.width, lanes):
            columns = slice(start, start + lanes)
            tiles = jnp.stack([source[at, columns] for at in reads], axis=0)
            tiles = jnp.transpose(tiles, (1, 0, 2))
            for place, at in enumerate(writes):
                target[at, columns] = tiles[place]
        return carried

    lax.fori_loop(0, sizes.rows * blocks, step, 0)


def span_before(tile, first):
    place = lax.broadcasted_iota(jnp.int32, tile.shape, 0)
    return jnp.where(place == 0, first, pltpu.roll(tile, 1, 0))


def span_after(tile, last):
    count = tile.shape[0]
    place = lax.broadcasted_iota(jnp.int32, tile.shape, 0)
    return jnp.where(place == count - 1, last, pltpu.roll(tile, count - 1, 0))


def across_spans(product, total, backward):
    spans = product.shape[0]
    so_far = (jnp.ones_like(product[:1]), jnp.zeros_like(total[:1]))
    ahead = [None] * spans
    for span in range(spans - 1, -1, -1) if backward else range(spans):
        ahead[span] = so_far
        now = product[span : span + 1]
        so_far = (so_far[0] * now, total[span : span + 1] + now * so_far[1])
    products, totals = (jnp.concatenate(part, axis=0) for part in zip(*ahead))
    return products, totals, so_far


def from_others(sizes, index_ref, all_ref, peers, backward):
    mine = index_ref[0]
    entering = [jnp.zeros((1, sizes.width), f32) for _ in range(sizes.rows)]
    for step in range(peers - 1):
        peer = peers - 1 - step if backward else step
        ahead = peer > mine if backward else peer < mine
        for row in range(sizes.rows):
            product = all_ref[peer, row : row + 1, :]
            total = all_ref[peer, sizes.rows + row : sizes.rows + row + 1, :]
            entering[row] = jnp.where(ahead, total + product * entering[row], entering[row])
    return entering


def sigmoid(values):
    return 0.5 * jnp.tanh(0.5 * values) + 0.5


def keep_ends(sizes, found, prefix, last, backward):
    rows, spans = sizes.rows, sizes.spans
    last[...] = jnp.zeros(last.shape, f32)
    for row in range(rows):
        mine = slice(row * spans, (row + 1) * spans)
        products, totals, whole = across_spans(found[0][mine], found[1][mine], backward)
        prefix[row * spans : (row + 1) * spans, :] = products
        prefix[(rows + row) * spans : (rows + row + 1) * spans, :] = totals
        last[row : row + 1, :] = whole[0]
        last[rows + row : rows + row + 1, :] = whole[1]


def entering_spans(sizes, prefix, entering):
    rows, spans = sizes.rows, sizes.spans
    return jnp.concatenate(
        [
            prefix[(rows + row) * spans : (rows + row + 1) * spans, :]
            + prefix[row * spans : (row + 1) * spans, :] * entering[row]
            for row in range(rows)
        ],
        axis=0,
    )


def per_row(sizes, function, pair, edges):
    spans = sizes.spans
    return jnp.concatenate(
        [function(pair[row * spans : (row + 1) * spans], edges[row]) for row in range(sizes.rows)],
        axis=0,
    )


parts = 4
dp = ("x", "y")


class Parts:
    def __init__(self, sources, targets, sems):
        self.pairs = list(zip(sources, targets))
        self.sems = sems

    def copy(self, which, part):
        source, target = self.pairs[which]
        count = source.shape[0] // parts
        at = pl.ds(pl.multiple_of(part * count, count), count)
        return pltpu.make_async_copy(source.at[at], target.at[at], self.sems.at[which, part])

    def start(self, part, which=None):
        for index in range(len(self.pairs)) if which is None else which:
            self.copy(index, part).start()

    def wait(self, part, which=None):
        for index in range(len(self.pairs)) if which is None else which:
            self.copy(index, part).wait()


def gates_kernel(sizes, conv_in, tail, masks, table, params, *refs):
    outs, refs = refs[:10], refs[10:]
    prefix, last, refs = refs[0], refs[1], refs[2:]
    held, refs = refs[:10], refs[10:]
    conv_now, conv_woven, mixed, sems = refs
    product, total, decay, conv_low, woven_low, direct_by, entry_by, state_by, rest_by, slope_by = held
    sent = Parts(held, outs, sems)
    seg, taps, width, spans = sizes.seg, sizes.conv_width, sizes.width, sizes.spans
    rows = sizes.rows
    bias = params[taps : taps + 1, :]
    weave(sizes, conv_in, conv_woven)
    before = []
    for tap in range(1, taps):
        edges = [tail[row * 8 + 8 - tap : row * 8 + 9 - tap, :] for row in range(rows)]
        before.append(per_row(sizes, span_before, conv_woven[sizes.pair(seg - tap), :], edges))
    recur_bias = params[taps + 1 : taps + 2, :]
    entry_bias = params[taps + 2 : taps + 3, :]
    rate = params[taps + 3 : taps + 4, :] * (-decay_power)
    per_part = seg // parts
    part_rows = per_part * rows * spans

    def part_step(part, carried):
        before, found = carried

        def conv_step(step, before):
            at = sizes.pair(part * per_part + step)
            valid = masks[at, :]
            tile = conv_woven[at, :]
            value = bias + params[0:1, :] * tile
            for tap in range(1, taps):
                value = value + params[tap : tap + 1, :] * before[tap - 1] * (
                    valid[:, tap : tap + 1]
                )
            conv_now[sizes.pair(step), :] = value
            conv_low[at, :] = value.astype(bf16)
            woven_low[at, :] = tile.astype(bf16)
            return (tile,) + tuple(before[:-1])

        before = lax.fori_loop(0, per_part, conv_step, before, unroll=4)
        part_at = pl.ds(pl.multiple_of(part * part_rows, part_rows), part_rows)
        mixed[...] = dot(conv_low[part_at, :], table[...], 1, 1)

        def gate_step(step, carried):
            at = sizes.pair(part * per_part + step)
            here = sizes.pair(step)
            starting = jnp.broadcast_to(masks[at, :][:, 0:1], (rows * spans, width)) > 0.5
            recur_now = sigmoid(mixed[here, :width] + recur_bias)
            entry_now = sigmoid(mixed[here, width:] + entry_bias)
            conv_here = conv_now[here, :]
            decay_now = jnp.where(starting, 0.0, jnp.exp(rate * recur_now))
            squared = 1.0 - decay_now * decay_now + mult_eps
            root = lax.rsqrt(squared)
            scale = jnp.where(starting, 1.0, squared * root)
            direct = scale * entry_now
            gated = entry_now * conv_here
            by_state = decay_now * recur_now
            product_now = carried[0] * decay_now
            total_now = carried[1] * decay_now + direct * conv_here
            product[at, :] = product_now
            total[at, :] = total_now
            decay[at, :] = decay_now
            direct_by[at, :] = direct.astype(bf16)
            entry_by[at, :] = (scale * gated * (1.0 - entry_now)).astype(bf16)
            state_by[at, :] = by_state.astype(bf16)
            rest_by[at, :] = (by_state * gated * decay_now * root).astype(bf16)
            slope_by[at, :] = (rate * (1.0 - recur_now)).astype(bf16)
            return (product_now, total_now)

        found = lax.fori_loop(0, per_part, gate_step, found, unroll=4)
        sent.start(part)
        return (before, found)

    shape = (rows * spans, width)
    first = (jnp.ones(shape, f32), jnp.zeros(shape, f32))
    _, found = lax.fori_loop(0, parts, part_step, (tuple(before), first))
    keep_ends(sizes, found, prefix, last, False)
    for part in range(parts):
        sent.wait(part)


def states_kernel(sizes, peers, index, gathered, prefix, *refs):
    sources, pre_hbm, outs, refs = refs[:4], refs[4], refs[5:8], refs[8:]
    held, refs = refs[:4], refs[4:]
    product, total, state_by, rest_by = held
    branch_pre, mixer_in, recur_by, natural, states, in_sems, pre_sem, out_sems = refs
    taken = Parts(sources, held, in_sems)
    sent = Parts((mixer_in, recur_by, natural), outs, out_sems)
    pre_copy = pltpu.make_async_copy(pre_hbm, branch_pre, pre_sem)
    for part in range(parts):
        taken.start(part, (0, 1))
    pre_copy.start()
    for part in range(parts):
        taken.start(part, (2, 3))
    rows, spans, seg = sizes.rows, sizes.spans, sizes.seg
    entering = from_others(sizes, index, gathered, peers, False)
    spans_in = entering_spans(sizes, prefix, entering)
    per_part = seg // parts
    for part in range(parts):
        taken.wait(part, (0, 1))

        def state_step(step, carried, part=part):
            at = sizes.pair(part * per_part + step)
            states[at, :] = total[at, :] + product[at, :] * spans_in
            return carried

        lax.fori_loop(0, per_part, state_step, 0, unroll=4)
    weave(sizes, states, natural, True)
    for part in range(parts):
        sent.start(part, (2,))
    pre_copy.wait()
    step_rows = 32
    steps = sizes.tokens // parts // step_rows

    def act_part(part, carried):
        def act_step(step, carried):
            start = pl.multiple_of((part * steps + step) * step_rows, step_rows)
            at = pl.ds(start, step_rows)
            mixer_in[at, :] = (natural[at, :] * gelu_parts(branch_pre[at, :])[0]).astype(bf16)
            return carried

        lax.fori_loop(0, steps, act_step, 0, unroll=2)
        sent.start(part, (0,))
        return carried

    lax.fori_loop(0, parts, act_part, 0)
    before = per_row(sizes, span_before, states[sizes.pair(seg - 1), :], entering)
    for part in range(parts):
        taken.wait(part, (2, 3))

    def recur_part(part, before):
        def recur_step(step, before):
            at = sizes.pair(part * per_part + step)
            found = before * state_by[at, :].astype(f32) - rest_by[at, :].astype(f32)
            recur_by[at, :] = found.astype(bf16)
            return states[at, :]

        before = lax.fori_loop(0, per_part, recur_step, before, unroll=4)
        sent.start(part, (1,))
        return before

    lax.fori_loop(0, parts, recur_part, before)
    for part in range(parts):
        sent.wait(part)


def reverse_kernel(
    sizes, out_at, place, pre_hbm, natural_hbm, decay_hbm, weights_hbm, *refs
):
    places = ring_places(sizes.stride)
    pieces, refs = refs[: len(places)], refs[len(places) :]
    outs, prefix, last, refs = refs[:4], refs[4], refs[5], refs[6:]
    grad_branch, grad_branch_pre, own_part, later_by, grad_states = refs[:5]
    branch_pre, natural, decay, grad_mixer, weights = refs[5:10]
    in_sems, piece_sems, out_sems, branch_sems = refs[10:]
    width, spans = sizes.width, sizes.spans
    z, core = place[0], place[1]
    stride = sizes.stride
    copies = []
    for number, (piece, (by, side, first, count)) in enumerate(zip(pieces, places)):
        span = (1 - core if side else core) * (spans // 2) + lax.rem(z + by, spans // 2)
        at = pl.ds(pl.multiple_of(span * stride + first, sizes.seg), count)
        copy = pltpu.make_async_copy(piece, grad_branch.at[at], piece_sems.at[number])
        copies.append((side, copy))
    taken = [
        pltpu.make_async_copy(source, target, in_sems.at[number])
        for number, (source, target) in enumerate(
            (
                (weights_hbm.at[:, out_at * width : (out_at + 1) * width], weights),
                (pre_hbm, branch_pre),
                (natural_hbm, natural),
                (decay_hbm, decay),
            )
        )
    ]
    taken[0].start()
    for _, copy in copies:
        copy.start()
    for copy in taken[1:]:
        copy.start()
    taken[0].wait()
    half = sizes.tokens // 2
    branch_out = []
    for side in range(2):
        for piece_side, copy in copies:
            if piece_side == side:
                copy.wait()
        at = pl.ds(pl.multiple_of((1 - core if side else core) * half, half), half)
        out = pltpu.make_async_copy(grad_branch.at[at], outs[0].at[at], branch_sems.at[side])
        out.start()
        branch_out.append(out)
        grad_mixer[at, :] = dot(grad_branch[at, :], weights[...])
    taken[1].wait()
    taken[2].wait()
    sent = Parts((grad_branch_pre, own_part, later_by), outs[1:], out_sems)
    step_rows = 32
    steps = sizes.tokens // parts // step_rows

    def part_step(part, carried):
        def gelu_step(step, carried):
            start = pl.multiple_of((part * steps + step) * step_rows, step_rows)
            at = pl.ds(start, step_rows)
            grad = grad_mixer[at, :]
            act, slope = gelu_parts(branch_pre[at, :])
            grad_branch_pre[at, :] = (grad * natural[at, :] * slope).astype(bf16)
            grad_mixer[at, :] = grad * act
            return carried

        lax.fori_loop(0, steps, gelu_step, 0, unroll=2)
        sent.start(part, (0,))
        return carried

    lax.fori_loop(0, parts, part_step, 0)
    weave(sizes, grad_mixer, grad_states)
    taken[3].wait()
    per_part = sizes.seg // parts

    def scan_part(index, carried):
        part = parts - 1 - index

        def scan_step(step, carried):
            at = sizes.pair(part * per_part + per_part - 1 - step)
            decay_now = decay[at, :]
            own = carried[1] + grad_states[at, :]
            own_part[at, :] = own
            later_by[at, :] = carried[0]
            return (carried[0] * decay_now, own * decay_now)

        carried = lax.fori_loop(0, per_part, scan_step, carried, unroll=4)
        sent.start(part, (1, 2))
        return carried

    shape = (sizes.rows * spans, width)
    first = (jnp.ones(shape, f32), jnp.zeros(shape, f32))
    found = lax.fori_loop(0, parts, scan_part, first)
    keep_ends(sizes, found, prefix, last, True)
    for part in range(parts):
        sent.wait(part)
    for out in branch_out:
        out.wait()


def gates_back_kernel(sizes, peers, index, gathered, prefix, tail, masks, table, params, *refs):
    sources, branch_hbm, refs = refs[:7], refs[7], refs[8:]
    outs, ends, head, sums, refs = refs[:2], refs[2], refs[3], refs[4], refs[5:]
    held, refs = refs[:7], refs[7:]
    grad_gates, grad_front, grad_conv, grad_conv_in, natural = refs[:5]
    in_sems, branch_sem, out_sems = refs[5:]
    own_part, later_by, direct_by, entry_by, recur_by, slope_by, woven_low = held
    seg, taps, width, spans = sizes.seg, sizes.conv_width, sizes.width, sizes.spans
    rows = sizes.rows
    taken = Parts(sources, held, in_sems)
    branch_copy = pltpu.make_async_copy(
        branch_hbm, grad_front.at[:, width : 2 * width], branch_sem
    )
    for part in range(2):
        taken.start(part, range(6))
    entering = from_others(sizes, index, gathered, peers, True)
    spans_in = entering_spans(sizes, prefix, entering)
    shape = (rows * spans, width)

    def gate_step(position, carried):
        at = sizes.pair(position)
        rate_sum, recur_sum, entry_sum = carried
        direct, entry, recur, slope = (
            ref[at, :].astype(f32) for ref in (direct_by, entry_by, recur_by, slope_by)
        )
        carried_now = own_part[at, :] + later_by[at, :] * spans_in
        rated = carried_now * recur
        recur_low = (rated * slope).astype(bf16)
        entry_low = (carried_now * entry).astype(bf16)
        grad_gates[at, :width] = recur_low
        grad_gates[at, width:] = entry_low
        grad_conv[at, :] = carried_now * direct
        return (
            rate_sum + rated,
            recur_sum + recur_low.astype(f32),
            entry_sum + entry_low.astype(f32),
        )

    empty = jnp.zeros(shape, f32)
    gate_sums = (empty,) * 3
    per_part = seg // parts
    part_rows = per_part * rows * spans
    sent = Parts((grad_gates, grad_front), outs, out_sems)
    for part in range(parts):
        taken.wait(part, range(6))
        if part + 2 < parts:
            taken.start(part + 2, range(6))
        elif part + 2 == parts:
            for later in range(parts):
                taken.start(later, (6,))
        else:
            branch_copy.start()
        gate_sums = lax.fori_loop(
            part * per_part, (part + 1) * per_part, gate_step, gate_sums, unroll=4
        )
        sent.start(part, (0,))
        at = pl.ds(part * part_rows, part_rows)
        grad_conv[at, :] = grad_conv[at, :] + dot(grad_gates[at, :], table[...], 1, 0)

    def weighted(position):
        at = sizes.pair(position)
        grad = grad_conv[at, :]
        valid = masks[at, :]
        return [grad] + [grad * valid[:, tap : tap + 1] for tap in range(1, taps)]

    tap_rows = [params[tap : tap + 1, :] for tap in range(taps)]
    ahead = [weighted(position) for position in range(taps - 1)]
    nothing_after = [jnp.zeros((1, width), f32)] * rows
    held_ahead = [
        per_row(sizes, span_after, ahead[place][tap], nothing_after)
        for tap in range(1, taps)
        for place in range(tap)
    ]

    def conv_step(index, carried):
        held_now, now_sums = carried
        at = sizes.pair(seg - 1 - index)
        tile = woven_low[at, :].astype(f32)
        now = weighted(seg - 1 - index)
        value = tap_rows[0] * now[0]
        new_held, new_sums, first = [], [now_sums[0] + tile * now[0]], 0
        for tap in range(1, taps):
            far = held_now[first + tap - 1]
            value = value + tap_rows[tap] * far
            new_sums.append(now_sums[tap] + tile * far)
            new_held += [now[tap]] + list(held_now[first : first + tap - 1])
            first += tap
        new_sums.append(now_sums[taps] + now[0])
        grad_conv_in[at, :] = value
        return tuple(new_held), tuple(new_sums)

    for part in range(parts):
        taken.wait(part, (6,))
    held_ahead, tap_sums = lax.fori_loop(
        0, seg, conv_step, (tuple(held_ahead), (empty,) * (taps + 1)), unroll=2
    )
    tap_sums = list(tap_sums)
    head[...] = jnp.zeros(head.shape, f32)
    for row in range(rows):
        for back in range(1, taps):
            value = jnp.zeros((1, width), f32)
            tail_row = tail[row * 8 + 8 - back : row * 8 + 9 - back, :]
            first = 0
            for tap in range(1, taps):
                if tap >= back:
                    first_row = held_ahead[first + tap - back][row * spans : row * spans + 1]
                    value = value + tap_rows[tap] * first_row
                    tap_sums[tap] = tap_sums[tap] + jnp.concatenate(
                        [tail_row * first_row, jnp.zeros((rows * spans - 1, width), f32)], axis=0
                    )
                first += tap
            head[row * 8 + 8 - back : row * 8 + 9 - back, :] = value
    weave(sizes, grad_conv_in, natural, True)
    branch_copy.wait()
    step_rows = 32
    steps = sizes.tokens // parts // step_rows

    def part_step(part, carried):
        def front_step(step, carried):
            start = pl.multiple_of((part * steps + step) * step_rows, step_rows)
            at = pl.ds(start, step_rows)
            grad_front[at, :width] = natural[at, :].astype(bf16)
            return carried

        lax.fori_loop(0, steps, front_step, 0, unroll=4)
        sent.start(part, (1,))
        return carried

    lax.fori_loop(0, parts, part_step, 0)
    for row in range(rows):
        end = (spans - 1) * sizes.stride + (row + 1) * seg
        ends[row * 8 : row * 8 + 8, :] = natural[end - 8 : end, :]
    for place, part_sum in enumerate(tap_sums + [gate_sums[1], gate_sums[2], gate_sums[0]]):
        sums[place : place + 1, :] = jnp.sum(part_sum, axis=0, keepdims=True)
    for part in range(parts):
        sent.wait(part)


def rows_kernel(body, inputs, *refs):
    ins, outs = refs[:inputs], refs[inputs:]
    rows, step_rows = ins[0].shape[0], 32
    for start in range(0, rows, step_rows):
        body(start, slice(start, start + step_rows), ins, outs)


def rows_call(body, ins, outs):
    vmem = pl.BlockSpec(memory_space=pltpu.VMEM)
    return pl.pallas_call(
        partial(rows_kernel, body, len(ins)),
        out_shape=[jax.ShapeDtypeStruct(shape, kind) for shape, kind in outs],
        in_specs=[vmem] * len(ins),
        out_specs=[vmem] * len(outs),
        cost_estimate=no_cost,
        compiler_params=pltpu.CompilerParams(vmem_limit_bytes=20 * 1024 * 1024),
    )(*ins)


def near_body(start, at, ins, outs):
    half = ins[2].shape[0]
    ahead, behind = ins[0][at, :], ins[1][at, :]
    if start < half:
        ahead = ahead + ins[2][at, :].astype(f32)
    else:
        behind = behind + ins[3][start - half : start - half + behind.shape[0], :].astype(f32)
    outs[0][at, :] = ahead.astype(bf16)
    outs[1][at, :] = behind.astype(bf16)


def own_sum(at, ins):
    return ins[0][at, :] + ins[1][at, :].astype(f32) + ins[2][at, :].astype(f32)


def branch_body(start, at, ins, outs):
    residual = own_sum(at, ins) + ins[3][at, :].astype(f32)
    outs[0][at, :] = residual
    outs[1][at, :] = (rms_unit(residual)[0] * ins[4][...]).astype(bf16)


def feed_back_body(start, at, ins, outs):
    grad = own_sum(at, ins)
    unit, inverse = rms_unit(ins[3][at, :])
    found = ins[4][at, :].astype(f32) + norm_back(grad, unit, inverse, ins[5][...])
    outs[0][at, :] = found
    outs[1][at, :] = found.astype(bf16)
    part = jnp.sum((grad * unit).reshape(-1, 8, grad.shape[1]), axis=0)
    outs[2][...] = part if start == 0 else outs[2][...] + part


def feed_body(start, at, ins, outs):
    outs[0][at, :] = (own_sum(at, ins) + ins[3][at, :]).astype(bf16)


def tokens_body(start, at, ins, outs):
    grad = own_sum(at, ins)
    unit, inverse = rms_unit(ins[3][at, :].astype(f32))
    outs[0][at, :] = ins[4][at, :] + norm_back(grad, unit, inverse, ins[5][...])


def call(kernel, outs, scratch, *operands, scalars=0, anywhere=(), out_anywhere=0, sems=(), takes=0):
    vmem = pl.BlockSpec(memory_space=pltpu.VMEM)
    hbm = pl.BlockSpec(memory_space=pl.ANY)
    in_specs = [pl.BlockSpec(memory_space=pltpu.SMEM)] * scalars
    in_specs += [vmem] * (len(operands) - scalars)
    for index in anywhere:
        in_specs[index] = hbm
    return pl.pallas_call(
        kernel,
        out_shape=[jax.ShapeDtypeStruct(shape, kind) for shape, kind in outs],
        in_specs=in_specs,
        out_specs=[hbm] * out_anywhere + [vmem] * (len(outs) - out_anywhere),
        scratch_shapes=[pltpu.VMEM(shape, kind) for shape, kind in scratch]
        + [pltpu.SemaphoreType.DMA(shape) for shape in sems],
        cost_estimate=cost(takes),
        compiler_params=pltpu.CompilerParams(vmem_limit_bytes=60 * 1024 * 1024),
    )(*operands)


def product_kernel(at, bys, place, x_hbm, got_hbm, own_hbm, other_hbm, *refs):
    outs, (x, weights, x_sem, weight_sem) = refs[:-4], refs[-4:]
    depth = got_hbm.shape[1]
    span = x.shape[0] // len(bys)
    rows = got_hbm.shape[0]
    columns = 512
    steps = weights.shape[0] // columns
    halves = (slice(0, depth), slice(depth, 2 * depth))

    def weight_copies(index):
        place = slice(index * columns, (index + 1) * columns)
        return [
            pltpu.make_async_copy(
                source.at[place, at * depth : (at + 1) * depth],
                weights.at[place, half],
                weight_sem.at[2 * index + side],
            )
            for side, (source, half) in enumerate(zip((own_hbm, other_hbm), halves))
        ]

    x_copies = []
    for number, by in enumerate(bys):
        first = lax.rem(place[0] + by, rows // span) * span
        to = slice(number * span, (number + 1) * span)
        mine = pl.ds(pl.multiple_of(place[1] * rows + first, span), span)
        theirs = pl.ds(pl.multiple_of(first, span), span)
        x_copies += [
            pltpu.make_async_copy(x_hbm.at[mine], x.at[to, halves[0]], x_sem.at[2 * number]),
            pltpu.make_async_copy(
                got_hbm.at[theirs], x.at[to, halves[1]], x_sem.at[2 * number + 1]
            ),
        ]
    for copy in x_copies:
        copy.start()
    for index in range(2):
        for copy in weight_copies(index):
            copy.start()
    for copy in x_copies:
        copy.wait()
    for index in range(steps):
        for copy in weight_copies(index):
            copy.wait()
        if index + 2 < steps:
            for copy in weight_copies(index + 2):
                copy.start()
        place_now = slice(index * columns, (index + 1) * columns)
        value = dot(x[...], weights[place_now, :], 1, 1)
        first = 0
        for out in outs:
            out[:, place_now] = value[first : first + out.shape[0]].astype(out.dtype)
            first += out.shape[0]


def product_pieces(bys, x, got, weights, others, at, outs, takes):
    depth, model = got.shape[1], weights.shape[0]
    span = got.shape[0] // lax.axis_size("z")
    place = jnp.stack([lax.axis_index("z"), lax.axis_index("core")]).astype(jnp.int32)
    anywhere = pl.BlockSpec(memory_space=pl.ANY)
    return pl.pallas_call(
        partial(product_kernel, at, bys),
        out_shape=[jax.ShapeDtypeStruct(shape, kind) for shape, kind in outs],
        in_specs=[pl.BlockSpec(memory_space=pltpu.SMEM)] + [anywhere] * 4,
        out_specs=[pl.BlockSpec(memory_space=pltpu.VMEM)] * len(outs),
        scratch_shapes=[
            pltpu.VMEM((len(bys) * span, 2 * depth), bf16),
            pltpu.VMEM((model, 2 * depth), bf16),
            pltpu.SemaphoreType.DMA((2 * len(bys),)),
            pltpu.SemaphoreType.DMA((2 * model // 512,)),
        ],
        cost_estimate=cost(takes),
        compiler_params=pltpu.CompilerParams(vmem_limit_bytes=60 * 1024 * 1024),
    )(place, x, got, weights, others)


def swap_rows(x):
    rows = x.shape[0] // 2
    theirs = (1 - lax.axis_index("core")) * rows
    return swap_cores(lax.dynamic_slice_in_dim(x, theirs, rows, 0))


def feed_kernel(aliased, sends, core, x_hbm, grad_hbm, weights_hbm, *refs):
    refs = refs[aliased:]
    hidden_hbm, both_hbm, refs = refs[0], refs[1], refs[2:]
    if sends:
        send_hbm, refs = refs[0], refs[1:]
    x, grad, weights, pre, hidden, both, in_sem, weight_sem, out_sem = refs
    rows = x.shape[0]
    inner = grad.shape[1]
    mine = pl.ds(pl.multiple_of(core[0] * rows, rows), rows)
    copies = [
        pltpu.make_async_copy(x_hbm.at[mine], x, in_sem.at[0]),
        pltpu.make_async_copy(grad_hbm.at[mine], grad, in_sem.at[1]),
    ]
    columns = weights.shape[2]
    count = 2 * inner // columns

    def weight_copy(index):
        at = slice(index * columns, (index + 1) * columns)
        return pltpu.make_async_copy(
            weights_hbm.at[:, at], weights.at[index], weight_sem.at[index]
        )

    copies[0].start()
    for index in range(count):
        weight_copy(index).start()
    copies[1].start()
    copies[0].wait()
    for index in range(count):
        weight_copy(index).wait()
        pre[:, index * columns : (index + 1) * columns] = dot(x[...], weights[index])
    copies[1].wait()
    step_rows = 32
    outs = []

    def out_copies(part):
        size = rows // parts
        here = pl.ds(pl.multiple_of(part * size, size), size)
        there = pl.ds(pl.multiple_of(core[0] * rows + part * size, size), size)
        found = [
            pltpu.make_async_copy(hidden.at[here], hidden_hbm.at[there], out_sem.at[part, 0]),
            pltpu.make_async_copy(both.at[here], both_hbm.at[there], out_sem.at[part, 1]),
        ]
        if sends:
            found.append(
                pltpu.make_async_copy(both.at[here], send_hbm.at[here], out_sem.at[part, 2])
            )
        return found

    steps = rows // parts // step_rows

    def part_step(part, carried):
        def act_step(step, carried):
            start = pl.multiple_of((part * steps + step) * step_rows, step_rows)
            at = pl.ds(start, step_rows)
            act, slope = gelu_parts(pre[at, :inner])
            up = pre[at, inner:]
            grad_now = grad[at, :]
            hidden[at, :] = (act * up).astype(bf16)
            both[at, :inner] = (grad_now * up * slope).astype(bf16)
            both[at, inner:] = (grad_now * act).astype(bf16)
            return carried

        lax.fori_loop(0, steps, act_step, 0)
        for copy in out_copies(part):
            copy.start()
        return carried

    lax.fori_loop(0, parts, part_step, 0)
    for part in range(parts):
        for copy in out_copies(part):
            copy.wait()


def feed_forward(core, flat, grad_hidden, weights, sends, given):
    tokens, model = flat.shape
    inner = grad_hidden.shape[1]
    rows = tokens // 2
    columns = 512
    anywhere = pl.BlockSpec(memory_space=pl.ANY)
    outs = [(tokens, inner), (tokens, 2 * inner)] + [(rows, 2 * inner)] * sends
    return pl.pallas_call(
        partial(feed_kernel, len(given), sends),
        out_shape=[jax.ShapeDtypeStruct(shape, bf16) for shape in outs],
        in_specs=[pl.BlockSpec(memory_space=pltpu.SMEM)] + [anywhere] * (3 + len(given)),
        out_specs=[anywhere] * len(outs),
        scratch_shapes=[
            pltpu.VMEM((rows, model), bf16),
            pltpu.VMEM((rows, inner), f32),
            pltpu.VMEM((2 * inner // columns, model, columns), bf16),
            pltpu.VMEM((rows, 2 * inner), f32),
            pltpu.VMEM((rows, inner), bf16),
            pltpu.VMEM((rows, 2 * inner), bf16),
            pltpu.SemaphoreType.DMA((2,)),
            pltpu.SemaphoreType.DMA((2 * inner // columns,)),
            pltpu.SemaphoreType.DMA((parts, 3)),
        ],
        input_output_aliases={4: 0, 5: 1} if given else {},
        cost_estimate=cost(8),
        compiler_params=pltpu.CompilerParams(vmem_limit_bytes=60 * 1024 * 1024),
    )(
        jnp.reshape(core, (1,)).astype(jnp.int32),
        flat,
        grad_hidden,
        weights,
        *given,
    )


def weight_kernel(with_sums, filled, left, right, *refs):
    value = dot(left[...], right[...], 0, 0)
    if with_sums:
        weight, (out, sums) = refs[0], refs[1 + filled :]
        product = value * weight[...].astype(f32)
        sums[...] = sum(
            product[:, start : start + lanes] for start in range(0, product.shape[1], lanes)
        )
    else:
        out = refs[filled]
    out[...] = value.astype(bf16).reshape(out.shape)


def weight_grad(left, right, width, total, place=0, given=None, weight=None, weight_at=0, blocks=0, room=60, peers=0, more=0):
    depth, rows = left.shape
    block = 512 if width > 1024 else 1024
    blocks = blocks or right.shape[1] // width
    in_specs = [
        pl.BlockSpec((depth, block), lambda j, i: (0, i)),
        pl.BlockSpec((depth, width), lambda j, i: (0, j)),
    ]
    operands = [left, right]
    out_shape = [jax.ShapeDtypeStruct((rows, total), bf16)]
    out_specs = [pl.BlockSpec((block, width), lambda j, i: (i, j + place))]
    if peers:
        share = rows // peers
        out_shape = [jax.ShapeDtypeStruct((peers, share + more, total), bf16)]
        out_specs = [pl.BlockSpec((block // share, share, width), lambda j, i: (i, 0, j + place))]
    if weight is not None:
        in_specs.append(pl.BlockSpec((block, width), lambda j, i: (i, weight_at)))
        operands.append(weight)
        out_shape.append(jax.ShapeDtypeStruct((rows, lanes), f32))
        out_specs.append(pl.BlockSpec((block, lanes), lambda j, i: (i, 0)))
    aliases = {}
    if given is not None:
        aliases = {len(operands): 0}
        in_specs.append(pl.BlockSpec(memory_space=pl.ANY))
        operands.append(given)
    found = pl.pallas_call(
        partial(weight_kernel, weight is not None, given is not None),
        grid=(blocks, rows // block),
        out_shape=out_shape,
        in_specs=in_specs,
        out_specs=out_specs,
        input_output_aliases=aliases,
        cost_estimate=pl.CostEstimate(
            flops=2 * depth * rows * blocks * width,
            bytes_accessed=2 * (depth * rows + depth * blocks * width + rows * blocks * width),
            transcendentals=0,
        ),
        compiler_params=pltpu.CompilerParams(vmem_limit_bytes=room * 1024 * 1024),
    )(*operands)
    return found if weight is not None else found[0]


def shards(
    tokens,
    cotangent,
    mixer_gain,
    feedforward_gain,
    branch_weight,
    input_weight,
    output_weight,
    recurrence_gate,
    input_gate,
    conv_kernel,
    conv_bias,
    recurrence_bias,
    input_bias,
    decay_param,
    gate_weight,
    up_weight,
    down_weight,
    doc_starts,
):
    spans = lax.axis_size("z") * 2
    core = lax.axis_index("core")
    dp_index = lax.axis_index(dp)
    peers = lax.axis_size(dp)
    rows, seg, model = tokens.shape
    units = branch_weight.shape[1]
    width = up_to(units, lanes)
    hidden_width = gate_weight.shape[1]
    taps = conv_kernel.shape[0]
    block = recurrence_gate.shape[0]
    blocks = units // block
    share = units // peers
    sizes = Sizes(rows, seg, spans, width, taps)
    own, length, block_tokens = rows * seg, seg * spans, sizes.tokens
    depth = model // peers

    mine = jnp.reshape(dp_index, (1,)).astype(jnp.int32)

    unit_one = rms_unit(tokens.reshape(own, model).astype(f32))[0]
    gain_one = mixer_gain.astype(f32)
    gain_two = feedforward_gain.astype(f32)
    normed_one = (unit_one * gain_one).astype(bf16)
    one_near = ring_near(normed_one)
    one_far = ring_far(one_near)

    small = jnp.concatenate(
        [
            recurrence_gate,
            input_gate,
            conv_kernel,
            conv_bias[None],
            recurrence_bias[None],
            input_bias[None],
            decay_param[None],
        ],
        axis=0,
    ).T
    small_width = up_to(small.shape[1], lanes)
    small_rows = up_to(share, 8)
    small_all = gather_small(widen(widen(small, small_width, 1), small_rows, 0), dp)
    small_all = small_all[:, :share].reshape(units, small_width)
    front_weights = lax.all_gather(
        jnp.concatenate(
            [
                widen(input_weight, width, 1),
                widen(branch_weight, width, 1),
                widen(output_weight.T, width, 1),
            ],
            axis=1,
        ),
        dp,
        axis=0,
        tiled=True,
    )
    flat_one = ring_whole(one_far)
    cot_near = ring_near(tie(cotangent.reshape(own, model), one_far))
    back_weights = lax.all_gather(
        jnp.concatenate(tie_all((gate_weight, up_weight, down_weight.T), one_near), axis=1),
        dp,
        axis=0,
        tiled=True,
    )
    input_matrix = front_weights[:, :width]
    branch_matrix = front_weights[:, width : 2 * width]
    down_turned = back_weights[:, 2 * hidden_width :]
    def diagonal(turned):
        lines = [
            jnp.pad(
                turned[h * block : (h + 1) * block],
                ((0, 0), (h * block, width - (h + 1) * block)),
            )
            for h in range(blocks)
        ]
        return widen(jnp.concatenate(lines, axis=0), width, 0)

    table = jnp.concatenate(
        [diagonal(small_all[:, :block]), diagonal(small_all[:, block : 2 * block])], axis=0
    )
    vectors = widen(small_all[:, 2 * block : 2 * block + taps + 4].astype(f32).T, width, 1)
    decay_values = vectors[taps + 3]
    params = widen(
        jnp.concatenate([vectors[: taps + 3], jax.nn.softplus(-decay_values)[None]], axis=0),
        up_to(taps + 4, 8),
        0,
    )

    positions = dp_index * length - (taps - 1) + jnp.arange(length + taps - 1, dtype=jnp.int32)
    starts = jnp.any(doc_starts[:, :, None] == positions[None, None, :], axis=1).astype(f32)
    columns = [starts[:, taps - 1 :]]
    valid = jnp.ones((rows, length), f32)
    for tap in range(1, taps):
        valid = valid * (1.0 - starts[:, taps - tap : taps - tap + length])
        columns.append(valid)
    masks = jnp.stack(columns + [valid] * (8 - taps), axis=-1)
    masks = masks.reshape(rows, spans, seg, 8).transpose(2, 0, 1, 3).reshape(block_tokens, 8)

    conv_in = dot(flat_one, input_matrix)
    conv_ends = conv_in.reshape(spans, rows, seg, width)[spans - 1, :, seg - 8 :, :]
    tail = lax.ppermute(
        conv_ends.reshape(rows * 8, width), dp, [(i, i + 1) for i in range(peers - 1)]
    )
    conv_in, cot_near = lax.optimization_barrier((conv_in, cot_near))
    flat = (block_tokens, width)
    prefix_kind, edge_kind = ((2 * rows * spans, width), f32), ((8, width), f32)
    kinds = [(flat, f32)] * 3 + [(flat, bf16)] * 7
    *gate_parts, prefix, last = call(
        partial(gates_kernel, sizes),
        kinds + [prefix_kind, edge_kind],
        kinds + [((block_tokens // parts, width), f32), (flat, f32)]
        + [((block_tokens // parts, 2 * width), f32)],
        conv_in,
        tail,
        masks,
        table,
        params,
        out_anywhere=10,
        sems=[(10, parts)],
    )
    product, total, decay, conv_low, woven_low, direct_by, entry_by, state_by, rest_by, slope_by = gate_parts
    front_other = swap_cores(tie(front_weights, last))
    kept = {}

    def branch_work(operand):
        kept["branch"] = dot(operand, branch_matrix)
        return kept["branch"]

    cot_far = ring_far(cot_near, (tie(flat_one, last), branch_work))
    branch_pre, _ = lax.optimization_barrier((kept["branch"], cot_far[3:5]))
    gathered = gather_small(last, dp)
    mixer_in, recur_by, states_natural = call(
        partial(states_kernel, sizes, peers),
        [(flat, bf16), (flat, bf16), (flat, f32)],
        [(flat, f32)] * 2
        + [(flat, bf16)] * 2
        + [(flat, f32), (flat, bf16), (flat, bf16), (flat, f32), (flat, f32)],
        mine,
        gathered,
        prefix,
        product,
        total,
        state_by,
        rest_by,
        branch_pre,
        scalars=1,
        anywhere=range(3, 8),
        out_anywhere=3,
        sems=[(4, parts), (), (3, parts)],
    )
    own_kind = ((own, model), f32)
    own_low = ((own, model), bf16)
    tokens_own, cotangent_own = (part.reshape(own, model) for part in (tokens, cotangent))
    residual, normed_two = ring_scatter(
        mixer_in,
        swap_rows(mixer_in),
        front_weights,
        front_other,
        2,
        branch_body,
        (tokens_own, gain_two[None]),
        [own_kind, own_low],
    )

    flat_two = lax.all_gather(normed_two, ("core", "z"), axis=0, tiled=True)
    back_other = swap_cores(tie(back_weights, normed_two))
    cotangent_flat = ring_whole(tie_all(cot_far, normed_two))
    grad_hidden = dot(cotangent_flat, down_turned)
    flat_two, back_other = lax.optimization_barrier((flat_two, back_other))
    hidden, grad_gate_up, gate_up_send = feed_forward(
        1 - core, flat_two, grad_hidden, back_weights, True, ()
    )
    gate_up_got = swap_cores(gate_up_send)
    hidden, grad_gate_up = feed_forward(
        core, flat_two, grad_hidden, back_weights, False, (hidden, grad_gate_up)
    )
    feed_width = 3 * hidden_width

    def feed_part(operand):
        both, inner = operand
        part = weight_grad(flat_two, both, 2 * hidden_width, feed_width, room=40)
        kept["feed"] = weight_grad(
            cotangent_flat, inner, hidden_width, feed_width, 2, part, room=40
        )
        return kept["feed"]

    grad_residual, grad_branch_own, gain_two_rows = ring_scatter(
        grad_gate_up,
        gate_up_got,
        back_weights,
        back_other,
        0,
        feed_back_body,
        (residual, cotangent_own, gain_two[None]),
        [own_kind, own_low, ((8, model), f32)],
        None,
        ((grad_gate_up, hidden), feed_part),
    )
    feed_part, grad_branch_own = lax.optimization_barrier((kept["feed"], grad_branch_own))
    feed_grads = lax.psum_scatter(feed_part, dp, scatter_dimension=0, tiled=True)
    gain_two_part = jnp.sum(gain_two_rows, axis=0)
    near = ring_near(grad_branch_own)
    hidden_got = swap_rows(tie(hidden, near[0]))
    feed_operands = (hidden, hidden_got, back_weights, back_other, 2)
    low, high = far_pieces(feed_operands)
    ahead, behind, feed_own = near_pieces(feed_operands)
    far = ring_far(tie_all(near, low, feed_own))

    places = jnp.stack([lax.axis_index("z"), core]).astype(jnp.int32)

    grad_branch, grad_branch_pre, own_part, later_by, back_prefix, back_last = call(
        partial(reverse_kernel, sizes, 2),
        [((block_tokens, model), bf16), (flat, bf16)]
        + [(flat, f32)] * 2
        + [prefix_kind, edge_kind],
        [((block_tokens, model), bf16), (flat, bf16)]
        + [(flat, f32)] * 7
        + [((model, width), bf16)],
        places,
        branch_pre,
        states_natural,
        decay,
        front_weights,
        *far,
        scalars=1,
        anywhere=range(1, 5 + len(far)),
        out_anywhere=4,
        sems=[(4,), (len(far),), (3, parts), (2,)],
        takes=24,
    )
    back_gathered = gather_small(back_last, dp)

    def output_work(operand):
        kept["middle"] = weight_grad(operand, mixer_in, width, 2 * width)
        return kept["middle"]

    from_below, from_above = ring_step(low, high, (grad_branch, output_work))
    ahead, behind = near_sums(ahead, behind, from_below, from_above)
    sum_rows = up_to(taps + 4, 8)
    wide = (block_tokens, 2 * width)

    def gates_back(operand):
        gathered, kept["middle"] = operand
        kept["gates"] = call(
            partial(gates_back_kernel, sizes, peers),
            [
                (wide, bf16),
                (wide, bf16),
                ((rows * 8, width), f32),
                ((rows * 8, width), f32),
                ((sum_rows, width), f32),
            ],
            [(flat, f32)] * 2
            + [(flat, bf16)] * 5
            + [(wide, bf16), (wide, bf16)]
            + [(flat, f32)] * 3,
            mine,
            gathered,
            back_prefix,
            tail,
            masks,
            table,
            params,
            own_part,
            later_by,
            direct_by,
            entry_by,
            recur_by,
            slope_by,
            woven_low,
            grad_branch_pre,
            scalars=1,
            anywhere=range(7, 15),
            out_anywhere=2,
            sems=[(7, parts), (), (2, parts)],
            takes=11,
        )
        return kept["gates"][-1]

    below, above = ring_step(ahead, behind, ((back_gathered, kept["middle"]), gates_back))
    kept["gates"], below, above = lax.optimization_barrier((kept["gates"], below, above))
    grad_gates, grad_front, ends, head, sums = kept["gates"]
    from_next = lax.ppermute(head, dp, [(i + 1, i) for i in range(peers - 1)])
    middle_part, branch_sums = weight_grad(
        flat_one,
        tie(grad_branch_pre, head),
        width,
        2 * width,
        1,
        kept["middle"],
        front_weights,
        1,
    )
    from_next, middle_part = lax.optimization_barrier((from_next, middle_part))
    middle_half = lax.psum_scatter(
        tie(middle_part, feed_grads), dp[0], scatter_dimension=0, tiled=True
    )
    grad_front = lax.dynamic_update_slice(
        grad_front.reshape(spans, rows, seg, 2 * width),
        (ends + from_next).astype(bf16).reshape(1, rows, 8, width),
        (spans - 1, 0, seg - 8, 0),
    ).reshape(block_tokens, 2 * width)
    normed_got = swap_rows(grad_front)
    payload, input_sums = weight_grad(
        flat_one,
        grad_front,
        width,
        width,
        0,
        None,
        front_weights,
        0,
        1,
        peers=peers,
        more=small_rows,
    )
    payload, normed_got = lax.optimization_barrier((payload, normed_got))
    table_grads = dot(grad_gates, conv_low, 0, 0)

    def diagonal_back(turned):
        block_of = (jnp.arange(units) // block)[:, None]
        kept = turned[:units, :block]
        for h in range(1, blocks):
            kept = jnp.where(block_of == h, turned[:units, h * block : (h + 1) * block], kept)
        return kept

    small_grads = jnp.concatenate(
        [
            diagonal_back(table_grads[:width]),
            diagonal_back(table_grads[width:]),
            sums[:, :units].T,
        ],
        axis=1,
    )
    gain_one_part = jnp.sum(branch_sums + input_sums, axis=1) / gain_one
    gain_parts = jnp.stack([gain_one_part, gain_two_part]).reshape(2, spans // 2, 2, -1)
    gain_parts = gain_parts.transpose(2, 1, 0, 3)
    gain_keep = lax.dynamic_index_in_dim(gain_parts, core, 0, keepdims=False)
    gain_send = lax.dynamic_index_in_dim(gain_parts, 1 - core, 0, keepdims=False)
    gain_got = swap_cores(gain_send)
    normed_operands = (grad_front, normed_got, front_weights, front_other, 0)
    low, high, ahead, behind, normed_own = all_pieces(normed_operands)
    low, high, gain_got = lax.optimization_barrier((low, high, gain_got))

    def fill_payload(operand):
        payload_now, gain_sum = operand
        gain_parts = scatter_direct(gain_sum, "z")
        gain_share = model // spans // peers
        gain_parts = gain_parts.reshape(2, peers, gain_share).transpose(1, 0, 2)

        small_now = widen(small_grads, small_width, 1).reshape(peers, share, small_width)
        small_now = jnp.concatenate([small_now, widen(gain_parts, small_width, 2)], axis=1)
        payload = lax.dynamic_update_slice(payload_now, small_now.astype(bf16), (0, depth, 0))
        kept["payload"] = payload
        return payload

    from_below, from_above = ring_step(low, high, ((payload, gain_keep + gain_got), fill_payload))
    from_below, from_above, middle_half, payload = lax.optimization_barrier(
        (from_below, from_above, middle_half, kept["payload"])
    )
    kept["sent"] = lax.all_to_all(payload, dp, 0, 0)
    normed_below, normed_above = ring_step(*near_sums(ahead, behind, from_below, from_above), None)
    middle_grad = lax.psum_scatter(middle_half, dp[1], scatter_dimension=0, tiled=True)
    (tokens_grad,) = rows_call(
        tokens_body,
        (normed_own, normed_below, normed_above, tokens_own, grad_residual, gain_one[None]),
        [own_kind],
    )
    below, above = tie_all((below, above), tokens_grad)
    (layer_output,) = rows_call(feed_body, (feed_own, below, above, residual), [own_low])
    feed_grads = tie(feed_grads, normed_own).astype(f32)
    summed = jnp.sum(tie(kept["sent"], tokens_grad).astype(f32), axis=0)
    middle_grad, summed = lax.optimization_barrier((middle_grad, summed))
    middle_grad = middle_grad.astype(f32)
    input_grad, small_grads = summed[:depth], summed[depth:]
    gain_share = model // spans // peers
    gain_grads = small_grads[share : share + 2, :gain_share]
    small_grads = small_grads[:share].T
    rate_slope = jax.nn.sigmoid(-decay_param.astype(f32)) * decay_power
    at = 2 * block
    return (
        layer_output.reshape(rows, seg, model),
        tokens_grad.reshape(rows, seg, model),
        gain_grads[0],
        gain_grads[1],
        middle_grad[:, width : width + units],
        input_grad[:, :units],
        middle_grad[:, :units].T,
        small_grads[:block],
        small_grads[block:at],
        small_grads[at : at + taps],
        small_grads[at + taps],
        small_grads[at + taps + 1],
        small_grads[at + taps + 2],
        small_grads[at + taps + 3] * rate_slope,
        feed_grads[:, :hidden_width],
        feed_grads[:, hidden_width : 2 * hidden_width],
        feed_grads[:, 2 * hidden_width :].T,
    )


def solution(mesh):
    peers, group = mesh.devices.shape
    side = 4
    split = Mesh(
        mesh.devices.reshape(side, peers // side, group // 2, 2), dp + ("z", "core")
    )
    tokens_spec = P(None, dp + ("z", "core"), None)
    split_units = P(None, ("z", "core") + dp)
    split_vector = P(("z", "core") + dp)
    rows_first, units_first = P(dp, ("z", "core")), P(("z", "core"), dp)
    return jax.shard_map(
        shards,
        mesh=split,
        in_specs=(tokens_spec, tokens_spec, P(), P(), rows_first, rows_first, units_first)
        + (split_units,) * 3
        + (split_vector,) * 4
        + (rows_first, rows_first, units_first, P()),
        out_specs=(tokens_spec, tokens_spec, split_vector, split_vector)
        + (rows_first, rows_first, units_first)
        + (split_units,) * 3
        + (split_vector,) * 4
        + (rows_first, rows_first, units_first),
        check_vma=False,
    )
```

```python
from functools import partial

import jax
import jax.numpy as jnp
from jax import lax
from jax.experimental import pallas as pl
from jax.experimental.pallas import tpu as pltpu
from jax.sharding import Mesh
from jax.sharding import PartitionSpec as P

eps_norm = 1e-06
decay_power = 8.0
mult_eps = 0.001
gelu_scale = 0.7978845608028654
gelu_cubic = 0.044715
lanes = 128
f32 = jnp.float32
bf16 = jnp.bfloat16


def cost(microseconds):
    return pl.CostEstimate(
        flops=microseconds * 1_100_000_000, bytes_accessed=0, transcendentals=0
    )


no_cost = cost(0)


def up_to(count, step):
    return -(-count // step) * step


def widen(values, width, axis):
    pads = [(0, 0)] * values.ndim
    pads[axis] = (0, width - values.shape[axis])
    return jnp.pad(values, pads)


def rms_unit(values):
    inverse = lax.rsqrt(jnp.mean(values * values, axis=-1, keepdims=True) + eps_norm)
    return (values * inverse, inverse)


def norm_back(grad_normed, unit_values, inverse, gain):
    scaled = grad_normed * gain
    return inverse * (scaled - unit_values * jnp.mean(scaled * unit_values, axis=-1, keepdims=True))


def gelu_parts(values):
    squared = values * values
    tanh_value = jnp.tanh(gelu_scale * values * (1.0 + gelu_cubic * squared))
    half = 0.5 * (1.0 + tanh_value)
    slope = half + 0.5 * values * (1.0 - tanh_value * tanh_value) * gelu_scale * (
        1.0 + 3.0 * gelu_cubic * squared
    )
    return (values * half, slope)


def dot(left, right, left_axis=1, right_axis=0):
    return lax.dot_general(
        left, right, (((left_axis,), (right_axis,)), ((), ())), preferred_element_type=f32
    )


def send_copies(copies, axis):
    return lax.all_to_all(copies, axis, 0, 0)


def gather_small(value, axis):
    peers = lax.axis_size(axis)
    return lax.all_to_all(jnp.broadcast_to(value[None], (peers,) + value.shape), axis, 0, 0)


def scatter_sum(value, axis):
    return jnp.sum(lax.all_to_all(value, axis, 0, 0).astype(f32), axis=0)


def tie(value, *before):
    return lax.optimization_barrier((value,) + before)[0]


def tie_all(values, *before):
    return lax.optimization_barrier((values,) + before)[0]


def swap_cores(value):
    return lax.ppermute(value, "core", [(0, 1), (1, 0)])


def turn(value, by):
    count = lax.axis_size("z")
    return lax.ppermute(value, "z", [(i, (i + by) % count) for i in range(count)])


def ring_near(value):
    return (value, turn(value, 1), turn(value, -1), swap_cores(value))


def ring_far(near, work=None):
    value, below, above, other = near
    half = value.shape[0] // 2
    far_low, far_high = ring_step(below[:half], above[half:], work)
    swapped = [swap_cores(part) for part in (above, below, far_low, far_high)]
    return [value, above, below, far_low, far_high, other] + swapped


def ring_places(rows):
    half = rows // 2
    places = [(0, 0, rows), (1, 0, rows), (3, 0, rows), (2, 0, half), (2, half, half)]
    return [(by, side, at, size) for side in range(2) for by, at, size in places]


def ring_whole(pieces):
    count = lax.axis_size("z")
    z, core = lax.axis_index("z"), lax.axis_index("core")
    rows, columns = pieces[0].shape
    whole = jnp.zeros((2 * count * rows, columns), pieces[0].dtype)
    for piece, (by, side, first, _) in zip(pieces, ring_places(rows)):
        span = (1 - core if side else core) * count + lax.rem(z + by, count)
        whole = lax.dynamic_update_slice(whole, piece, (span * rows + first, 0))
    return whole


def scatter_direct(part, axis):
    count = lax.axis_size(axis)
    index = lax.axis_index(axis)

    def piece(by):
        return lax.dynamic_index_in_dim(part, lax.rem(index + by, count), 0, keepdims=False)

    found = piece(0).astype(f32)
    for by in range(1, count):
        pairs = [(i, (i + by) % count) for i in range(count)]
        found = found + lax.ppermute(piece(by), axis, pairs).astype(f32)
    return found


def ring_step(low, high, work):
    if work is None:
        return turn(low, 1), turn(high, -1)
    operand, function = work
    low, high, operand = lax.optimization_barrier((low, high, operand))
    below, above = turn(low, 1), turn(high, -1)
    below, above, _ = lax.optimization_barrier((below, above, function(operand)))
    return below, above


def far_pieces(operands, takes=0):
    model = operands[2].shape[0]
    half = operands[1].shape[0] // lax.axis_size("z") // 2
    return product_pieces((2,), *operands, [((half, model), bf16)] * 2, takes)


def near_pieces(operands, takes=0):
    model = operands[2].shape[0]
    rows = operands[1].shape[0] // lax.axis_size("z")
    return product_pieces((1, 3, 0), *operands, [((rows, model), f32)] * 3, takes, 24)


def all_pieces(operands, takes=0):
    model = operands[2].shape[0]
    rows = operands[1].shape[0] // lax.axis_size("z")
    outs = [((rows // 2, model), bf16)] * 2 + [((rows, model), f32)] * 3
    return product_pieces((2, 1, 3, 0), *operands, outs, takes)


def near_sums(ahead, behind, from_below, from_above):
    return rows_call(near_body, (ahead, behind, from_below, from_above), [(ahead.shape, bf16)] * 2)


def ring_scatter(x, got, weights, others, at, body, extra, outs, first=None, second=None, last=None):
    operands = (x, got, weights, others, at)
    if first is not None:
        low, high, ahead, behind, mine = all_pieces(operands, 9)
        below, above = ring_step(low, high, first)
    else:
        low, high = far_pieces(operands, 5)
        found = []

        def near_work(operand):
            found.extend(near_pieces(operand + operands[2:], 6))
            return found

        below, above = ring_step(low, high, ((x, got), near_work))
        ahead, behind, mine = found
    below, above = ring_step(*near_sums(ahead, behind, below, above), second)
    if last is not None:
        below, above = last(below, above)
    return rows_call(body, (mine, below, above) + extra, outs)


class Sizes:
    def __init__(self, rows, seg, spans, width, conv_width):
        self.rows, self.seg, self.spans = rows, seg, spans
        self.width, self.conv_width = width, conv_width
        self.stride = rows * seg
        self.tokens = spans * self.stride
    def pair(self, position):
        count = self.rows * self.spans
        return pl.ds(pl.multiple_of(position * count, count), count)


def weave(sizes, source, target, back=False):
    blocks = sizes.seg // 8

    def step(index, carried):
        row, block = index // blocks, index % blocks
        natural = [
            pl.ds(
                pl.multiple_of(
                    (span % 2 * (sizes.spans // 2) + span // 2) * sizes.stride
                    + row * sizes.seg
                    + block * 8,
                    8,
                ),
                8,
            )
            for span in range(sizes.spans)
        ]
        woven = [
            pl.ds(pl.multiple_of(((block * 8 + place) * sizes.rows + row) * sizes.spans, 8), 8)
            for place in range(8)
        ]
        reads, writes = (woven, natural) if back else (natural, woven)
        for start in range(0, sizes.width, lanes):
            columns = slice(start, start + lanes)
            tiles = jnp.stack([source[at, columns] for at in reads], axis=0)
            tiles = jnp.transpose(tiles, (1, 0, 2))
            for place, at in enumerate(writes):
                target[at, columns] = tiles[place]
        return carried

    lax.fori_loop(0, sizes.rows * blocks, step, 0)


def span_before(tile, first):
    place = lax.broadcasted_iota(jnp.int32, tile.shape, 0)
    return jnp.where(place == 0, first, pltpu.roll(tile, 1, 0))


def span_after(tile, last):
    count = tile.shape[0]
    place = lax.broadcasted_iota(jnp.int32, tile.shape, 0)
    return jnp.where(place == count - 1, last, pltpu.roll(tile, count - 1, 0))


def across_spans(product, total, backward):
    spans = product.shape[0]
    so_far = (jnp.ones_like(product[:1]), jnp.zeros_like(total[:1]))
    ahead = [None] * spans
    for span in range(spans - 1, -1, -1) if backward else range(spans):
        ahead[span] = so_far
        now = product[span : span + 1]
        so_far = (so_far[0] * now, total[span : span + 1] + now * so_far[1])
    products, totals = (jnp.concatenate(part, axis=0) for part in zip(*ahead))
    return products, totals, so_far


def from_others(sizes, index_ref, all_ref, peers, backward):
    mine = index_ref[0]
    entering = [jnp.zeros((1, sizes.width), f32) for _ in range(sizes.rows)]
    for step in range(peers - 1):
        peer = peers - 1 - step if backward else step
        ahead = peer > mine if backward else peer < mine
        for row in range(sizes.rows):
            product = all_ref[peer, row : row + 1, :]
            total = all_ref[peer, sizes.rows + row : sizes.rows + row + 1, :]
            entering[row] = jnp.where(ahead, total + product * entering[row], entering[row])
    return entering


def sigmoid(values):
    return 0.5 * jnp.tanh(0.5 * values) + 0.5


def keep_ends(sizes, found, prefix, last, backward):
    rows, spans = sizes.rows, sizes.spans
    ends = []
    for row in range(rows):
        mine = slice(row * spans, (row + 1) * spans)
        products, totals, whole = across_spans(found[0][mine], found[1][mine], backward)
        prefix[row * spans : (row + 1) * spans, :] = products
        prefix[(rows + row) * spans : (rows + row + 1) * spans, :] = totals
        ends.append(whole)
    padding = [jnp.zeros((last.shape[1] - 2 * rows, sizes.width), f32)]
    block = jnp.concatenate([end[0] for end in ends] + [end[1] for end in ends] + padding, axis=0)
    for peer in range(last.shape[0]):
        last[peer] = block


def entering_spans(sizes, prefix, entering):
    rows, spans = sizes.rows, sizes.spans
    return jnp.concatenate(
        [
            prefix[(rows + row) * spans : (rows + row + 1) * spans, :]
            + prefix[row * spans : (row + 1) * spans, :] * entering[row]
            for row in range(rows)
        ],
        axis=0,
    )


def per_row(sizes, function, pair, edges):
    spans = sizes.spans
    return jnp.concatenate(
        [function(pair[row * spans : (row + 1) * spans], edges[row]) for row in range(sizes.rows)],
        axis=0,
    )


parts = 4
dp = ("x", "y")


class Parts:
    def __init__(self, sources, targets, sems):
        self.pairs = list(zip(sources, targets))
        self.sems = sems

    def copy(self, which, part):
        source, target = self.pairs[which]
        count = source.shape[0] // parts
        at = pl.ds(pl.multiple_of(part * count, count), count)
        return pltpu.make_async_copy(source.at[at], target.at[at], self.sems.at[which, part])

    def start(self, part, which=None):
        for index in range(len(self.pairs)) if which is None else which:
            self.copy(index, part).start()

    def wait(self, part, which=None):
        for index in range(len(self.pairs)) if which is None else which:
            self.copy(index, part).wait()


def gates_kernel(sizes, conv_in, tail, masks, table, params, *refs):
    outs, refs = refs[:10], refs[10:]
    prefix, last, refs = refs[0], refs[1], refs[2:]
    held, refs = refs[:10], refs[10:]
    conv_now, conv_woven, mixed, sems = refs
    product, total, decay, conv_low, woven_low, direct_by, entry_by, state_by, rest_by, slope_by = held
    sent = Parts(held, outs, sems)
    seg, taps, width, spans = sizes.seg, sizes.conv_width, sizes.width, sizes.spans
    rows = sizes.rows
    bias = params[taps : taps + 1, :]
    weave(sizes, conv_in, conv_woven)
    before = []
    for tap in range(1, taps):
        edges = [tail[row * 8 + 8 - tap : row * 8 + 9 - tap, :] for row in range(rows)]
        before.append(per_row(sizes, span_before, conv_woven[sizes.pair(seg - tap), :], edges))
    recur_bias = params[taps + 1 : taps + 2, :]
    entry_bias = params[taps + 2 : taps + 3, :]
    rate = params[taps + 3 : taps + 4, :] * (-decay_power)
    per_part = seg // parts
    part_rows = per_part * rows * spans

    def part_step(part, carried):
        before, found = carried

        def conv_step(step, before):
            at = sizes.pair(part * per_part + step)
            valid = masks[at, :]
            tile = conv_woven[at, :]
            value = bias + params[0:1, :] * tile
            for tap in range(1, taps):
                value = value + params[tap : tap + 1, :] * before[tap - 1] * (
                    valid[:, tap : tap + 1]
                )
            conv_now[sizes.pair(step), :] = value
            conv_low[at, :] = value.astype(bf16)
            woven_low[at, :] = tile.astype(bf16)
            return (tile,) + tuple(before[:-1])

        before = lax.fori_loop(0, per_part, conv_step, before, unroll=8)
        part_at = pl.ds(pl.multiple_of(part * part_rows, part_rows), part_rows)
        mixed[...] = dot(conv_low[part_at, :], table[...], 1, 1)

        def gate_step(step, carried):
            at = sizes.pair(part * per_part + step)
            here = sizes.pair(step)
            starting = jnp.broadcast_to(masks[at, :][:, 0:1], (rows * spans, width)) > 0.5
            recur_now = sigmoid(mixed[here, :width] + recur_bias)
            entry_now = sigmoid(mixed[here, width:] + entry_bias)
            conv_here = conv_now[here, :]
            decay_now = jnp.where(starting, 0.0, jnp.exp(rate * recur_now))
            squared = 1.0 - decay_now * decay_now + mult_eps
            root = lax.rsqrt(squared)
            scale = jnp.where(starting, 1.0, squared * root)
            direct = scale * entry_now
            gated = entry_now * conv_here
            by_state = decay_now * recur_now
            product_now = carried[0] * decay_now
            total_now = carried[1] * decay_now + direct * conv_here
            product[at, :] = product_now
            total[at, :] = total_now
            decay[at, :] = decay_now
            direct_by[at, :] = direct.astype(bf16)
            entry_by[at, :] = (scale * gated * (1.0 - entry_now)).astype(bf16)
            state_by[at, :] = by_state.astype(bf16)
            rest_by[at, :] = (by_state * gated * decay_now * root).astype(bf16)
            slope_by[at, :] = (rate * (1.0 - recur_now)).astype(bf16)
            return (product_now, total_now)

        found = lax.fori_loop(0, per_part, gate_step, found, unroll=8)
        sent.start(part)
        return (before, found)

    shape = (rows * spans, width)
    first = (jnp.ones(shape, f32), jnp.zeros(shape, f32))
    _, found = lax.fori_loop(0, parts, part_step, (tuple(before), first))
    keep_ends(sizes, found, prefix, last, False)
    for part in range(parts):
        sent.wait(part)


def states_kernel(sizes, peers, index, gathered, prefix, *refs):
    sources, pre_hbm, outs, refs = refs[:4], refs[4], refs[5:8], refs[8:]
    held, refs = refs[:4], refs[4:]
    product, total, state_by, rest_by = held
    branch_pre, mixer_in, recur_by, natural, states, in_sems, pre_sem, out_sems = refs
    taken = Parts(sources, held, in_sems)
    sent = Parts((mixer_in, recur_by, natural), outs, out_sems)
    pre_copy = pltpu.make_async_copy(pre_hbm, branch_pre, pre_sem)
    for part in range(parts):
        taken.start(part, (0, 1))
    pre_copy.start()
    for part in range(parts):
        taken.start(part, (2, 3))
    rows, spans, seg = sizes.rows, sizes.spans, sizes.seg
    entering = from_others(sizes, index, gathered, peers, False)
    spans_in = entering_spans(sizes, prefix, entering)
    per_part = seg // parts
    for part in range(parts):
        taken.wait(part, (0, 1))

        def state_step(step, carried, part=part):
            at = sizes.pair(part * per_part + step)
            states[at, :] = total[at, :] + product[at, :] * spans_in
            return carried

        lax.fori_loop(0, per_part, state_step, 0, unroll=4)
    weave(sizes, states, natural, True)
    for part in range(parts):
        sent.start(part, (2,))
    pre_copy.wait()
    step_rows = 32
    steps = sizes.tokens // parts // step_rows

    def act_part(part, carried):
        def act_step(step, carried):
            start = pl.multiple_of((part * steps + step) * step_rows, step_rows)
            at = pl.ds(start, step_rows)
            mixer_in[at, :] = (natural[at, :] * gelu_parts(branch_pre[at, :])[0]).astype(bf16)
            return carried

        lax.fori_loop(0, steps, act_step, 0, unroll=2)
        sent.start(part, (0,))
        return carried

    lax.fori_loop(0, parts, act_part, 0)
    before = per_row(sizes, span_before, states[sizes.pair(seg - 1), :], entering)
    for part in range(parts):
        taken.wait(part, (2, 3))

    def recur_part(part, before):
        def recur_step(step, before):
            at = sizes.pair(part * per_part + step)
            found = before * state_by[at, :].astype(f32) - rest_by[at, :].astype(f32)
            recur_by[at, :] = found.astype(bf16)
            return states[at, :]

        before = lax.fori_loop(0, per_part, recur_step, before, unroll=4)
        sent.start(part, (1,))
        return before

    lax.fori_loop(0, parts, recur_part, before)
    for part in range(parts):
        sent.wait(part)


def reverse_kernel(
    sizes, out_at, place, pre_hbm, natural_hbm, decay_hbm, weights_hbm, *refs
):
    places = ring_places(sizes.stride)
    pieces, refs = refs[: len(places)], refs[len(places) :]
    outs, prefix, last, refs = refs[:4], refs[4], refs[5], refs[6:]
    grad_branch, grad_branch_pre, own_part, later_by, grad_states = refs[:5]
    branch_pre, natural, decay, grad_mixer, weights = refs[5:10]
    in_sems, piece_sems, out_sems, branch_sems = refs[10:]
    width, spans = sizes.width, sizes.spans
    z, core = place[0], place[1]
    stride = sizes.stride
    copies = []
    for number, (piece, (by, side, first, count)) in enumerate(zip(pieces, places)):
        span = (1 - core if side else core) * (spans // 2) + lax.rem(z + by, spans // 2)
        at = pl.ds(pl.multiple_of(span * stride + first, sizes.seg), count)
        copy = pltpu.make_async_copy(piece, grad_branch.at[at], piece_sems.at[number])
        copies.append((side, copy))
    taken = [
        pltpu.make_async_copy(source, target, in_sems.at[number])
        for number, (source, target) in enumerate(
            (
                (weights_hbm.at[:, out_at * width : (out_at + 1) * width], weights),
                (pre_hbm, branch_pre),
                (natural_hbm, natural),
                (decay_hbm, decay),
            )
        )
    ]
    taken[0].start()
    for _, copy in copies:
        copy.start()
    for copy in taken[1:]:
        copy.start()
    taken[0].wait()
    half = sizes.tokens // 2
    branch_out = []
    for side in range(2):
        for piece_side, copy in copies:
            if piece_side == side:
                copy.wait()
        at = pl.ds(pl.multiple_of((1 - core if side else core) * half, half), half)
        out = pltpu.make_async_copy(grad_branch.at[at], outs[0].at[at], branch_sems.at[side])
        out.start()
        branch_out.append(out)
        grad_mixer[at, :] = dot(grad_branch[at, :], weights[...])
    taken[1].wait()
    taken[2].wait()
    sent = Parts((grad_branch_pre, own_part, later_by), outs[1:], out_sems)
    step_rows = 32
    steps = sizes.tokens // parts // step_rows

    def part_step(part, carried):
        def gelu_step(step, carried):
            start = pl.multiple_of((part * steps + step) * step_rows, step_rows)
            at = pl.ds(start, step_rows)
            grad = grad_mixer[at, :]
            act, slope = gelu_parts(branch_pre[at, :])
            grad_branch_pre[at, :] = (grad * natural[at, :] * slope).astype(bf16)
            grad_mixer[at, :] = grad * act
            return carried

        lax.fori_loop(0, steps, gelu_step, 0, unroll=2)
        sent.start(part, (0,))
        return carried

    lax.fori_loop(0, parts, part_step, 0)
    weave(sizes, grad_mixer, grad_states)
    taken[3].wait()
    per_part = sizes.seg // parts

    def scan_part(index, carried):
        part = parts - 1 - index

        def scan_step(step, carried):
            at = sizes.pair(part * per_part + per_part - 1 - step)
            decay_now = decay[at, :]
            own = carried[1] + grad_states[at, :]
            own_part[at, :] = own
            later_by[at, :] = carried[0]
            return (carried[0] * decay_now, own * decay_now)

        carried = lax.fori_loop(0, per_part, scan_step, carried, unroll=4)
        sent.start(part, (1, 2))
        return carried

    shape = (sizes.rows * spans, width)
    first = (jnp.ones(shape, f32), jnp.zeros(shape, f32))
    found = lax.fori_loop(0, parts, scan_part, first)
    keep_ends(sizes, found, prefix, last, True)
    for part in range(parts):
        sent.wait(part)
    for out in branch_out:
        out.wait()


def gates_back_kernel(sizes, peers, index, gathered, prefix, tail, masks, table, params, *refs):
    sources, branch_hbm, refs = refs[:7], refs[7], refs[8:]
    outs, ends, head, sums, refs = refs[:2], refs[2], refs[3], refs[4], refs[5:]
    held, refs = refs[:7], refs[7:]
    grad_gates, grad_front, grad_conv, grad_conv_in, natural = refs[:5]
    in_sems, branch_sem, out_sems = refs[5:]
    own_part, later_by, direct_by, entry_by, recur_by, slope_by, woven_low = held
    seg, taps, width, spans = sizes.seg, sizes.conv_width, sizes.width, sizes.spans
    rows = sizes.rows
    taken = Parts(sources, held, in_sems)
    branch_copy = pltpu.make_async_copy(
        branch_hbm, grad_front.at[:, width : 2 * width], branch_sem
    )
    for part in range(2):
        taken.start(part, range(6))
    entering = from_others(sizes, index, gathered, peers, True)
    spans_in = entering_spans(sizes, prefix, entering)
    shape = (rows * spans, width)

    def gate_step(position, carried):
        at = sizes.pair(position)
        rate_sum, recur_sum, entry_sum = carried
        direct, entry, recur, slope = (
            ref[at, :].astype(f32) for ref in (direct_by, entry_by, recur_by, slope_by)
        )
        carried_now = own_part[at, :] + later_by[at, :] * spans_in
        rated = carried_now * recur
        recur_low = (rated * slope).astype(bf16)
        entry_low = (carried_now * entry).astype(bf16)
        grad_gates[at, :width] = recur_low
        grad_gates[at, width:] = entry_low
        grad_conv[at, :] = carried_now * direct
        return (
            rate_sum + rated,
            recur_sum + recur_low.astype(f32),
            entry_sum + entry_low.astype(f32),
        )

    empty = jnp.zeros(shape, f32)
    gate_sums = (empty,) * 3
    per_part = seg // parts
    part_rows = per_part * rows * spans
    sent = Parts((grad_gates, grad_front), outs, out_sems)
    for part in range(parts):
        taken.wait(part, range(6))
        if part + 2 < parts:
            taken.start(part + 2, range(6))
        elif part + 2 == parts:
            for later in range(parts):
                taken.start(later, (6,))
        else:
            branch_copy.start()
        gate_sums = lax.fori_loop(
            part * per_part, (part + 1) * per_part, gate_step, gate_sums, unroll=4
        )
        sent.start(part, (0,))
        at = pl.ds(part * part_rows, part_rows)
        grad_conv[at, :] = grad_conv[at, :] + dot(grad_gates[at, :], table[...], 1, 0)

    def weighted(position):
        at = sizes.pair(position)
        grad = grad_conv[at, :]
        valid = masks[at, :]
        return [grad] + [grad * valid[:, tap : tap + 1] for tap in range(1, taps)]

    tap_rows = [params[tap : tap + 1, :] for tap in range(taps)]
    ahead = [weighted(position) for position in range(taps - 1)]
    nothing_after = [jnp.zeros((1, width), f32)] * rows
    held_ahead = [
        per_row(sizes, span_after, ahead[place][tap], nothing_after)
        for tap in range(1, taps)
        for place in range(tap)
    ]

    def conv_step(index, carried):
        held_now, now_sums = carried
        at = sizes.pair(seg - 1 - index)
        tile = woven_low[at, :].astype(f32)
        now = weighted(seg - 1 - index)
        value = tap_rows[0] * now[0]
        new_held, new_sums, first = [], [now_sums[0] + tile * now[0]], 0
        for tap in range(1, taps):
            far = held_now[first + tap - 1]
            value = value + tap_rows[tap] * far
            new_sums.append(now_sums[tap] + tile * far)
            new_held += [now[tap]] + list(held_now[first : first + tap - 1])
            first += tap
        new_sums.append(now_sums[taps] + now[0])
        grad_conv_in[at, :] = value
        return tuple(new_held), tuple(new_sums)

    for part in range(parts):
        taken.wait(part, (6,))
    held_ahead, tap_sums = lax.fori_loop(
        0, seg, conv_step, (tuple(held_ahead), (empty,) * (taps + 1)), unroll=8
    )
    tap_sums = list(tap_sums)
    head[...] = jnp.zeros(head.shape, f32)
    for row in range(rows):
        for back in range(1, taps):
            value = jnp.zeros((1, width), f32)
            tail_row = tail[row * 8 + 8 - back : row * 8 + 9 - back, :]
            first = 0
            for tap in range(1, taps):
                if tap >= back:
                    first_row = held_ahead[first + tap - back][row * spans : row * spans + 1]
                    value = value + tap_rows[tap] * first_row
                    tap_sums[tap] = tap_sums[tap] + jnp.concatenate(
                        [tail_row * first_row, jnp.zeros((rows * spans - 1, width), f32)], axis=0
                    )
                first += tap
            head[row * 8 + 8 - back : row * 8 + 9 - back, :] = value
    weave(sizes, grad_conv_in, natural, True)
    branch_copy.wait()
    step_rows = 32
    steps = sizes.tokens // parts // step_rows

    def part_step(part, carried):
        def front_step(step, carried):
            start = pl.multiple_of((part * steps + step) * step_rows, step_rows)
            at = pl.ds(start, step_rows)
            grad_front[at, :width] = natural[at, :].astype(bf16)
            return carried

        lax.fori_loop(0, steps, front_step, 0, unroll=4)
        sent.start(part, (1,))
        return carried

    lax.fori_loop(0, parts, part_step, 0)
    for row in range(rows):
        end = (spans - 1) * sizes.stride + (row + 1) * seg
        ends[row * 8 : row * 8 + 8, :] = natural[end - 8 : end, :]
    for place, part_sum in enumerate(tap_sums + [gate_sums[1], gate_sums[2], gate_sums[0]]):
        sums[place : place + 1, :] = jnp.sum(part_sum, axis=0, keepdims=True)
    for part in range(parts):
        sent.wait(part)


def rows_kernel(body, inputs, *refs):
    ins, outs = refs[:inputs], refs[inputs:]
    rows, step_rows = ins[0].shape[0], 32
    for start in range(0, rows, step_rows):
        body(start, slice(start, start + step_rows), ins, outs)


def rows_call(body, ins, outs):
    vmem = pl.BlockSpec(memory_space=pltpu.VMEM)
    return pl.pallas_call(
        partial(rows_kernel, body, len(ins)),
        out_shape=[jax.ShapeDtypeStruct(shape, kind) for shape, kind in outs],
        in_specs=[vmem] * len(ins),
        out_specs=[vmem] * len(outs),
        cost_estimate=no_cost,
        compiler_params=pltpu.CompilerParams(vmem_limit_bytes=20 * 1024 * 1024),
    )(*ins)


def near_body(start, at, ins, outs):
    half = ins[2].shape[0]
    ahead, behind = ins[0][at, :], ins[1][at, :]
    if start < half:
        ahead = ahead + ins[2][at, :].astype(f32)
    else:
        behind = behind + ins[3][start - half : start - half + behind.shape[0], :].astype(f32)
    outs[0][at, :] = ahead.astype(bf16)
    outs[1][at, :] = behind.astype(bf16)


def own_sum(at, ins):
    return ins[0][at, :] + ins[1][at, :].astype(f32) + ins[2][at, :].astype(f32)


def branch_body(start, at, ins, outs):
    residual = own_sum(at, ins) + ins[3][at, :].astype(f32)
    outs[0][at, :] = residual
    outs[1][at, :] = (rms_unit(residual)[0] * ins[4][...]).astype(bf16)


def feed_back_body(start, at, ins, outs):
    grad = own_sum(at, ins)
    unit, inverse = rms_unit(ins[3][at, :])
    found = ins[4][at, :].astype(f32) + norm_back(grad, unit, inverse, ins[5][...])
    outs[0][at, :] = found
    outs[1][at, :] = found.astype(bf16)
    part = jnp.sum((grad * unit).reshape(-1, 8, grad.shape[1]), axis=0)
    outs[2][...] = part if start == 0 else outs[2][...] + part


def feed_body(start, at, ins, outs):
    outs[0][at, :] = (own_sum(at, ins) + ins[3][at, :]).astype(bf16)


def tokens_body(start, at, ins, outs):
    grad = own_sum(at, ins)
    unit, inverse = rms_unit(ins[3][at, :].astype(f32))
    outs[0][at, :] = ins[4][at, :] + norm_back(grad, unit, inverse, ins[5][...])


def call(kernel, outs, scratch, *operands, scalars=0, anywhere=(), out_anywhere=0, sems=(), takes=0):
    vmem = pl.BlockSpec(memory_space=pltpu.VMEM)
    hbm = pl.BlockSpec(memory_space=pl.ANY)
    in_specs = [pl.BlockSpec(memory_space=pltpu.SMEM)] * scalars
    in_specs += [vmem] * (len(operands) - scalars)
    for index in anywhere:
        in_specs[index] = hbm
    return pl.pallas_call(
        kernel,
        out_shape=[jax.ShapeDtypeStruct(shape, kind) for shape, kind in outs],
        in_specs=in_specs,
        out_specs=[hbm] * out_anywhere + [vmem] * (len(outs) - out_anywhere),
        scratch_shapes=[pltpu.VMEM(shape, kind) for shape, kind in scratch]
        + [pltpu.SemaphoreType.DMA(shape) for shape in sems],
        cost_estimate=cost(takes),
        compiler_params=pltpu.CompilerParams(vmem_limit_bytes=60 * 1024 * 1024),
    )(*operands)


def product_kernel(at, bys, place, x_hbm, got_hbm, own_hbm, other_hbm, *refs):
    outs, (x, weights, x_sem, weight_sem) = refs[:-4], refs[-4:]
    depth = got_hbm.shape[1]
    span = x.shape[0] // len(bys)
    rows = got_hbm.shape[0]
    columns = 512
    steps = weights.shape[0] // columns
    halves = (slice(0, depth), slice(depth, 2 * depth))

    def weight_copies(index):
        place = slice(index * columns, (index + 1) * columns)
        return [
            pltpu.make_async_copy(
                source.at[place, at * depth : (at + 1) * depth],
                weights.at[place, half],
                weight_sem.at[2 * index + side],
            )
            for side, (source, half) in enumerate(zip((own_hbm, other_hbm), halves))
        ]

    x_copies = []
    for number, by in enumerate(bys):
        first = lax.rem(place[0] + by, rows // span) * span
        to = slice(number * span, (number + 1) * span)
        mine = pl.ds(pl.multiple_of(place[1] * rows + first, span), span)
        theirs = pl.ds(pl.multiple_of(first, span), span)
        x_copies += [
            pltpu.make_async_copy(x_hbm.at[mine], x.at[to, halves[0]], x_sem.at[2 * number]),
            pltpu.make_async_copy(
                got_hbm.at[theirs], x.at[to, halves[1]], x_sem.at[2 * number + 1]
            ),
        ]
    for side in range(2):
        for copy in x_copies[side::2]:
            copy.start()
        weight_copies(0)[side].start()
    for copy in weight_copies(1):
        copy.start()
    for index in range(steps):
        place_now = slice(index * columns, (index + 1) * columns)
        if index == 0:
            value = 0.0
            for side, half in enumerate(halves):
                for copy in x_copies[side::2]:
                    copy.wait()
                weight_copies(0)[side].wait()
                value = value + dot(x[:, half], weights[place_now, half], 1, 1)
        else:
            for copy in weight_copies(index):
                copy.wait()
        if index + 2 < steps:
            for copy in weight_copies(index + 2):
                copy.start()
        if index > 0:
            value = dot(x[...], weights[place_now, :], 1, 1)
        first = 0
        for out in outs:
            out[:, place_now] = value[first : first + out.shape[0]].astype(out.dtype)
            first += out.shape[0]


def product_pieces(bys, x, got, weights, others, at, outs, takes, room=60):
    depth, model = got.shape[1], weights.shape[0]
    span = got.shape[0] // lax.axis_size("z")
    place = jnp.stack([lax.axis_index("z"), lax.axis_index("core")]).astype(jnp.int32)
    anywhere = pl.BlockSpec(memory_space=pl.ANY)
    return pl.pallas_call(
        partial(product_kernel, at, bys),
        out_shape=[jax.ShapeDtypeStruct(shape, kind) for shape, kind in outs],
        in_specs=[pl.BlockSpec(memory_space=pltpu.SMEM)] + [anywhere] * 4,
        out_specs=[pl.BlockSpec(memory_space=pltpu.VMEM)] * len(outs),
        scratch_shapes=[
            pltpu.VMEM((len(bys) * span, 2 * depth), bf16),
            pltpu.VMEM((model, 2 * depth), bf16),
            pltpu.SemaphoreType.DMA((2 * len(bys),)),
            pltpu.SemaphoreType.DMA((2 * model // 512,)),
        ],
        cost_estimate=cost(takes),
        compiler_params=pltpu.CompilerParams(vmem_limit_bytes=room * 1024 * 1024),
    )(place, x, got, weights, others)


def swap_rows(x):
    rows = x.shape[0] // 2
    theirs = (1 - lax.axis_index("core")) * rows
    return swap_cores(lax.dynamic_slice_in_dim(x, theirs, rows, 0))


def feed_kernel(aliased, sends, core, x_hbm, grad_hbm, weights_hbm, *refs):
    refs = refs[aliased:]
    hidden_hbm, both_hbm, refs = refs[0], refs[1], refs[2:]
    if sends:
        send_hbm, refs = refs[0], refs[1:]
    x, grad, weights, pre, hidden, both, in_sem, weight_sem, out_sem = refs
    rows = x.shape[0]
    inner = grad.shape[1]
    mine = pl.ds(pl.multiple_of(core[0] * rows, rows), rows)
    copies = [
        pltpu.make_async_copy(x_hbm.at[mine], x, in_sem.at[0]),
        pltpu.make_async_copy(grad_hbm.at[mine], grad, in_sem.at[1]),
    ]
    columns = weights.shape[2]
    count = 2 * inner // columns

    def weight_copy(index):
        at = slice(index * columns, (index + 1) * columns)
        return pltpu.make_async_copy(
            weights_hbm.at[:, at], weights.at[index], weight_sem.at[index]
        )

    copies[0].start()
    for index in range(count):
        weight_copy(index).start()
    copies[1].start()
    copies[0].wait()
    for index in range(count):
        weight_copy(index).wait()
        pre[:, index * columns : (index + 1) * columns] = dot(x[...], weights[index])
    copies[1].wait()
    step_rows = 32
    outs = []

    def out_copies(part):
        size = rows // parts
        here = pl.ds(pl.multiple_of(part * size, size), size)
        there = pl.ds(pl.multiple_of(core[0] * rows + part * size, size), size)
        found = [
            pltpu.make_async_copy(hidden.at[here], hidden_hbm.at[there], out_sem.at[part, 0]),
            pltpu.make_async_copy(both.at[here], both_hbm.at[there], out_sem.at[part, 1]),
        ]
        if sends:
            found.append(
                pltpu.make_async_copy(both.at[here], send_hbm.at[here], out_sem.at[part, 2])
            )
        return found

    steps = rows // parts // step_rows

    def part_step(part, carried):
        def act_step(step, carried):
            start = pl.multiple_of((part * steps + step) * step_rows, step_rows)
            at = pl.ds(start, step_rows)
            act, slope = gelu_parts(pre[at, :inner])
            up = pre[at, inner:]
            grad_now = grad[at, :]
            hidden[at, :] = (act * up).astype(bf16)
            both[at, :inner] = (grad_now * up * slope).astype(bf16)
            both[at, inner:] = (grad_now * act).astype(bf16)
            return carried

        lax.fori_loop(0, steps, act_step, 0)
        for copy in out_copies(part):
            copy.start()
        return carried

    lax.fori_loop(0, parts, part_step, 0)
    for part in range(parts):
        for copy in out_copies(part):
            copy.wait()


def feed_forward(core, flat, grad_hidden, weights, sends, given):
    tokens, model = flat.shape
    inner = grad_hidden.shape[1]
    rows = tokens // 2
    columns = 512
    anywhere = pl.BlockSpec(memory_space=pl.ANY)
    outs = [(tokens, inner), (tokens, 2 * inner)] + [(rows, 2 * inner)] * sends
    return pl.pallas_call(
        partial(feed_kernel, len(given), sends),
        out_shape=[jax.ShapeDtypeStruct(shape, bf16) for shape in outs],
        in_specs=[pl.BlockSpec(memory_space=pltpu.SMEM)] + [anywhere] * (3 + len(given)),
        out_specs=[anywhere] * len(outs),
        scratch_shapes=[
            pltpu.VMEM((rows, model), bf16),
            pltpu.VMEM((rows, inner), f32),
            pltpu.VMEM((2 * inner // columns, model, columns), bf16),
            pltpu.VMEM((rows, 2 * inner), f32),
            pltpu.VMEM((rows, inner), bf16),
            pltpu.VMEM((rows, 2 * inner), bf16),
            pltpu.SemaphoreType.DMA((2,)),
            pltpu.SemaphoreType.DMA((2 * inner // columns,)),
            pltpu.SemaphoreType.DMA((parts, 3)),
        ],
        input_output_aliases={4: 0, 5: 1} if given else {},
        cost_estimate=cost(8),
        compiler_params=pltpu.CompilerParams(vmem_limit_bytes=60 * 1024 * 1024),
    )(
        jnp.reshape(core, (1,)).astype(jnp.int32),
        flat,
        grad_hidden,
        weights,
        *given,
    )


def weight_kernel(with_sums, filled, left, right, *refs):
    value = dot(left[...], right[...], 0, 0)
    if with_sums:
        weight, (out, sums) = refs[0], refs[1 + filled :]
        product = value * weight[...].astype(f32)
        sums[...] = sum(
            product[:, start : start + lanes] for start in range(0, product.shape[1], lanes)
        )
    else:
        out = refs[filled]
    out[...] = value.astype(bf16).reshape(out.shape)


def weight_grad(left, right, width, total, place=0, given=None, weight=None, weight_at=0, blocks=0, room=60, peers=0, more=0):
    depth, rows = left.shape
    block = 512 if width > 1024 else 1024
    blocks = blocks or right.shape[1] // width
    in_specs = [
        pl.BlockSpec((depth, block), lambda j, i: (0, i)),
        pl.BlockSpec((depth, width), lambda j, i: (0, j)),
    ]
    operands = [left, right]
    out_shape = [jax.ShapeDtypeStruct((rows, total), bf16)]
    out_specs = [pl.BlockSpec((block, width), lambda j, i: (i, j + place))]
    if peers:
        share = rows // peers
        out_shape = [jax.ShapeDtypeStruct((peers, share + more, total), bf16)]
        out_specs = [pl.BlockSpec((block // share, share, width), lambda j, i: (i, 0, j + place))]
    if weight is not None:
        in_specs.append(pl.BlockSpec((block, width), lambda j, i: (i, weight_at)))
        operands.append(weight)
        out_shape.append(jax.ShapeDtypeStruct((rows, lanes), f32))
        out_specs.append(pl.BlockSpec((block, lanes), lambda j, i: (i, 0)))
    aliases = {}
    if given is not None:
        aliases = {len(operands): 0}
        in_specs.append(pl.BlockSpec(memory_space=pl.ANY))
        operands.append(given)
    found = pl.pallas_call(
        partial(weight_kernel, weight is not None, given is not None),
        grid=(blocks, rows // block),
        out_shape=out_shape,
        in_specs=in_specs,
        out_specs=out_specs,
        input_output_aliases=aliases,
        cost_estimate=pl.CostEstimate(
            flops=2 * depth * rows * blocks * width,
            bytes_accessed=2 * (depth * rows + depth * blocks * width + rows * blocks * width),
            transcendentals=0,
        ),
        compiler_params=pltpu.CompilerParams(vmem_limit_bytes=room * 1024 * 1024),
    )(*operands)
    return found if weight is not None else found[0]


def shards(
    tokens,
    cotangent,
    mixer_gain,
    feedforward_gain,
    branch_weight,
    input_weight,
    output_weight,
    recurrence_gate,
    input_gate,
    conv_kernel,
    conv_bias,
    recurrence_bias,
    input_bias,
    decay_param,
    gate_weight,
    up_weight,
    down_weight,
    doc_starts,
):
    spans = lax.axis_size("z") * 2
    core = lax.axis_index("core")
    dp_index = lax.axis_index(dp)
    peers = lax.axis_size(dp)
    rows, seg, model = tokens.shape
    units = branch_weight.shape[1]
    width = up_to(units, lanes)
    hidden_width = gate_weight.shape[1]
    taps = conv_kernel.shape[0]
    block = recurrence_gate.shape[0]
    blocks = units // block
    share = units // peers
    sizes = Sizes(rows, seg, spans, width, taps)
    own, length, block_tokens = rows * seg, seg * spans, sizes.tokens
    depth = model // peers

    mine = jnp.reshape(dp_index, (1,)).astype(jnp.int32)

    unit_one = rms_unit(tokens.reshape(own, model).astype(f32))[0]
    gain_one = mixer_gain.astype(f32)
    gain_two = feedforward_gain.astype(f32)
    normed_one = (unit_one * gain_one).astype(bf16)
    one_near = ring_near(normed_one)
    one_far = ring_far(one_near)

    small = jnp.concatenate(
        tie_all(
            [
                recurrence_gate,
                input_gate,
                conv_kernel,
                conv_bias[None],
                recurrence_bias[None],
                input_bias[None],
                decay_param[None],
            ],
            normed_one,
        ),
        axis=0,
    ).T
    small_width = up_to(small.shape[1], lanes)
    small_rows = up_to(share, 8)
    small_all = gather_small(widen(widen(small, small_width, 1), small_rows, 0), dp)
    small_all = small_all[:, :share].reshape(units, small_width)
    front_weights = lax.all_gather(
        jnp.concatenate(
            [
                widen(input_weight, width, 1),
                widen(branch_weight, width, 1),
                widen(output_weight.T, width, 1),
            ],
            axis=1,
        ),
        dp,
        axis=0,
        tiled=True,
    )
    flat_one = ring_whole(one_far)
    cot_near = ring_near(tie(cotangent.reshape(own, model), one_far))
    def back_parts(weights):
        return jnp.concatenate([weights[0], weights[1], weights[2].T], axis=1)

    back_weights = lax.all_gather(
        back_parts(tie_all((gate_weight, up_weight, down_weight), one_near)),
        dp,
        axis=0,
        tiled=True,
    )
    input_matrix = front_weights[:, :width]
    branch_matrix = front_weights[:, width : 2 * width]
    down_turned = back_weights[:, 2 * hidden_width :]
    def diagonal(turned):
        lines = [
            jnp.pad(
                turned[h * block : (h + 1) * block],
                ((0, 0), (h * block, width - (h + 1) * block)),
            )
            for h in range(blocks)
        ]
        return widen(jnp.concatenate(lines, axis=0), width, 0)

    table = jnp.concatenate(
        [diagonal(small_all[:, :block]), diagonal(small_all[:, block : 2 * block])], axis=0
    )
    vectors = widen(small_all[:, 2 * block : 2 * block + taps + 4].astype(f32).T, width, 1)
    decay_values = vectors[taps + 3]
    params = widen(
        jnp.concatenate([vectors[: taps + 3], jax.nn.softplus(-decay_values)[None]], axis=0),
        up_to(taps + 4, 8),
        0,
    )

    positions = dp_index * length - (taps - 1) + jnp.arange(length + taps - 1, dtype=jnp.int32)
    starts = jnp.any(doc_starts[:, :, None] == positions[None, None, :], axis=1).astype(f32)
    columns = [starts[:, taps - 1 :]]
    valid = jnp.ones((rows, length), f32)
    for tap in range(1, taps):
        valid = valid * (1.0 - starts[:, taps - tap : taps - tap + length])
        columns.append(valid)
    masks = jnp.stack(columns + [valid] * (8 - taps), axis=-1)
    masks = masks.reshape(rows, spans, seg, 8).transpose(2, 0, 1, 3).reshape(block_tokens, 8)

    conv_in = dot(flat_one, input_matrix)
    conv_ends = conv_in.reshape(spans, rows, seg, width)[spans - 1, :, seg - 8 :, :]
    tail = lax.ppermute(
        conv_ends.reshape(rows * 8, width), dp, [(i, i + 1) for i in range(peers - 1)]
    )
    conv_in, cot_near = lax.optimization_barrier((conv_in, cot_near))
    flat = (block_tokens, width)
    prefix_kind, edge_kind = ((2 * rows * spans, width), f32), ((peers, 8, width), f32)
    kinds = [(flat, f32)] * 3 + [(flat, bf16)] * 7
    *gate_parts, prefix, last = call(
        partial(gates_kernel, sizes),
        kinds + [prefix_kind, edge_kind],
        kinds + [((block_tokens // parts, width), f32), (flat, f32)]
        + [((block_tokens // parts, 2 * width), f32)],
        conv_in,
        tail,
        masks,
        table,
        params,
        out_anywhere=10,
        sems=[(10, parts)],
    )
    product, total, decay, conv_low, woven_low, direct_by, entry_by, state_by, rest_by, slope_by = gate_parts
    front_other = swap_cores(tie(front_weights, last))
    kept = {}

    def branch_work(operand):
        kept["branch"] = dot(operand, branch_matrix)
        return kept["branch"]

    cot_far = ring_far(cot_near, (tie(flat_one, last), branch_work))
    branch_pre, _ = lax.optimization_barrier((kept["branch"], cot_far[3:5]))
    gathered = send_copies(last, dp)
    mixer_in, recur_by, states_natural = call(
        partial(states_kernel, sizes, peers),
        [(flat, bf16), (flat, bf16), (flat, f32)],
        [(flat, f32)] * 2
        + [(flat, bf16)] * 2
        + [(flat, f32), (flat, bf16), (flat, bf16), (flat, f32), (flat, f32)],
        mine,
        gathered,
        prefix,
        product,
        total,
        state_by,
        rest_by,
        branch_pre,
        scalars=1,
        anywhere=range(3, 8),
        out_anywhere=3,
        sems=[(4, parts), (), (3, parts)],
    )
    own_kind = ((own, model), f32)
    own_low = ((own, model), bf16)
    tokens_own, cotangent_own = (part.reshape(own, model) for part in (tokens, cotangent))
    residual, normed_two = ring_scatter(
        mixer_in,
        swap_rows(mixer_in),
        front_weights,
        front_other,
        2,
        branch_body,
        (tokens_own, gain_two[None]),
        [own_kind, own_low],
    )

    flat_two = lax.all_gather(normed_two, ("core", "z"), axis=0, tiled=True)
    back_other = swap_cores(tie(back_weights, normed_two))
    cotangent_flat = ring_whole(tie_all(cot_far, normed_two))
    grad_hidden = dot(cotangent_flat, down_turned)
    flat_two, back_other = lax.optimization_barrier((flat_two, back_other))
    hidden, grad_gate_up, gate_up_send = feed_forward(
        1 - core, flat_two, grad_hidden, back_weights, True, ()
    )
    gate_up_got = swap_cores(gate_up_send)
    hidden, grad_gate_up = feed_forward(
        core, flat_two, grad_hidden, back_weights, False, (hidden, grad_gate_up)
    )
    feed_width = 3 * hidden_width

    def gate_up_part(operand):
        kept["feed"] = weight_grad(flat_two, operand, 2 * hidden_width, feed_width)
        return kept["feed"]

    def down_part(operand):
        kept["feed"] = weight_grad(
            cotangent_flat, operand, hidden_width, feed_width, 2, kept["feed"], room=40
        )
        return kept["feed"]

    def feed_scatter(below, above):
        below, above, part = lax.optimization_barrier((below, above, kept["feed"]))
        kept["feed"] = lax.psum_scatter(part, dp, scatter_dimension=0, tiled=True)
        return below, above

    grad_residual, grad_branch_own, gain_two_rows = ring_scatter(
        grad_gate_up,
        gate_up_got,
        back_weights,
        back_other,
        0,
        feed_back_body,
        (residual, cotangent_own, gain_two[None]),
        [own_kind, own_low, ((8, model), f32)],
        (grad_gate_up, gate_up_part),
        (hidden, down_part),
        feed_scatter,
    )
    feed_grads = kept["feed"]
    gain_two_part = jnp.sum(gain_two_rows, axis=0)
    near = ring_near(grad_branch_own)
    hidden_got = swap_rows(tie(hidden, near[0]))
    feed_operands = (hidden, hidden_got, back_weights, back_other, 2)
    low, high, ahead, behind, feed_own = all_pieces(feed_operands)
    far = ring_far(tie_all(near, low, feed_own))

    places = jnp.stack([lax.axis_index("z"), core]).astype(jnp.int32)

    grad_branch, grad_branch_pre, own_part, later_by, back_prefix, back_last = call(
        partial(reverse_kernel, sizes, 2),
        [((block_tokens, model), bf16), (flat, bf16)]
        + [(flat, f32)] * 2
        + [prefix_kind, edge_kind],
        [((block_tokens, model), bf16), (flat, bf16)]
        + [(flat, f32)] * 7
        + [((model, width), bf16)],
        places,
        branch_pre,
        states_natural,
        decay,
        front_weights,
        *far,
        scalars=1,
        anywhere=range(1, 5 + len(far)),
        out_anywhere=4,
        sems=[(4,), (len(far),), (3, parts), (2,)],
        takes=24,
    )
    back_gathered = send_copies(back_last, dp)

    def output_work(operand):
        kept["middle"] = weight_grad(operand, mixer_in, width, 2 * width)
        return kept["middle"]

    from_below, from_above = ring_step(low, high, (grad_branch, output_work))
    ahead, behind = near_sums(ahead, behind, from_below, from_above)
    sum_rows = up_to(taps + 4, 8)
    wide = (block_tokens, 2 * width)

    def gates_back(operand):
        gathered, kept["middle"] = operand
        kept["gates"] = call(
            partial(gates_back_kernel, sizes, peers),
            [
                (wide, bf16),
                (wide, bf16),
                ((rows * 8, width), f32),
                ((rows * 8, width), f32),
                ((sum_rows, width), f32),
            ],
            [(flat, f32)] * 2
            + [(flat, bf16)] * 5
            + [(wide, bf16), (wide, bf16)]
            + [(flat, f32)] * 3,
            mine,
            gathered,
            back_prefix,
            tail,
            masks,
            table,
            params,
            own_part,
            later_by,
            direct_by,
            entry_by,
            recur_by,
            slope_by,
            woven_low,
            grad_branch_pre,
            scalars=1,
            anywhere=range(7, 15),
            out_anywhere=2,
            sems=[(7, parts), (), (2, parts)],
            takes=11,
        )
        return kept["gates"][-1]

    below, above = ring_step(ahead, behind, ((back_gathered, kept["middle"]), gates_back))
    kept["gates"], below, above = lax.optimization_barrier((kept["gates"], below, above))
    grad_gates, grad_front, ends, head, sums = kept["gates"]
    from_next = lax.ppermute(head, dp, [(i + 1, i) for i in range(peers - 1)])
    middle_part, branch_sums = weight_grad(
        flat_one,
        tie(grad_branch_pre, head),
        width,
        2 * width,
        1,
        kept["middle"],
        front_weights,
        1,
    )
    from_next, middle_part = lax.optimization_barrier((from_next, middle_part))
    middle_half = lax.psum_scatter(
        tie(middle_part, feed_grads), dp[0], scatter_dimension=0, tiled=True
    )
    grad_front = lax.dynamic_update_slice(
        grad_front.reshape(spans, rows, seg, 2 * width),
        (ends + from_next).astype(bf16).reshape(1, rows, 8, width),
        (spans - 1, 0, seg - 8, 0),
    ).reshape(block_tokens, 2 * width)
    normed_got = swap_rows(grad_front)
    payload, input_sums = weight_grad(
        flat_one,
        grad_front,
        width,
        width,
        0,
        None,
        front_weights,
        0,
        1,
        peers=peers,
        more=small_rows,
    )
    payload, normed_got = lax.optimization_barrier((payload, normed_got))
    table_grads = dot(grad_gates, conv_low, 0, 0)

    def diagonal_back(turned):
        block_of = (jnp.arange(units) // block)[:, None]
        kept = turned[:units, :block]
        for h in range(1, blocks):
            kept = jnp.where(block_of == h, turned[:units, h * block : (h + 1) * block], kept)
        return kept

    small_grads = jnp.concatenate(
        [
            diagonal_back(table_grads[:width]),
            diagonal_back(table_grads[width:]),
            sums[:, :units].T,
        ],
        axis=1,
    )
    gain_one_part = jnp.sum(branch_sums + input_sums, axis=1) / gain_one
    gain_parts = jnp.stack([gain_one_part, gain_two_part]).reshape(2, spans // 2, 2, -1)
    gain_parts = gain_parts.transpose(2, 1, 0, 3)
    gain_keep = lax.dynamic_index_in_dim(gain_parts, core, 0, keepdims=False)
    gain_send = lax.dynamic_index_in_dim(gain_parts, 1 - core, 0, keepdims=False)
    gain_got = swap_cores(gain_send)
    normed_operands = (grad_front, normed_got, front_weights, front_other, 0)
    low, high, ahead, behind, normed_own = all_pieces(normed_operands)
    low, high, gain_got = lax.optimization_barrier((low, high, gain_got))

    def fill_payload(operand):
        payload_now, gain_sum = operand
        gain_parts = scatter_direct(gain_sum, "z")
        gain_share = model // spans // peers
        gain_parts = gain_parts.reshape(2, peers, gain_share).transpose(1, 0, 2)

        small_now = widen(small_grads, small_width, 1).reshape(peers, share, small_width)
        small_now = jnp.concatenate([small_now, widen(gain_parts, small_width, 2)], axis=1)
        payload = lax.dynamic_update_slice(payload_now, small_now.astype(bf16), (0, depth, 0))
        kept["payload"] = payload
        return payload

    from_below, from_above = ring_step(low, high, ((payload, gain_keep + gain_got), fill_payload))
    from_below, from_above, middle_half, payload = lax.optimization_barrier(
        (from_below, from_above, middle_half, kept["payload"])
    )
    middle_grad = lax.psum_scatter(middle_half, dp[1], scatter_dimension=0, tiled=True)

    kept["sent"] = lax.all_to_all(payload, dp, 0, 0)
    normed_below, normed_above = ring_step(*near_sums(ahead, behind, from_below, from_above), None)
    (tokens_grad,) = rows_call(
        tokens_body,
        (normed_own, normed_below, normed_above, tokens_own, grad_residual, gain_one[None]),
        [own_kind],
    )
    below, above = tie_all((below, above), tokens_grad)
    (layer_output,) = rows_call(feed_body, (feed_own, below, above, residual), [own_low])
    feed_grads = tie(feed_grads, normed_own).astype(f32)
    middle_grad = middle_grad.astype(f32)
    summed = jnp.sum(tie(kept["sent"], tokens_grad).astype(f32), axis=0)
    input_grad, small_grads = summed[:depth], summed[depth:]
    gain_share = model // spans // peers
    gain_grads = small_grads[share : share + 2, :gain_share]
    small_grads = small_grads[:share].T
    rate_slope = jax.nn.sigmoid(-decay_param.astype(f32)) * decay_power
    at = 2 * block
    return (
        layer_output.reshape(rows, seg, model),
        tokens_grad.reshape(rows, seg, model),
        gain_grads[0],
        gain_grads[1],
        middle_grad[:, width : width + units],
        input_grad[:, :units],
        middle_grad[:, :units].T,
        small_grads[:block],
        small_grads[block:at],
        small_grads[at : at + taps],
        small_grads[at + taps],
        small_grads[at + taps + 1],
        small_grads[at + taps + 2],
        small_grads[at + taps + 3] * rate_slope,
        feed_grads[:, :hidden_width],
        feed_grads[:, hidden_width : 2 * hidden_width],
        feed_grads[:, 2 * hidden_width :].T,
    )


def solution(mesh):
    peers, group = mesh.devices.shape
    side = 4
    split = Mesh(
        mesh.devices.reshape(side, peers // side, group // 2, 2), dp + ("z", "core")
    )
    tokens_spec = P(None, dp + ("z", "core"), None)
    split_units = P(None, ("z", "core") + dp)
    split_vector = P(("z", "core") + dp)
    rows_first, units_first = P(dp, ("z", "core")), P(("z", "core"), dp)
    return jax.shard_map(
        shards,
        mesh=split,
        in_specs=(tokens_spec, tokens_spec, P(), P(), rows_first, rows_first, units_first)
        + (split_units,) * 3
        + (split_vector,) * 4
        + (rows_first, rows_first, units_first, P()),
        out_specs=(tokens_spec, tokens_spec, split_vector, split_vector)
        + (rows_first, rows_first, units_first)
        + (split_units,) * 3
        + (split_vector,) * 4
        + (rows_first, rows_first, units_first),
        check_vma=False,
    )
```

```python
from functools import partial

import jax
import jax.numpy as jnp
from jax import lax
from jax.experimental import pallas as pl
from jax.experimental.pallas import tpu as pltpu
from jax.sharding import Mesh
from jax.sharding import PartitionSpec as P

eps_norm = 1e-06
decay_power = 8.0
mult_eps = 0.001
gelu_scale = 0.7978845608028654
gelu_cubic = 0.044715
lanes = 128
f32 = jnp.float32
bf16 = jnp.bfloat16


def cost(microseconds):
    return pl.CostEstimate(
        flops=microseconds * 1_100_000_000, bytes_accessed=0, transcendentals=0
    )


no_cost = cost(0)


def up_to(count, step):
    return -(-count // step) * step


def widen(values, width, axis):
    pads = [(0, 0)] * values.ndim
    pads[axis] = (0, width - values.shape[axis])
    return jnp.pad(values, pads)


def rms_unit(values):
    inverse = lax.rsqrt(jnp.mean(values * values, axis=-1, keepdims=True) + eps_norm)
    return (values * inverse, inverse)


def norm_back(grad_normed, unit_values, inverse, gain):
    scaled = grad_normed * gain
    return inverse * (scaled - unit_values * jnp.mean(scaled * unit_values, axis=-1, keepdims=True))


def gelu_parts(values):
    squared = values * values
    tanh_value = jnp.tanh(gelu_scale * values * (1.0 + gelu_cubic * squared))
    half = 0.5 * (1.0 + tanh_value)
    slope = half + 0.5 * values * (1.0 - tanh_value * tanh_value) * gelu_scale * (
        1.0 + 3.0 * gelu_cubic * squared
    )
    return (values * half, slope)


def dot(left, right, left_axis=1, right_axis=0):
    return lax.dot_general(
        left, right, (((left_axis,), (right_axis,)), ((), ())), preferred_element_type=f32
    )


def send_copies(copies, axis):
    return lax.all_to_all(copies, axis, 0, 0)


def gather_small(value, axis):
    peers = lax.axis_size(axis)
    return lax.all_to_all(jnp.broadcast_to(value[None], (peers,) + value.shape), axis, 0, 0)


def scatter_sum(value, axis):
    return jnp.sum(lax.all_to_all(value, axis, 0, 0).astype(f32), axis=0)


def tie(value, *before):
    return lax.optimization_barrier((value,) + before)[0]


def tie_all(values, *before):
    return lax.optimization_barrier((values,) + before)[0]


def swap_cores(value):
    return lax.ppermute(value, "core", [(0, 1), (1, 0)])


def turn(value, by):
    count = lax.axis_size("z")
    return lax.ppermute(value, "z", [(i, (i + by) % count) for i in range(count)])


def ring_near(value):
    return (value, turn(value, 1), turn(value, -1), swap_cores(value))


def ring_far(near, work=None):
    value, below, above, other = near
    half = value.shape[0] // 2
    far_low, far_high = ring_step(below[:half], above[half:], work)
    swapped = [swap_cores(part) for part in (above, below, far_low, far_high)]
    return [value, above, below, far_low, far_high, other] + swapped


def ring_places(rows):
    half = rows // 2
    places = [(0, 0, rows), (1, 0, rows), (3, 0, rows), (2, 0, half), (2, half, half)]
    return [(by, side, at, size) for side in range(2) for by, at, size in places]


def ring_whole(pieces):
    count = lax.axis_size("z")
    z, core = lax.axis_index("z"), lax.axis_index("core")
    rows, columns = pieces[0].shape
    whole = jnp.zeros((2 * count * rows, columns), pieces[0].dtype)
    for piece, (by, side, first, _) in zip(pieces, ring_places(rows)):
        span = (1 - core if side else core) * count + lax.rem(z + by, count)
        whole = lax.dynamic_update_slice(whole, piece, (span * rows + first, 0))
    return whole


def scatter_direct(part, axis):
    count = lax.axis_size(axis)
    index = lax.axis_index(axis)

    def piece(by):
        return lax.dynamic_index_in_dim(part, lax.rem(index + by, count), 0, keepdims=False)

    found = piece(0).astype(f32)
    for by in range(1, count):
        pairs = [(i, (i + by) % count) for i in range(count)]
        found = found + lax.ppermute(piece(by), axis, pairs).astype(f32)
    return found


def ring_step(low, high, work):
    if work is None:
        return turn(low, 1), turn(high, -1)
    operand, function = work
    low, high, operand = lax.optimization_barrier((low, high, operand))
    below, above = turn(low, 1), turn(high, -1)
    below, above, _ = lax.optimization_barrier((below, above, function(operand)))
    return below, above


def far_pieces(operands, takes=0):
    model = operands[2].shape[0]
    half = operands[1].shape[0] // lax.axis_size("z") // 2
    return product_pieces((2,), *operands, [((half, model), bf16)] * 2, takes)


def near_pieces(operands, takes=0):
    model = operands[2].shape[0]
    rows = operands[1].shape[0] // lax.axis_size("z")
    return product_pieces((1, 3, 0), *operands, [((rows, model), f32)] * 3, takes, 24)


def all_pieces(operands, takes=0):
    model = operands[2].shape[0]
    rows = operands[1].shape[0] // lax.axis_size("z")
    outs = [((rows // 2, model), bf16)] * 2 + [((rows, model), f32)] * 3
    return product_pieces((2, 1, 3, 0), *operands, outs, takes)


def near_sums(ahead, behind, from_below, from_above):
    return rows_call(near_body, (ahead, behind, from_below, from_above), [(ahead.shape, bf16)] * 2)


def ring_scatter(x, got, weights, others, at, body, extra, outs, first=None, second=None, last=None):
    operands = (x, got, weights, others, at)
    if first is not None:
        low, high, ahead, behind, mine = all_pieces(operands, 9)
        below, above = ring_step(low, high, first)
    else:
        low, high = far_pieces(operands, 5)
        found = []

        def near_work(operand):
            found.extend(near_pieces(operand + operands[2:], 6))
            return found

        below, above = ring_step(low, high, ((x, got), near_work))
        ahead, behind, mine = found
    below, above = ring_step(*near_sums(ahead, behind, below, above), second)
    if last is not None:
        below, above = last(below, above)
    return rows_call(body, (mine, below, above) + extra, outs)


class Sizes:
    def __init__(self, rows, seg, spans, width, conv_width):
        self.rows, self.seg, self.spans = rows, seg, spans
        self.width, self.conv_width = width, conv_width
        self.stride = rows * seg
        self.tokens = spans * self.stride
    def pair(self, position):
        count = self.rows * self.spans
        return pl.ds(pl.multiple_of(position * count, count), count)


def weave(sizes, source, target, back=False):
    blocks = sizes.seg // 8

    def step(index, carried):
        row, block = index // blocks, index % blocks
        natural = [
            pl.ds(
                pl.multiple_of(
                    (span % 2 * (sizes.spans // 2) + span // 2) * sizes.stride
                    + row * sizes.seg
                    + block * 8,
                    8,
                ),
                8,
            )
            for span in range(sizes.spans)
        ]
        woven = [
            pl.ds(pl.multiple_of(((block * 8 + place) * sizes.rows + row) * sizes.spans, 8), 8)
            for place in range(8)
        ]
        reads, writes = (woven, natural) if back else (natural, woven)
        for start in range(0, sizes.width, lanes):
            columns = slice(start, start + lanes)
            tiles = jnp.stack([source[at, columns] for at in reads], axis=0)
            tiles = jnp.transpose(tiles, (1, 0, 2))
            for place, at in enumerate(writes):
                target[at, columns] = tiles[place]
        return carried

    lax.fori_loop(0, sizes.rows * blocks, step, 0)


def span_before(tile, first):
    place = lax.broadcasted_iota(jnp.int32, tile.shape, 0)
    return jnp.where(place == 0, first, pltpu.roll(tile, 1, 0))


def span_after(tile, last):
    count = tile.shape[0]
    place = lax.broadcasted_iota(jnp.int32, tile.shape, 0)
    return jnp.where(place == count - 1, last, pltpu.roll(tile, count - 1, 0))


def across_spans(product, total, backward):
    spans = product.shape[0]
    so_far = (jnp.ones_like(product[:1]), jnp.zeros_like(total[:1]))
    ahead = [None] * spans
    for span in range(spans - 1, -1, -1) if backward else range(spans):
        ahead[span] = so_far
        now = product[span : span + 1]
        so_far = (so_far[0] * now, total[span : span + 1] + now * so_far[1])
    products, totals = (jnp.concatenate(part, axis=0) for part in zip(*ahead))
    return products, totals, so_far


def from_others(sizes, index_ref, all_ref, peers, backward):
    mine = index_ref[0]
    entering = [jnp.zeros((1, sizes.width), f32) for _ in range(sizes.rows)]
    for step in range(peers - 1):
        peer = peers - 1 - step if backward else step
        ahead = peer > mine if backward else peer < mine
        for row in range(sizes.rows):
            product = all_ref[peer, row : row + 1, :]
            total = all_ref[peer, sizes.rows + row : sizes.rows + row + 1, :]
            entering[row] = jnp.where(ahead, total + product * entering[row], entering[row])
    return entering


def sigmoid(values):
    return 0.5 * jnp.tanh(0.5 * values) + 0.5


def keep_ends(sizes, found, prefix, last, backward):
    rows, spans = sizes.rows, sizes.spans
    ends = []
    for row in range(rows):
        mine = slice(row * spans, (row + 1) * spans)
        products, totals, whole = across_spans(found[0][mine], found[1][mine], backward)
        prefix[row * spans : (row + 1) * spans, :] = products
        prefix[(rows + row) * spans : (rows + row + 1) * spans, :] = totals
        ends.append(whole)
    padding = [jnp.zeros((last.shape[1] - 2 * rows, sizes.width), f32)]
    block = jnp.concatenate([end[0] for end in ends] + [end[1] for end in ends] + padding, axis=0)
    for peer in range(last.shape[0]):
        last[peer] = block


def entering_spans(sizes, prefix, entering):
    rows, spans = sizes.rows, sizes.spans
    return jnp.concatenate(
        [
            prefix[(rows + row) * spans : (rows + row + 1) * spans, :]
            + prefix[row * spans : (row + 1) * spans, :] * entering[row]
            for row in range(rows)
        ],
        axis=0,
    )


def per_row(sizes, function, pair, edges):
    spans = sizes.spans
    return jnp.concatenate(
        [function(pair[row * spans : (row + 1) * spans], edges[row]) for row in range(sizes.rows)],
        axis=0,
    )


parts = 4
dp = ("x", "y")


class Parts:
    def __init__(self, sources, targets, sems):
        self.pairs = list(zip(sources, targets))
        self.sems = sems

    def copy(self, which, part):
        source, target = self.pairs[which]
        count = source.shape[0] // parts
        at = pl.ds(pl.multiple_of(part * count, count), count)
        return pltpu.make_async_copy(source.at[at], target.at[at], self.sems.at[which, part])

    def start(self, part, which=None):
        for index in range(len(self.pairs)) if which is None else which:
            self.copy(index, part).start()

    def wait(self, part, which=None):
        for index in range(len(self.pairs)) if which is None else which:
            self.copy(index, part).wait()


def gates_kernel(sizes, conv_in, tail, masks, table, params, *refs):
    outs, refs = refs[:10], refs[10:]
    prefix, last, refs = refs[0], refs[1], refs[2:]
    held, refs = refs[:10], refs[10:]
    conv_now, conv_woven, mixed, sems = refs
    product, total, decay, conv_low, woven_low, direct_by, entry_by, state_by, rest_by, slope_by = held
    sent = Parts(held, outs, sems)
    seg, taps, width, spans = sizes.seg, sizes.conv_width, sizes.width, sizes.spans
    rows = sizes.rows
    bias = params[taps : taps + 1, :]
    weave(sizes, conv_in, conv_woven)
    before = []
    for tap in range(1, taps):
        edges = [tail[row * 8 + 8 - tap : row * 8 + 9 - tap, :] for row in range(rows)]
        before.append(per_row(sizes, span_before, conv_woven[sizes.pair(seg - tap), :], edges))
    recur_bias = params[taps + 1 : taps + 2, :]
    entry_bias = params[taps + 2 : taps + 3, :]
    rate = params[taps + 3 : taps + 4, :] * (-decay_power)
    per_part = seg // parts
    part_rows = per_part * rows * spans

    def part_step(part, carried):
        before, found = carried

        def conv_step(step, before):
            at = sizes.pair(part * per_part + step)
            valid = masks[at, :]
            tile = conv_woven[at, :]
            value = bias + params[0:1, :] * tile
            for tap in range(1, taps):
                value = value + params[tap : tap + 1, :] * before[tap - 1] * (
                    valid[:, tap : tap + 1]
                )
            conv_now[sizes.pair(step), :] = value
            conv_low[at, :] = value.astype(bf16)
            woven_low[at, :] = tile.astype(bf16)
            return (tile,) + tuple(before[:-1])

        before = lax.fori_loop(0, per_part, conv_step, before, unroll=8)
        part_at = pl.ds(pl.multiple_of(part * part_rows, part_rows), part_rows)
        mixed[...] = dot(conv_low[part_at, :], table[...], 1, 1)

        def gate_step(step, carried):
            at = sizes.pair(part * per_part + step)
            here = sizes.pair(step)
            starting = jnp.broadcast_to(masks[at, :][:, 0:1], (rows * spans, width)) > 0.5
            recur_now = sigmoid(mixed[here, :width] + recur_bias)
            entry_now = sigmoid(mixed[here, width:] + entry_bias)
            conv_here = conv_now[here, :]
            decay_now = jnp.where(starting, 0.0, jnp.exp(rate * recur_now))
            squared = 1.0 - decay_now * decay_now + mult_eps
            root = lax.rsqrt(squared)
            scale = jnp.where(starting, 1.0, squared * root)
            direct = scale * entry_now
            gated = entry_now * conv_here
            by_state = decay_now * recur_now
            product_now = carried[0] * decay_now
            total_now = carried[1] * decay_now + direct * conv_here
            product[at, :] = product_now
            total[at, :] = total_now
            decay[at, :] = decay_now
            direct_by[at, :] = direct.astype(bf16)
            entry_by[at, :] = (scale * gated * (1.0 - entry_now)).astype(bf16)
            state_by[at, :] = by_state.astype(bf16)
            rest_by[at, :] = (by_state * gated * decay_now * root).astype(bf16)
            slope_by[at, :] = (rate * (1.0 - recur_now)).astype(bf16)
            return (product_now, total_now)

        found = lax.fori_loop(0, per_part, gate_step, found, unroll=8)
        sent.start(part)
        return (before, found)

    shape = (rows * spans, width)
    first = (jnp.ones(shape, f32), jnp.zeros(shape, f32))
    _, found = lax.fori_loop(0, parts, part_step, (tuple(before), first))
    keep_ends(sizes, found, prefix, last, False)
    for part in range(parts):
        sent.wait(part)


def states_kernel(sizes, peers, index, gathered, prefix, *refs):
    sources, pre_hbm, outs, entered, refs = refs[:2], refs[2], refs[3:5], refs[5], refs[6:]
    product, total, branch_pre, mixer_in, natural, states, in_sems, pre_sem, out_sems = refs
    taken = Parts(sources, (product, total), in_sems)
    sent = Parts((mixer_in, natural), outs, out_sems)
    pre_copy = pltpu.make_async_copy(pre_hbm, branch_pre, pre_sem)
    for part in range(parts):
        taken.start(part)
    pre_copy.start()
    entering = from_others(sizes, index, gathered, peers, False)
    entered[...] = jnp.zeros(entered.shape, f32)
    for row in range(sizes.rows):
        entered[row : row + 1, :] = entering[row]
    spans_in = entering_spans(sizes, prefix, entering)
    per_part = sizes.seg // parts
    for part in range(parts):
        taken.wait(part)

        def state_step(step, carried, part=part):
            at = sizes.pair(part * per_part + step)
            states[at, :] = total[at, :] + product[at, :] * spans_in
            return carried

        lax.fori_loop(0, per_part, state_step, 0, unroll=8)
    weave(sizes, states, natural, True)
    for part in range(parts):
        sent.start(part, (1,))
    pre_copy.wait()
    step_rows = 32
    steps = sizes.tokens // parts // step_rows

    def act_part(part, carried):
        def act_step(step, carried):
            start = pl.multiple_of((part * steps + step) * step_rows, step_rows)
            at = pl.ds(start, step_rows)
            mixer_in[at, :] = (natural[at, :] * gelu_parts(branch_pre[at, :])[0]).astype(bf16)
            return carried

        lax.fori_loop(0, steps, act_step, 0, unroll=4)
        sent.start(part, (0,))
        return carried

    lax.fori_loop(0, parts, act_part, 0)
    for part in range(parts):
        sent.wait(part)


def recur_kernel(sizes, entered, *refs):
    sources, out, refs = refs[:3], refs[3], refs[4:]
    natural, state_by, rest_by, recur_by, states, in_sems, out_sems = refs
    taken = Parts(sources, (natural, state_by, rest_by), in_sems)
    sent = Parts((recur_by,), (out,), out_sems)
    for which in range(3):
        for part in range(parts):
            taken.start(part, (which,))
    for part in range(parts):
        taken.wait(part)
    weave(sizes, natural, states)
    entering = [entered[row : row + 1, :] for row in range(sizes.rows)]
    before = per_row(sizes, span_before, states[sizes.pair(sizes.seg - 1), :], entering)
    per_part = sizes.seg // parts

    def recur_part(part, before):
        def recur_step(step, before):
            at = sizes.pair(part * per_part + step)
            found = before * state_by[at, :].astype(f32) - rest_by[at, :].astype(f32)
            recur_by[at, :] = found.astype(bf16)
            return states[at, :]

        before = lax.fori_loop(0, per_part, recur_step, before, unroll=8)
        sent.start(part)
        return before

    lax.fori_loop(0, parts, recur_part, before)
    for part in range(parts):
        sent.wait(part)


def reverse_kernel(
    sizes, out_at, place, pre_hbm, natural_hbm, decay_hbm, weights_hbm, *refs
):
    places = ring_places(sizes.stride)
    pieces, refs = refs[: len(places)], refs[len(places) :]
    outs, prefix, last, refs = refs[:4], refs[4], refs[5], refs[6:]
    grad_branch, grad_branch_pre, own_part, later_by, grad_states = refs[:5]
    branch_pre, natural, decay, grad_mixer, weights = refs[5:10]
    in_sems, piece_sems, out_sems, branch_sems = refs[10:]
    width, spans = sizes.width, sizes.spans
    z, core = place[0], place[1]
    stride = sizes.stride
    copies = []
    for number, (piece, (by, side, first, count)) in enumerate(zip(pieces, places)):
        span = (1 - core if side else core) * (spans // 2) + lax.rem(z + by, spans // 2)
        at = pl.ds(pl.multiple_of(span * stride + first, sizes.seg), count)
        copy = pltpu.make_async_copy(piece, grad_branch.at[at], piece_sems.at[number])
        copies.append((side, copy))
    taken = [
        pltpu.make_async_copy(source, target, in_sems.at[number])
        for number, (source, target) in enumerate(
            (
                (weights_hbm.at[:, out_at * width : (out_at + 1) * width], weights),
                (pre_hbm, branch_pre),
                (natural_hbm, natural),
                (decay_hbm, decay),
            )
        )
    ]
    taken[0].start()
    for _, copy in copies:
        copy.start()
    for copy in taken[1:]:
        copy.start()
    taken[0].wait()
    half = sizes.tokens // 2
    branch_out = []
    for side in range(2):
        for piece_side, copy in copies:
            if piece_side == side:
                copy.wait()
        at = pl.ds(pl.multiple_of((1 - core if side else core) * half, half), half)
        out = pltpu.make_async_copy(grad_branch.at[at], outs[0].at[at], branch_sems.at[side])
        out.start()
        branch_out.append(out)
        grad_mixer[at, :] = dot(grad_branch[at, :], weights[...])
    taken[1].wait()
    taken[2].wait()
    sent = Parts((grad_branch_pre, own_part, later_by), outs[1:], out_sems)
    step_rows = 32
    steps = sizes.tokens // parts // step_rows

    def part_step(part, carried):
        def gelu_step(step, carried):
            start = pl.multiple_of((part * steps + step) * step_rows, step_rows)
            at = pl.ds(start, step_rows)
            grad = grad_mixer[at, :]
            act, slope = gelu_parts(branch_pre[at, :])
            grad_branch_pre[at, :] = (grad * natural[at, :] * slope).astype(bf16)
            grad_mixer[at, :] = grad * act
            return carried

        lax.fori_loop(0, steps, gelu_step, 0, unroll=2)
        sent.start(part, (0,))
        return carried

    lax.fori_loop(0, parts, part_step, 0)
    weave(sizes, grad_mixer, grad_states)
    taken[3].wait()
    per_part = sizes.seg // parts

    def scan_part(index, carried):
        part = parts - 1 - index

        def scan_step(step, carried):
            at = sizes.pair(part * per_part + per_part - 1 - step)
            decay_now = decay[at, :]
            own = carried[1] + grad_states[at, :]
            own_part[at, :] = own
            later_by[at, :] = carried[0]
            return (carried[0] * decay_now, own * decay_now)

        carried = lax.fori_loop(0, per_part, scan_step, carried, unroll=4)
        sent.start(part, (1, 2))
        return carried

    shape = (sizes.rows * spans, width)
    first = (jnp.ones(shape, f32), jnp.zeros(shape, f32))
    found = lax.fori_loop(0, parts, scan_part, first)
    keep_ends(sizes, found, prefix, last, True)
    for part in range(parts):
        sent.wait(part)
    for out in branch_out:
        out.wait()


def gates_back_kernel(sizes, peers, index, gathered, prefix, tail, masks, table, params, *refs):
    sources, branch_hbm, refs = refs[:7], refs[7], refs[8:]
    outs, ends, head, sums, refs = refs[:2], refs[2], refs[3], refs[4], refs[5:]
    held, refs = refs[:7], refs[7:]
    grad_gates, grad_front, grad_conv, grad_conv_in, natural = refs[:5]
    in_sems, branch_sem, out_sems = refs[5:]
    own_part, later_by, direct_by, entry_by, recur_by, slope_by, woven_low = held
    seg, taps, width, spans = sizes.seg, sizes.conv_width, sizes.width, sizes.spans
    rows = sizes.rows
    taken = Parts(sources, held, in_sems)
    branch_copy = pltpu.make_async_copy(
        branch_hbm, grad_front.at[:, width : 2 * width], branch_sem
    )
    for part in range(2):
        taken.start(part, range(6))
    entering = from_others(sizes, index, gathered, peers, True)
    spans_in = entering_spans(sizes, prefix, entering)
    shape = (rows * spans, width)

    def gate_step(position, carried):
        at = sizes.pair(position)
        rate_sum, recur_sum, entry_sum = carried
        direct, entry, recur, slope = (
            ref[at, :].astype(f32) for ref in (direct_by, entry_by, recur_by, slope_by)
        )
        carried_now = own_part[at, :] + later_by[at, :] * spans_in
        rated = carried_now * recur
        recur_low = (rated * slope).astype(bf16)
        entry_low = (carried_now * entry).astype(bf16)
        grad_gates[at, :width] = recur_low
        grad_gates[at, width:] = entry_low
        grad_conv[at, :] = carried_now * direct
        return (
            rate_sum + rated,
            recur_sum + recur_low.astype(f32),
            entry_sum + entry_low.astype(f32),
        )

    empty = jnp.zeros(shape, f32)
    gate_sums = (empty,) * 3
    per_part = seg // parts
    part_rows = per_part * rows * spans
    sent = Parts((grad_gates, grad_front), outs, out_sems)
    for part in range(parts):
        taken.wait(part, range(6))
        if part + 2 < parts:
            taken.start(part + 2, range(6))
        elif part + 2 == parts:
            for later in range(parts):
                taken.start(later, (6,))
        else:
            branch_copy.start()
        gate_sums = lax.fori_loop(
            part * per_part, (part + 1) * per_part, gate_step, gate_sums, unroll=4
        )
        sent.start(part, (0,))
        at = pl.ds(part * part_rows, part_rows)
        grad_conv[at, :] = grad_conv[at, :] + dot(grad_gates[at, :], table[...], 1, 0)

    def weighted(position):
        at = sizes.pair(position)
        grad = grad_conv[at, :]
        valid = masks[at, :]
        return [grad] + [grad * valid[:, tap : tap + 1] for tap in range(1, taps)]

    tap_rows = [params[tap : tap + 1, :] for tap in range(taps)]
    ahead = [weighted(position) for position in range(taps - 1)]
    nothing_after = [jnp.zeros((1, width), f32)] * rows
    held_ahead = [
        per_row(sizes, span_after, ahead[place][tap], nothing_after)
        for tap in range(1, taps)
        for place in range(tap)
    ]

    def conv_step(index, carried):
        held_now, now_sums = carried
        at = sizes.pair(seg - 1 - index)
        tile = woven_low[at, :].astype(f32)
        now = weighted(seg - 1 - index)
        value = tap_rows[0] * now[0]
        new_held, new_sums, first = [], [now_sums[0] + tile * now[0]], 0
        for tap in range(1, taps):
            far = held_now[first + tap - 1]
            value = value + tap_rows[tap] * far
            new_sums.append(now_sums[tap] + tile * far)
            new_held += [now[tap]] + list(held_now[first : first + tap - 1])
            first += tap
        new_sums.append(now_sums[taps] + now[0])
        grad_conv_in[at, :] = value
        return tuple(new_held), tuple(new_sums)

    for part in range(parts):
        taken.wait(part, (6,))
    held_ahead, tap_sums = lax.fori_loop(
        0, seg, conv_step, (tuple(held_ahead), (empty,) * (taps + 1)), unroll=8
    )
    tap_sums = list(tap_sums)
    head[...] = jnp.zeros(head.shape, f32)
    for row in range(rows):
        for back in range(1, taps):
            value = jnp.zeros((1, width), f32)
            tail_row = tail[row * 8 + 8 - back : row * 8 + 9 - back, :]
            first = 0
            for tap in range(1, taps):
                if tap >= back:
                    first_row = held_ahead[first + tap - back][row * spans : row * spans + 1]
                    value = value + tap_rows[tap] * first_row
                    tap_sums[tap] = tap_sums[tap] + jnp.concatenate(
                        [tail_row * first_row, jnp.zeros((rows * spans - 1, width), f32)], axis=0
                    )
                first += tap
            head[row * 8 + 8 - back : row * 8 + 9 - back, :] = value
    weave(sizes, grad_conv_in, natural, True)
    branch_copy.wait()
    step_rows = 32
    steps = sizes.tokens // parts // step_rows

    def part_step(part, carried):
        def front_step(step, carried):
            start = pl.multiple_of((part * steps + step) * step_rows, step_rows)
            at = pl.ds(start, step_rows)
            grad_front[at, :width] = natural[at, :].astype(bf16)
            return carried

        lax.fori_loop(0, steps, front_step, 0, unroll=4)
        sent.start(part, (1,))
        return carried

    lax.fori_loop(0, parts, part_step, 0)
    for row in range(rows):
        end = (spans - 1) * sizes.stride + (row + 1) * seg
        ends[row * 8 : row * 8 + 8, :] = natural[end - 8 : end, :]
    for place, part_sum in enumerate(tap_sums + [gate_sums[1], gate_sums[2], gate_sums[0]]):
        sums[place : place + 1, :] = jnp.sum(part_sum, axis=0, keepdims=True)
    for part in range(parts):
        sent.wait(part)


def rows_kernel(body, inputs, *refs):
    ins, outs = refs[:inputs], refs[inputs:]
    rows, step_rows = ins[0].shape[0], 32
    for start in range(0, rows, step_rows):
        body(start, slice(start, start + step_rows), ins, outs)


def rows_call(body, ins, outs):
    vmem = pl.BlockSpec(memory_space=pltpu.VMEM)
    return pl.pallas_call(
        partial(rows_kernel, body, len(ins)),
        out_shape=[jax.ShapeDtypeStruct(shape, kind) for shape, kind in outs],
        in_specs=[vmem] * len(ins),
        out_specs=[vmem] * len(outs),
        cost_estimate=no_cost,
        compiler_params=pltpu.CompilerParams(vmem_limit_bytes=20 * 1024 * 1024),
    )(*ins)


def near_body(start, at, ins, outs):
    half = ins[2].shape[0]
    ahead, behind = ins[0][at, :], ins[1][at, :]
    if start < half:
        ahead = ahead + ins[2][at, :].astype(f32)
    else:
        behind = behind + ins[3][start - half : start - half + behind.shape[0], :].astype(f32)
    outs[0][at, :] = ahead.astype(bf16)
    outs[1][at, :] = behind.astype(bf16)


def own_sum(at, ins):
    return ins[0][at, :] + ins[1][at, :].astype(f32) + ins[2][at, :].astype(f32)


def branch_body(start, at, ins, outs):
    residual = own_sum(at, ins) + ins[3][at, :].astype(f32)
    outs[0][at, :] = residual
    outs[1][at, :] = (rms_unit(residual)[0] * ins[4][...]).astype(bf16)


def feed_back_body(start, at, ins, outs):
    grad = own_sum(at, ins)
    unit, inverse = rms_unit(ins[3][at, :])
    found = ins[4][at, :].astype(f32) + norm_back(grad, unit, inverse, ins[5][...])
    outs[0][at, :] = found
    outs[1][at, :] = found.astype(bf16)
    part = jnp.sum((grad * unit).reshape(-1, 8, grad.shape[1]), axis=0)
    outs[2][...] = part if start == 0 else outs[2][...] + part


def feed_body(start, at, ins, outs):
    outs[0][at, :] = (own_sum(at, ins) + ins[3][at, :]).astype(bf16)


def tokens_body(start, at, ins, outs):
    grad = own_sum(at, ins)
    unit, inverse = rms_unit(ins[3][at, :].astype(f32))
    outs[0][at, :] = ins[4][at, :] + norm_back(grad, unit, inverse, ins[5][...])


def call(kernel, outs, scratch, *operands, scalars=0, anywhere=(), out_anywhere=0, sems=(), takes=0):
    vmem = pl.BlockSpec(memory_space=pltpu.VMEM)
    hbm = pl.BlockSpec(memory_space=pl.ANY)
    in_specs = [pl.BlockSpec(memory_space=pltpu.SMEM)] * scalars
    in_specs += [vmem] * (len(operands) - scalars)
    for index in anywhere:
        in_specs[index] = hbm
    return pl.pallas_call(
        kernel,
        out_shape=[jax.ShapeDtypeStruct(shape, kind) for shape, kind in outs],
        in_specs=in_specs,
        out_specs=[hbm] * out_anywhere + [vmem] * (len(outs) - out_anywhere),
        scratch_shapes=[pltpu.VMEM(shape, kind) for shape, kind in scratch]
        + [pltpu.SemaphoreType.DMA(shape) for shape in sems],
        cost_estimate=cost(takes),
        compiler_params=pltpu.CompilerParams(vmem_limit_bytes=60 * 1024 * 1024),
    )(*operands)


def product_kernel(at, bys, place, x_hbm, got_hbm, own_hbm, other_hbm, *refs):
    count = (len(refs) - 5) // 2
    targets, outs = refs[:count], refs[count : 2 * count]
    x, weights, x_sem, weight_sem, out_sem = refs[2 * count :]
    depth = got_hbm.shape[1]
    span = x.shape[0] // len(bys)
    rows = got_hbm.shape[0]
    columns = 512
    steps = weights.shape[0] // columns
    halves = (slice(0, depth), slice(depth, 2 * depth))

    def weight_copies(index):
        place = slice(index * columns, (index + 1) * columns)
        return [
            pltpu.make_async_copy(
                source.at[place, at * depth : (at + 1) * depth],
                weights.at[place, half],
                weight_sem.at[2 * index + side],
            )
            for side, (source, half) in enumerate(zip((own_hbm, other_hbm), halves))
        ]

    x_copies = []
    for number, by in enumerate(bys):
        first = lax.rem(place[0] + by, rows // span) * span
        to = slice(number * span, (number + 1) * span)
        mine = pl.ds(pl.multiple_of(place[1] * rows + first, span), span)
        theirs = pl.ds(pl.multiple_of(first, span), span)
        x_copies += [
            pltpu.make_async_copy(x_hbm.at[mine], x.at[to, halves[0]], x_sem.at[2 * number]),
            pltpu.make_async_copy(
                got_hbm.at[theirs], x.at[to, halves[1]], x_sem.at[2 * number + 1]
            ),
        ]
    sent = []
    for side in range(2):
        for copy in x_copies[side::2]:
            copy.start()
        weight_copies(0)[side].start()
    for copy in weight_copies(1):
        copy.start()
    for index in range(steps):
        place_now = slice(index * columns, (index + 1) * columns)
        if index == 0:
            value = 0.0
            for side, half in enumerate(halves):
                for copy in x_copies[side::2]:
                    copy.wait()
                weight_copies(0)[side].wait()
                value = value + dot(x[:, half], weights[place_now, half], 1, 1)
        else:
            for copy in weight_copies(index):
                copy.wait()
        if index + 2 < steps:
            for copy in weight_copies(index + 2):
                copy.start()
        if index > 0:
            value = dot(x[...], weights[place_now, :], 1, 1)
        first = 0
        for number, (out, target) in enumerate(zip(outs, targets)):
            out[:, place_now] = value[first : first + out.shape[0]].astype(out.dtype)
            first += out.shape[0]
            copy = pltpu.make_async_copy(
                out.at[:, place_now], target.at[:, place_now], out_sem.at[number, index]
            )
            copy.start()
            sent.append(copy)
    for copy in sent:
        copy.wait()


def product_pieces(bys, x, got, weights, others, at, outs, takes, room=60):
    depth, model = got.shape[1], weights.shape[0]
    span = got.shape[0] // lax.axis_size("z")
    place = jnp.stack([lax.axis_index("z"), lax.axis_index("core")]).astype(jnp.int32)
    anywhere = pl.BlockSpec(memory_space=pl.ANY)
    return pl.pallas_call(
        partial(product_kernel, at, bys),
        out_shape=[jax.ShapeDtypeStruct(shape, kind) for shape, kind in outs],
        in_specs=[pl.BlockSpec(memory_space=pltpu.SMEM)] + [anywhere] * 4,
        out_specs=[anywhere] * len(outs),
        scratch_shapes=[pltpu.VMEM(shape, kind) for shape, kind in outs]
        + [
            pltpu.VMEM((len(bys) * span, 2 * depth), bf16),
            pltpu.VMEM((model, 2 * depth), bf16),
            pltpu.SemaphoreType.DMA((2 * len(bys),)),
            pltpu.SemaphoreType.DMA((2 * model // 512,)),
            pltpu.SemaphoreType.DMA((len(outs), model // 512)),
        ],
        cost_estimate=cost(takes),
        compiler_params=pltpu.CompilerParams(vmem_limit_bytes=room * 1024 * 1024),
    )(place, x, got, weights, others)


def swap_rows(x):
    rows = x.shape[0] // 2
    theirs = (1 - lax.axis_index("core")) * rows
    return swap_cores(lax.dynamic_slice_in_dim(x, theirs, rows, 0))


def feed_kernel(aliased, sends, core, x_hbm, grad_hbm, weights_hbm, *refs):
    refs = refs[aliased:]
    hidden_hbm, both_hbm, refs = refs[0], refs[1], refs[2:]
    if sends:
        send_hbm, refs = refs[0], refs[1:]
    x, grad, weights, pre, hidden, both, in_sem, weight_sem, out_sem = refs
    rows = x.shape[0]
    inner = grad.shape[1]
    mine = pl.ds(pl.multiple_of(core[0] * rows, rows), rows)
    copies = [
        pltpu.make_async_copy(x_hbm.at[mine], x, in_sem.at[0]),
        pltpu.make_async_copy(grad_hbm.at[mine], grad, in_sem.at[1]),
    ]
    columns = weights.shape[2]
    count = 2 * inner // columns

    def weight_copy(index):
        at = slice(index * columns, (index + 1) * columns)
        return pltpu.make_async_copy(
            weights_hbm.at[:, at], weights.at[index], weight_sem.at[index]
        )

    copies[0].start()
    for index in range(count):
        weight_copy(index).start()
    copies[1].start()
    copies[0].wait()
    for index in range(count):
        weight_copy(index).wait()
        pre[:, index * columns : (index + 1) * columns] = dot(x[...], weights[index])
    copies[1].wait()
    step_rows = 32
    outs = []

    def out_copies(part):
        size = rows // parts
        here = pl.ds(pl.multiple_of(part * size, size), size)
        there = pl.ds(pl.multiple_of(core[0] * rows + part * size, size), size)
        found = [
            pltpu.make_async_copy(hidden.at[here], hidden_hbm.at[there], out_sem.at[part, 0]),
            pltpu.make_async_copy(both.at[here], both_hbm.at[there], out_sem.at[part, 1]),
        ]
        if sends:
            found.append(
                pltpu.make_async_copy(both.at[here], send_hbm.at[here], out_sem.at[part, 2])
            )
        return found

    steps = rows // parts // step_rows

    def part_step(part, carried):
        def act_step(step, carried):
            start = pl.multiple_of((part * steps + step) * step_rows, step_rows)
            at = pl.ds(start, step_rows)
            act, slope = gelu_parts(pre[at, :inner])
            up = pre[at, inner:]
            grad_now = grad[at, :]
            hidden[at, :] = (act * up).astype(bf16)
            both[at, :inner] = (grad_now * up * slope).astype(bf16)
            both[at, inner:] = (grad_now * act).astype(bf16)
            return carried

        lax.fori_loop(0, steps, act_step, 0)
        for copy in out_copies(part):
            copy.start()
        return carried

    lax.fori_loop(0, parts, part_step, 0)
    for part in range(parts):
        for copy in out_copies(part):
            copy.wait()


def feed_forward(core, flat, grad_hidden, weights, sends, given):
    tokens, model = flat.shape
    inner = grad_hidden.shape[1]
    rows = tokens // 2
    columns = 512
    anywhere = pl.BlockSpec(memory_space=pl.ANY)
    outs = [(tokens, inner), (tokens, 2 * inner)] + [(rows, 2 * inner)] * sends
    return pl.pallas_call(
        partial(feed_kernel, len(given), sends),
        out_shape=[jax.ShapeDtypeStruct(shape, bf16) for shape in outs],
        in_specs=[pl.BlockSpec(memory_space=pltpu.SMEM)] + [anywhere] * (3 + len(given)),
        out_specs=[anywhere] * len(outs),
        scratch_shapes=[
            pltpu.VMEM((rows, model), bf16),
            pltpu.VMEM((rows, inner), f32),
            pltpu.VMEM((2 * inner // columns, model, columns), bf16),
            pltpu.VMEM((rows, 2 * inner), f32),
            pltpu.VMEM((rows, inner), bf16),
            pltpu.VMEM((rows, 2 * inner), bf16),
            pltpu.SemaphoreType.DMA((2,)),
            pltpu.SemaphoreType.DMA((2 * inner // columns,)),
            pltpu.SemaphoreType.DMA((parts, 3)),
        ],
        input_output_aliases={4: 0, 5: 1} if given else {},
        cost_estimate=cost(8),
        compiler_params=pltpu.CompilerParams(vmem_limit_bytes=60 * 1024 * 1024),
    )(
        jnp.reshape(core, (1,)).astype(jnp.int32),
        flat,
        grad_hidden,
        weights,
        *given,
    )


def weight_kernel(with_sums, filled, left, right, *refs):
    value = dot(left[...], right[...], 0, 0)
    if with_sums:
        weight, (out, sums) = refs[0], refs[1 + filled :]
        product = value * weight[...].astype(f32)
        sums[...] = sum(
            product[:, start : start + lanes] for start in range(0, product.shape[1], lanes)
        )
    else:
        out = refs[filled]
    out[...] = value.astype(bf16).reshape(out.shape)


def weight_grad(left, right, width, total, place=0, given=None, weight=None, weight_at=0, blocks=0, room=60, peers=0, more=0):
    depth, rows = left.shape
    block = 512 if width > 1024 else 1024
    blocks = blocks or right.shape[1] // width
    in_specs = [
        pl.BlockSpec((depth, block), lambda j, i: (0, i)),
        pl.BlockSpec((depth, width), lambda j, i: (0, j)),
    ]
    operands = [left, right]
    out_shape = [jax.ShapeDtypeStruct((rows, total), bf16)]
    out_specs = [pl.BlockSpec((block, width), lambda j, i: (i, j + place))]
    if peers:
        share = rows // peers
        out_shape = [jax.ShapeDtypeStruct((peers, share + more, total), bf16)]
        out_specs = [pl.BlockSpec((block // share, share, width), lambda j, i: (i, 0, j + place))]
    if weight is not None:
        in_specs.append(pl.BlockSpec((block, width), lambda j, i: (i, weight_at)))
        operands.append(weight)
        out_shape.append(jax.ShapeDtypeStruct((rows, lanes), f32))
        out_specs.append(pl.BlockSpec((block, lanes), lambda j, i: (i, 0)))
    aliases = {}
    if given is not None:
        aliases = {len(operands): 0}
        in_specs.append(pl.BlockSpec(memory_space=pl.ANY))
        operands.append(given)
    found = pl.pallas_call(
        partial(weight_kernel, weight is not None, given is not None),
        grid=(blocks, rows // block),
        out_shape=out_shape,
        in_specs=in_specs,
        out_specs=out_specs,
        input_output_aliases=aliases,
        cost_estimate=pl.CostEstimate(
            flops=2 * depth * rows * blocks * width,
            bytes_accessed=2 * (depth * rows + depth * blocks * width + rows * blocks * width),
            transcendentals=0,
        ),
        compiler_params=pltpu.CompilerParams(vmem_limit_bytes=room * 1024 * 1024),
    )(*operands)
    return found if weight is not None else found[0]


def shards(
    tokens,
    cotangent,
    mixer_gain,
    feedforward_gain,
    branch_weight,
    input_weight,
    output_weight,
    recurrence_gate,
    input_gate,
    conv_kernel,
    conv_bias,
    recurrence_bias,
    input_bias,
    decay_param,
    gate_weight,
    up_weight,
    down_weight,
    doc_starts,
):
    spans = lax.axis_size("z") * 2
    core = lax.axis_index("core")
    dp_index = lax.axis_index(dp)
    peers = lax.axis_size(dp)
    rows, seg, model = tokens.shape
    units = branch_weight.shape[1]
    width = up_to(units, lanes)
    hidden_width = gate_weight.shape[1]
    taps = conv_kernel.shape[0]
    block = recurrence_gate.shape[0]
    blocks = units // block
    share = units // peers
    sizes = Sizes(rows, seg, spans, width, taps)
    own, length, block_tokens = rows * seg, seg * spans, sizes.tokens
    depth = model // peers

    mine = jnp.reshape(dp_index, (1,)).astype(jnp.int32)

    unit_one = rms_unit(tokens.reshape(own, model).astype(f32))[0]
    gain_one = mixer_gain.astype(f32)
    gain_two = feedforward_gain.astype(f32)
    normed_one = (unit_one * gain_one).astype(bf16)
    one_near = ring_near(normed_one)
    one_far = ring_far(one_near)

    small = jnp.concatenate(
        tie_all(
            [
                recurrence_gate,
                input_gate,
                conv_kernel,
                conv_bias[None],
                recurrence_bias[None],
                input_bias[None],
                decay_param[None],
            ],
            normed_one,
        ),
        axis=0,
    ).T
    small_width = up_to(small.shape[1], lanes)
    small_rows = up_to(share, 8)
    small_all = gather_small(widen(widen(small, small_width, 1), small_rows, 0), dp)
    small_all = small_all[:, :share].reshape(units, small_width)
    front_weights = lax.all_gather(
        jnp.concatenate(
            [
                widen(input_weight, width, 1),
                widen(branch_weight, width, 1),
                widen(output_weight.T, width, 1),
            ],
            axis=1,
        ),
        dp,
        axis=0,
        tiled=True,
    )
    flat_one = ring_whole(one_far)
    cot_near = ring_near(tie(cotangent.reshape(own, model), one_far))
    def back_parts(weights):
        return jnp.concatenate([weights[0], weights[1], weights[2].T], axis=1)

    back_weights = lax.all_gather(
        back_parts(tie_all((gate_weight, up_weight, down_weight), one_near)),
        dp,
        axis=0,
        tiled=True,
    )
    input_matrix = front_weights[:, :width]
    branch_matrix = front_weights[:, width : 2 * width]
    down_turned = back_weights[:, 2 * hidden_width :]
    def diagonal(turned):
        lines = [
            jnp.pad(
                turned[h * block : (h + 1) * block],
                ((0, 0), (h * block, width - (h + 1) * block)),
            )
            for h in range(blocks)
        ]
        return widen(jnp.concatenate(lines, axis=0), width, 0)

    table = jnp.concatenate(
        [diagonal(small_all[:, :block]), diagonal(small_all[:, block : 2 * block])], axis=0
    )
    vectors = widen(small_all[:, 2 * block : 2 * block + taps + 4].astype(f32).T, width, 1)
    decay_values = vectors[taps + 3]
    params = widen(
        jnp.concatenate([vectors[: taps + 3], jax.nn.softplus(-decay_values)[None]], axis=0),
        up_to(taps + 4, 8),
        0,
    )

    positions = dp_index * length - (taps - 1) + jnp.arange(length + taps - 1, dtype=jnp.int32)
    starts = jnp.any(doc_starts[:, :, None] == positions[None, None, :], axis=1).astype(f32)
    columns = [starts[:, taps - 1 :]]
    valid = jnp.ones((rows, length), f32)
    for tap in range(1, taps):
        valid = valid * (1.0 - starts[:, taps - tap : taps - tap + length])
        columns.append(valid)
    masks = jnp.stack(columns + [valid] * (8 - taps), axis=-1)
    masks = masks.reshape(rows, spans, seg, 8).transpose(2, 0, 1, 3).reshape(block_tokens, 8)

    conv_in = dot(flat_one, input_matrix)
    conv_ends = conv_in.reshape(spans, rows, seg, width)[spans - 1, :, seg - 8 :, :]
    tail = lax.ppermute(
        conv_ends.reshape(rows * 8, width), dp, [(i, i + 1) for i in range(peers - 1)]
    )
    conv_in, cot_near = lax.optimization_barrier((conv_in, cot_near))
    flat = (block_tokens, width)
    prefix_kind, edge_kind = ((2 * rows * spans, width), f32), ((peers, 8, width), f32)
    kinds = [(flat, f32)] * 3 + [(flat, bf16)] * 7
    *gate_parts, prefix, last = call(
        partial(gates_kernel, sizes),
        kinds + [prefix_kind, edge_kind],
        kinds + [((block_tokens // parts, width), f32), (flat, f32)]
        + [((block_tokens // parts, 2 * width), f32)],
        conv_in,
        tail,
        masks,
        table,
        params,
        out_anywhere=10,
        sems=[(10, parts)],
    )
    product, total, decay, conv_low, woven_low, direct_by, entry_by, state_by, rest_by, slope_by = gate_parts
    front_other = swap_cores(tie(front_weights, last))
    kept = {}

    def branch_work(operand):
        kept["branch"] = dot(operand, branch_matrix)
        return kept["branch"]

    cot_far = ring_far(cot_near, (tie(flat_one, last), branch_work))
    branch_pre, _ = lax.optimization_barrier((kept["branch"], cot_far[3:5]))
    gathered = send_copies(last, dp)
    mixer_in, states_natural, entered = call(
        partial(states_kernel, sizes, peers),
        [(flat, bf16), (flat, f32), ((8, width), f32)],
        [(flat, f32)] * 3 + [(flat, bf16), (flat, f32), (flat, f32)],
        mine,
        gathered,
        prefix,
        product,
        total,
        branch_pre,
        scalars=1,
        anywhere=range(3, 6),
        out_anywhere=2,
        sems=[(2, parts), (), (2, parts)],
    )
    own_kind = ((own, model), f32)
    own_low = ((own, model), bf16)
    tokens_own, cotangent_own = (part.reshape(own, model) for part in (tokens, cotangent))
    residual, normed_two = ring_scatter(
        mixer_in,
        swap_rows(mixer_in),
        front_weights,
        front_other,
        2,
        branch_body,
        (tokens_own, gain_two[None]),
        [own_kind, own_low],
    )

    flat_two = lax.all_gather(normed_two, ("core", "z"), axis=0, tiled=True)
    back_other = swap_cores(tie(back_weights, normed_two))
    cotangent_flat = ring_whole(tie_all(cot_far, normed_two))
    grad_hidden = dot(cotangent_flat, down_turned)
    (recur_by,) = call(
        partial(recur_kernel, sizes),
        [(flat, bf16)],
        [(flat, f32), (flat, bf16), (flat, bf16), (flat, bf16), (flat, f32)],
        tie(entered, normed_two),
        states_natural,
        state_by,
        rest_by,
        anywhere=range(1, 4),
        out_anywhere=1,
        sems=[(3, parts), (1, parts)],
    )
    flat_two, back_other, recur_by = lax.optimization_barrier((flat_two, back_other, recur_by))
    hidden, grad_gate_up, gate_up_send = feed_forward(
        1 - core, flat_two, grad_hidden, back_weights, True, ()
    )
    gate_up_got = swap_cores(gate_up_send)
    hidden, grad_gate_up = feed_forward(
        core, flat_two, grad_hidden, back_weights, False, (hidden, grad_gate_up)
    )
    feed_width = 3 * hidden_width

    def gate_up_part(operand):
        kept["feed"] = weight_grad(flat_two, operand, 2 * hidden_width, feed_width)
        return kept["feed"]

    def down_part(operand):
        kept["feed"] = weight_grad(
            cotangent_flat, operand, hidden_width, feed_width, 2, kept["feed"], room=40
        )
        return kept["feed"]

    def feed_scatter(below, above):
        kept["feed"] = lax.psum_scatter(kept["feed"], dp, scatter_dimension=0, tiled=True)
        return below, above

    grad_residual, grad_branch_own, gain_two_rows = ring_scatter(
        grad_gate_up,
        gate_up_got,
        back_weights,
        back_other,
        0,
        feed_back_body,
        (residual, cotangent_own, gain_two[None]),
        [own_kind, own_low, ((8, model), f32)],
        (grad_gate_up, gate_up_part),
        (hidden, down_part),
        feed_scatter,
    )
    feed_grads = kept["feed"]
    gain_two_part = jnp.sum(gain_two_rows, axis=0)
    near = ring_near(grad_branch_own)
    hidden_got = swap_rows(tie(hidden, near[0]))
    feed_operands = (hidden, hidden_got, back_weights, back_other, 2)
    low, high, ahead, behind, feed_own = all_pieces(feed_operands)
    far = ring_far(tie_all(near, low, feed_own))

    places = jnp.stack([lax.axis_index("z"), core]).astype(jnp.int32)

    grad_branch, grad_branch_pre, own_part, later_by, back_prefix, back_last = call(
        partial(reverse_kernel, sizes, 2),
        [((block_tokens, model), bf16), (flat, bf16)]
        + [(flat, f32)] * 2
        + [prefix_kind, edge_kind],
        [((block_tokens, model), bf16), (flat, bf16)]
        + [(flat, f32)] * 7
        + [((model, width), bf16)],
        places,
        branch_pre,
        states_natural,
        decay,
        front_weights,
        *far,
        scalars=1,
        anywhere=range(1, 5 + len(far)),
        out_anywhere=4,
        sems=[(4,), (len(far),), (3, parts), (2,)],
        takes=24,
    )
    back_gathered = send_copies(back_last, dp)

    kept["middle"] = weight_grad(
        tie(grad_branch, back_last), mixer_in, width, 2 * width
    )
    sum_rows = up_to(taps + 4, 8)
    wide = (block_tokens, 2 * width)

    def gates_back(operand):
        gathered, kept["middle"] = operand
        kept["gates"] = call(
            partial(gates_back_kernel, sizes, peers),
            [
                (wide, bf16),
                (wide, bf16),
                ((rows * 8, width), f32),
                ((rows * 8, width), f32),
                ((sum_rows, width), f32),
            ],
            [(flat, f32)] * 2
            + [(flat, bf16)] * 5
            + [(wide, bf16), (wide, bf16)]
            + [(flat, f32)] * 3,
            mine,
            gathered,
            back_prefix,
            tail,
            masks,
            table,
            params,
            own_part,
            later_by,
            direct_by,
            entry_by,
            recur_by,
            slope_by,
            woven_low,
            grad_branch_pre,
            scalars=1,
            anywhere=range(7, 15),
            out_anywhere=2,
            sems=[(7, parts), (), (2, parts)],
            takes=11,
        )
        return kept["gates"][-1]

    from_below, from_above = ring_step(low, high, ((back_gathered, kept["middle"]), gates_back))
    kept["gates"], from_below, from_above = lax.optimization_barrier(
        (kept["gates"], from_below, from_above)
    )
    feed_sums = near_sums(ahead, behind, from_below, from_above)
    grad_gates, grad_front, ends, head, sums = kept["gates"]
    from_next = lax.ppermute(head, dp, [(i + 1, i) for i in range(peers - 1)])
    middle_part, branch_sums = weight_grad(
        flat_one,
        tie(grad_branch_pre, head),
        width,
        2 * width,
        1,
        kept["middle"],
        front_weights,
        1,
    )
    from_next, middle_part = lax.optimization_barrier((from_next, middle_part))
    middle_half = lax.psum_scatter(
        tie(middle_part, feed_grads), dp[0], scatter_dimension=0, tiled=True
    )
    grad_front = lax.dynamic_update_slice(
        grad_front.reshape(spans, rows, seg, 2 * width),
        (ends + from_next).astype(bf16).reshape(1, rows, 8, width),
        (spans - 1, 0, seg - 8, 0),
    ).reshape(block_tokens, 2 * width)
    normed_got = swap_rows(grad_front)
    payload, input_sums = weight_grad(
        flat_one,
        grad_front,
        width,
        width,
        0,
        None,
        front_weights,
        0,
        1,
        peers=peers,
        more=small_rows,
    )
    payload, normed_got = lax.optimization_barrier((payload, normed_got))
    gain_one_part = jnp.sum(branch_sums + input_sums, axis=1) / gain_one
    gain_parts = jnp.stack([gain_one_part, gain_two_part]).reshape(2, spans // 2, 2, -1)
    gain_parts = gain_parts.transpose(2, 1, 0, 3)
    gain_keep = lax.dynamic_index_in_dim(gain_parts, core, 0, keepdims=False)
    gain_send = lax.dynamic_index_in_dim(gain_parts, 1 - core, 0, keepdims=False)
    gain_got = swap_cores(gain_send)

    def normed_work(operand):
        kept["normed"] = all_pieces(operand + (front_weights, front_other, 0))
        return kept["normed"]

    below, above = ring_step(*feed_sums, ((grad_front, normed_got), normed_work))
    kept["normed"], below, above = lax.optimization_barrier((kept["normed"], below, above))
    low, high, ahead, behind, normed_own = kept["normed"]
    low, high, gain_got = lax.optimization_barrier((low, high, gain_got))

    def fill_payload(operand):
        payload_now, gain_sum, gates_now = operand
        table_grads = dot(gates_now, conv_low, 0, 0)

        def diagonal_back(turned):
            block_of = (jnp.arange(units) // block)[:, None]
            kept = turned[:units, :block]
            for h in range(1, blocks):
                kept = jnp.where(block_of == h, turned[:units, h * block : (h + 1) * block], kept)
            return kept

        small_grads = jnp.concatenate(
            [
                diagonal_back(table_grads[:width]),
                diagonal_back(table_grads[width:]),
                sums[:, :units].T,
            ],
            axis=1,
        )
        small_grads, middle_now = lax.optimization_barrier((small_grads, middle_half))
        kept["middle"] = lax.psum_scatter(middle_now, dp[1], scatter_dimension=0, tiled=True)
        gain_parts = scatter_direct(gain_sum, "z")
        gain_share = model // spans // peers
        gain_parts = gain_parts.reshape(2, peers, gain_share).transpose(1, 0, 2)

        small_now = widen(small_grads, small_width, 1).reshape(peers, share, small_width)
        small_now = jnp.concatenate([small_now, widen(gain_parts, small_width, 2)], axis=1)
        payload = lax.dynamic_update_slice(payload_now, small_now.astype(bf16), (0, depth, 0))
        kept["payload"] = payload
        return payload

    from_below, from_above = ring_step(low, high, ((payload, gain_keep + gain_got, grad_gates), fill_payload))
    from_below, from_above, payload = lax.optimization_barrier(
        (from_below, from_above, kept["payload"])
    )
    middle_grad = kept["middle"]

    kept["sent"] = lax.all_to_all(payload, dp, 0, 0)
    normed_below, normed_above = ring_step(*near_sums(ahead, behind, from_below, from_above), None)
    (tokens_grad,) = rows_call(
        tokens_body,
        (normed_own, normed_below, normed_above, tokens_own, grad_residual, gain_one[None]),
        [own_kind],
    )
    below, above = tie_all((below, above), tokens_grad)
    (layer_output,) = rows_call(feed_body, (feed_own, below, above, residual), [own_low])
    feed_grads = tie(feed_grads, normed_own).astype(f32)
    middle_grad = middle_grad.astype(f32)
    summed = jnp.sum(tie(kept["sent"], tokens_grad).astype(f32), axis=0)
    input_grad, small_grads = summed[:depth], summed[depth:]
    gain_share = model // spans // peers
    gain_grads = small_grads[share : share + 2, :gain_share]
    small_grads = small_grads[:share].T
    rate_slope = jax.nn.sigmoid(-decay_param.astype(f32)) * decay_power
    at = 2 * block
    return (
        layer_output.reshape(rows, seg, model),
        tokens_grad.reshape(rows, seg, model),
        gain_grads[0],
        gain_grads[1],
        middle_grad[:, width : width + units],
        input_grad[:, :units],
        middle_grad[:, :units].T,
        small_grads[:block],
        small_grads[block:at],
        small_grads[at : at + taps],
        small_grads[at + taps],
        small_grads[at + taps + 1],
        small_grads[at + taps + 2],
        small_grads[at + taps + 3] * rate_slope,
        feed_grads[:, :hidden_width],
        feed_grads[:, hidden_width : 2 * hidden_width],
        feed_grads[:, 2 * hidden_width :].T,
    )


def solution(mesh):
    peers, group = mesh.devices.shape
    side = 4
    split = Mesh(
        mesh.devices.reshape(side, peers // side, group // 2, 2), dp + ("z", "core")
    )
    tokens_spec = P(None, dp + ("z", "core"), None)
    split_units = P(None, ("z", "core") + dp)
    split_vector = P(("z", "core") + dp)
    rows_first, units_first = P(dp, ("z", "core")), P(("z", "core"), dp)
    return jax.shard_map(
        shards,
        mesh=split,
        in_specs=(tokens_spec, tokens_spec, P(), P(), rows_first, rows_first, units_first)
        + (split_units,) * 3
        + (split_vector,) * 4
        + (rows_first, rows_first, units_first, P()),
        out_specs=(tokens_spec, tokens_spec, split_vector, split_vector)
        + (rows_first, rows_first, units_first)
        + (split_units,) * 3
        + (split_vector,) * 4
        + (rows_first, rows_first, units_first),
        check_vma=False,
    )
```

```python
from functools import partial

import jax
import jax.numpy as jnp
from jax import lax
from jax.experimental import pallas as pl
from jax.experimental.pallas import tpu as pltpu
from jax.sharding import Mesh
from jax.sharding import PartitionSpec as P

eps_norm = 1e-06
decay_power = 8.0
mult_eps = 0.001
gelu_scale = 0.7978845608028654
gelu_cubic = 0.044715
lanes = 128
f32 = jnp.float32
bf16 = jnp.bfloat16


def cost(microseconds):
    return pl.CostEstimate(
        flops=microseconds * 1_100_000_000, bytes_accessed=0, transcendentals=0
    )


no_cost = cost(0)


def up_to(count, step):
    return -(-count // step) * step


def widen(values, width, axis):
    pads = [(0, 0)] * values.ndim
    pads[axis] = (0, width - values.shape[axis])
    return jnp.pad(values, pads)


def rms_unit(values):
    inverse = lax.rsqrt(jnp.mean(values * values, axis=-1, keepdims=True) + eps_norm)
    return (values * inverse, inverse)


def norm_back(grad_normed, unit_values, inverse, gain):
    scaled = grad_normed * gain
    return inverse * (scaled - unit_values * jnp.mean(scaled * unit_values, axis=-1, keepdims=True))


def gelu_parts(values):
    squared = values * values
    tanh_value = jnp.tanh(gelu_scale * values * (1.0 + gelu_cubic * squared))
    half = 0.5 * (1.0 + tanh_value)
    slope = half + 0.5 * values * (1.0 - tanh_value * tanh_value) * gelu_scale * (
        1.0 + 3.0 * gelu_cubic * squared
    )
    return (values * half, slope)


def dot(left, right, left_axis=1, right_axis=0):
    return lax.dot_general(
        left, right, (((left_axis,), (right_axis,)), ((), ())), preferred_element_type=f32
    )


def send_copies(copies, axis):
    return lax.all_to_all(copies, axis, 0, 0)


def gather_small(value, axis):
    peers = lax.axis_size(axis)
    return lax.all_to_all(jnp.broadcast_to(value[None], (peers,) + value.shape), axis, 0, 0)


def scatter_sum(value, axis):
    return jnp.sum(lax.all_to_all(value, axis, 0, 0).astype(f32), axis=0)


def tie(value, *before):
    return lax.optimization_barrier((value,) + before)[0]


def tie_all(values, *before):
    return lax.optimization_barrier((values,) + before)[0]


def swap_cores(value):
    return lax.ppermute(value, "core", [(0, 1), (1, 0)])


def turn(value, by):
    count = lax.axis_size("z")
    return lax.ppermute(value, "z", [(i, (i + by) % count) for i in range(count)])


def ring_near(value):
    return (value, turn(value, 1), turn(value, -1), swap_cores(value))


def ring_far(near, work=None):
    value, below, above, other = near
    half = value.shape[0] // 2
    far_low, far_high = ring_step(below[:half], above[half:], work)
    swapped = [swap_cores(part) for part in (above, below, far_low, far_high)]
    return [value, above, below, far_low, far_high, other] + swapped


def ring_places(rows):
    half = rows // 2
    places = [(0, 0, rows), (1, 0, rows), (3, 0, rows), (2, 0, half), (2, half, half)]
    return [(by, side, at, size) for side in range(2) for by, at, size in places]


def ring_whole(pieces):
    count = lax.axis_size("z")
    z, core = lax.axis_index("z"), lax.axis_index("core")
    rows, columns = pieces[0].shape
    whole = jnp.zeros((2 * count * rows, columns), pieces[0].dtype)
    for piece, (by, side, first, _) in zip(pieces, ring_places(rows)):
        span = (1 - core if side else core) * count + lax.rem(z + by, count)
        whole = lax.dynamic_update_slice(whole, piece, (span * rows + first, 0))
    return whole


def scatter_direct(part, axis):
    count = lax.axis_size(axis)
    index = lax.axis_index(axis)

    def piece(by):
        return lax.dynamic_index_in_dim(part, lax.rem(index + by, count), 0, keepdims=False)

    found = piece(0).astype(f32)
    for by in range(1, count):
        pairs = [(i, (i + by) % count) for i in range(count)]
        found = found + lax.ppermute(piece(by), axis, pairs).astype(f32)
    return found


def ring_step(low, high, work):
    if work is None:
        return turn(low, 1), turn(high, -1)
    operand, function = work
    low, high, operand = lax.optimization_barrier((low, high, operand))
    below, above = turn(low, 1), turn(high, -1)
    below, above, _ = lax.optimization_barrier((below, above, function(operand)))
    return below, above


def far_pieces(operands, takes=0):
    model = operands[2].shape[0]
    half = operands[1].shape[0] // lax.axis_size("z") // 2
    return product_pieces((2,), *operands, [((half, model), bf16)] * 2, takes)


def near_pieces(operands, takes=0):
    model = operands[2].shape[0]
    rows = operands[1].shape[0] // lax.axis_size("z")
    return product_pieces((1, 3, 0), *operands, [((rows, model), f32)] * 3, takes, 24)


def all_pieces(operands, takes=0):
    model = operands[2].shape[0]
    rows = operands[1].shape[0] // lax.axis_size("z")
    outs = [((rows // 2, model), bf16)] * 2 + [((rows, model), f32)] * 3
    return product_pieces((2, 1, 3, 0), *operands, outs, takes)


def near_sums(ahead, behind, from_below, from_above):
    return rows_call(near_body, (ahead, behind, from_below, from_above), [(ahead.shape, bf16)] * 2)


def ring_scatter(x, got, weights, others, at, body, extra, outs, first=None, second=None, last=None):
    operands = (x, got, weights, others, at)
    if first is not None:
        low, high, ahead, behind, mine = all_pieces(operands, 9)
        below, above = ring_step(low, high, first)
    else:
        low, high = far_pieces(operands, 5)
        found = []

        def near_work(operand):
            found.extend(near_pieces(operand + operands[2:], 6))
            return found

        below, above = ring_step(low, high, ((x, got), near_work))
        ahead, behind, mine = found
    below, above = ring_step(*near_sums(ahead, behind, below, above), second)
    if last is not None:
        below, above = last(below, above)
    return rows_call(body, (mine, below, above) + extra, outs)


class Sizes:
    def __init__(self, rows, seg, spans, width, conv_width):
        self.rows, self.seg, self.spans = rows, seg, spans
        self.width, self.conv_width = width, conv_width
        self.stride = rows * seg
        self.tokens = spans * self.stride
    def pair(self, position):
        count = self.rows * self.spans
        return pl.ds(pl.multiple_of(position * count, count), count)


def weave(sizes, source, target, back=False):
    blocks = sizes.seg // 8

    def step(index, carried):
        row, block = index // blocks, index % blocks
        natural = [
            pl.ds(
                pl.multiple_of(
                    (span % 2 * (sizes.spans // 2) + span // 2) * sizes.stride
                    + row * sizes.seg
                    + block * 8,
                    8,
                ),
                8,
            )
            for span in range(sizes.spans)
        ]
        woven = [
            pl.ds(pl.multiple_of(((block * 8 + place) * sizes.rows + row) * sizes.spans, 8), 8)
            for place in range(8)
        ]
        reads, writes = (woven, natural) if back else (natural, woven)
        for start in range(0, sizes.width, lanes):
            columns = slice(start, start + lanes)
            tiles = jnp.stack([source[at, columns] for at in reads], axis=0)
            tiles = jnp.transpose(tiles, (1, 0, 2))
            for place, at in enumerate(writes):
                target[at, columns] = tiles[place]
        return carried

    lax.fori_loop(0, sizes.rows * blocks, step, 0)


def span_before(tile, first):
    place = lax.broadcasted_iota(jnp.int32, tile.shape, 0)
    return jnp.where(place == 0, first, pltpu.roll(tile, 1, 0))


def span_after(tile, last):
    count = tile.shape[0]
    place = lax.broadcasted_iota(jnp.int32, tile.shape, 0)
    return jnp.where(place == count - 1, last, pltpu.roll(tile, count - 1, 0))


def across_spans(product, total, backward):
    spans = product.shape[0]
    so_far = (jnp.ones_like(product[:1]), jnp.zeros_like(total[:1]))
    ahead = [None] * spans
    for span in range(spans - 1, -1, -1) if backward else range(spans):
        ahead[span] = so_far
        now = product[span : span + 1]
        so_far = (so_far[0] * now, total[span : span + 1] + now * so_far[1])
    products, totals = (jnp.concatenate(part, axis=0) for part in zip(*ahead))
    return products, totals, so_far


def from_others(sizes, index_ref, all_ref, peers, backward):
    mine = index_ref[0]
    entering = [jnp.zeros((1, sizes.width), f32) for _ in range(sizes.rows)]
    for step in range(peers - 1):
        peer = peers - 1 - step if backward else step
        ahead = peer > mine if backward else peer < mine
        for row in range(sizes.rows):
            product = all_ref[peer, row : row + 1, :]
            total = all_ref[peer, sizes.rows + row : sizes.rows + row + 1, :]
            entering[row] = jnp.where(ahead, total + product * entering[row], entering[row])
    return entering


def sigmoid(values):
    return 0.5 * jnp.tanh(0.5 * values) + 0.5


def keep_ends(sizes, found, prefix, last, backward):
    rows, spans = sizes.rows, sizes.spans
    ends = []
    for row in range(rows):
        mine = slice(row * spans, (row + 1) * spans)
        products, totals, whole = across_spans(found[0][mine], found[1][mine], backward)
        prefix[row * spans : (row + 1) * spans, :] = products
        prefix[(rows + row) * spans : (rows + row + 1) * spans, :] = totals
        ends.append(whole)
    padding = [jnp.zeros((last.shape[1] - 2 * rows, sizes.width), f32)]
    block = jnp.concatenate([end[0] for end in ends] + [end[1] for end in ends] + padding, axis=0)
    for peer in range(last.shape[0]):
        last[peer] = block


def entering_spans(sizes, prefix, entering):
    rows, spans = sizes.rows, sizes.spans
    return jnp.concatenate(
        [
            prefix[(rows + row) * spans : (rows + row + 1) * spans, :]
            + prefix[row * spans : (row + 1) * spans, :] * entering[row]
            for row in range(rows)
        ],
        axis=0,
    )


def per_row(sizes, function, pair, edges):
    spans = sizes.spans
    return jnp.concatenate(
        [function(pair[row * spans : (row + 1) * spans], edges[row]) for row in range(sizes.rows)],
        axis=0,
    )


parts = 4
dp = ("x", "y")


class Parts:
    def __init__(self, sources, targets, sems):
        self.pairs = list(zip(sources, targets))
        self.sems = sems

    def copy(self, which, part):
        source, target = self.pairs[which]
        count = source.shape[0] // parts
        at = pl.ds(pl.multiple_of(part * count, count), count)
        return pltpu.make_async_copy(source.at[at], target.at[at], self.sems.at[which, part])

    def start(self, part, which=None):
        for index in range(len(self.pairs)) if which is None else which:
            self.copy(index, part).start()

    def wait(self, part, which=None):
        for index in range(len(self.pairs)) if which is None else which:
            self.copy(index, part).wait()


def gates_kernel(sizes, conv_in, tail, masks, table, params, *refs):
    outs, refs = refs[:10], refs[10:]
    prefix, last, refs = refs[0], refs[1], refs[2:]
    held, refs = refs[:10], refs[10:]
    conv_now, conv_woven, mixed, sems = refs
    product, total, decay, conv_low, woven_low, direct_by, entry_by, state_by, rest_by, slope_by = held
    sent = Parts(held, outs, sems)
    seg, taps, width, spans = sizes.seg, sizes.conv_width, sizes.width, sizes.spans
    rows = sizes.rows
    bias = params[taps : taps + 1, :]
    weave(sizes, conv_in, conv_woven)
    before = []
    for tap in range(1, taps):
        edges = [tail[row * 8 + 8 - tap : row * 8 + 9 - tap, :] for row in range(rows)]
        before.append(per_row(sizes, span_before, conv_woven[sizes.pair(seg - tap), :], edges))
    recur_bias = params[taps + 1 : taps + 2, :]
    entry_bias = params[taps + 2 : taps + 3, :]
    rate = params[taps + 3 : taps + 4, :] * (-decay_power)
    per_part = seg // parts
    part_rows = per_part * rows * spans

    def part_step(part, carried):
        before, found = carried

        def conv_step(step, before):
            at = sizes.pair(part * per_part + step)
            valid = masks[at, :]
            tile = conv_woven[at, :]
            value = bias + params[0:1, :] * tile
            for tap in range(1, taps):
                value = value + params[tap : tap + 1, :] * before[tap - 1] * (
                    valid[:, tap : tap + 1]
                )
            conv_now[sizes.pair(step), :] = value
            conv_low[at, :] = value.astype(bf16)
            woven_low[at, :] = tile.astype(bf16)
            return (tile,) + tuple(before[:-1])

        before = lax.fori_loop(0, per_part, conv_step, before, unroll=8)
        part_at = pl.ds(pl.multiple_of(part * part_rows, part_rows), part_rows)
        mixed[...] = dot(conv_low[part_at, :], table[...], 1, 1)

        def gate_step(step, carried):
            at = sizes.pair(part * per_part + step)
            here = sizes.pair(step)
            starting = jnp.broadcast_to(masks[at, :][:, 0:1], (rows * spans, width)) > 0.5
            recur_now = sigmoid(mixed[here, :width] + recur_bias)
            entry_now = sigmoid(mixed[here, width:] + entry_bias)
            conv_here = conv_now[here, :]
            decay_now = jnp.where(starting, 0.0, jnp.exp(rate * recur_now))
            squared = 1.0 - decay_now * decay_now + mult_eps
            root = lax.rsqrt(squared)
            scale = jnp.where(starting, 1.0, squared * root)
            direct = scale * entry_now
            gated = entry_now * conv_here
            by_state = decay_now * recur_now
            product_now = carried[0] * decay_now
            total_now = carried[1] * decay_now + direct * conv_here
            product[at, :] = product_now
            total[at, :] = total_now
            decay[at, :] = decay_now
            direct_by[at, :] = direct.astype(bf16)
            entry_by[at, :] = (scale * gated * (1.0 - entry_now)).astype(bf16)
            state_by[at, :] = by_state.astype(bf16)
            rest_by[at, :] = (by_state * gated * decay_now * root).astype(bf16)
            slope_by[at, :] = (rate * (1.0 - recur_now)).astype(bf16)
            return (product_now, total_now)

        found = lax.fori_loop(0, per_part, gate_step, found, unroll=8)
        sent.start(part)
        return (before, found)

    shape = (rows * spans, width)
    first = (jnp.ones(shape, f32), jnp.zeros(shape, f32))
    _, found = lax.fori_loop(0, parts, part_step, (tuple(before), first))
    keep_ends(sizes, found, prefix, last, False)
    for part in range(parts):
        sent.wait(part)


def states_kernel(sizes, peers, index, gathered, prefix, *refs):
    sources, pre_hbm, outs, entered, refs = refs[:2], refs[2], refs[3:5], refs[5], refs[6:]
    product, total, branch_pre, mixer_in, natural, states, in_sems, pre_sem, out_sems = refs
    taken = Parts(sources, (product, total), in_sems)
    sent = Parts((mixer_in, natural), outs, out_sems)
    pre_copy = pltpu.make_async_copy(pre_hbm, branch_pre, pre_sem)
    for part in range(parts):
        taken.start(part)
    pre_copy.start()
    entering = from_others(sizes, index, gathered, peers, False)
    entered[...] = jnp.zeros(entered.shape, f32)
    for row in range(sizes.rows):
        entered[row : row + 1, :] = entering[row]
    spans_in = entering_spans(sizes, prefix, entering)
    per_part = sizes.seg // parts
    for part in range(parts):
        taken.wait(part)

        def state_step(step, carried, part=part):
            at = sizes.pair(part * per_part + step)
            states[at, :] = total[at, :] + product[at, :] * spans_in
            return carried

        lax.fori_loop(0, per_part, state_step, 0, unroll=8)
    weave(sizes, states, natural, True)
    for part in range(parts):
        sent.start(part, (1,))
    pre_copy.wait()
    step_rows = 32
    steps = sizes.tokens // parts // step_rows

    def act_part(part, carried):
        def act_step(step, carried):
            start = pl.multiple_of((part * steps + step) * step_rows, step_rows)
            at = pl.ds(start, step_rows)
            mixer_in[at, :] = (natural[at, :] * gelu_parts(branch_pre[at, :])[0]).astype(bf16)
            return carried

        lax.fori_loop(0, steps, act_step, 0, unroll=4)
        sent.start(part, (0,))
        return carried

    lax.fori_loop(0, parts, act_part, 0)
    for part in range(parts):
        sent.wait(part)


def recur_kernel(sizes, entered, *refs):
    sources, out, refs = refs[:3], refs[3], refs[4:]
    natural, state_by, rest_by, recur_by, states, in_sems, out_sems = refs
    taken = Parts(sources, (natural, state_by, rest_by), in_sems)
    sent = Parts((recur_by,), (out,), out_sems)
    for which in range(3):
        for part in range(parts):
            taken.start(part, (which,))
    for part in range(parts):
        taken.wait(part)
    weave(sizes, natural, states)
    entering = [entered[row : row + 1, :] for row in range(sizes.rows)]
    before = per_row(sizes, span_before, states[sizes.pair(sizes.seg - 1), :], entering)
    per_part = sizes.seg // parts

    def recur_part(part, before):
        def recur_step(step, before):
            at = sizes.pair(part * per_part + step)
            found = before * state_by[at, :].astype(f32) - rest_by[at, :].astype(f32)
            recur_by[at, :] = found.astype(bf16)
            return states[at, :]

        before = lax.fori_loop(0, per_part, recur_step, before, unroll=8)
        sent.start(part)
        return before

    lax.fori_loop(0, parts, recur_part, before)
    for part in range(parts):
        sent.wait(part)


def reverse_kernel(
    sizes, out_at, place, pre_hbm, natural_hbm, decay_hbm, weights_hbm, *refs
):
    places = ring_places(sizes.stride)
    pieces, refs = refs[: len(places)], refs[len(places) :]
    outs, prefix, last, refs = refs[:4], refs[4], refs[5], refs[6:]
    grad_branch, grad_branch_pre, own_part, later_by, grad_states = refs[:5]
    branch_pre, natural, decay, grad_mixer, weights = refs[5:10]
    in_sems, piece_sems, out_sems, branch_sems = refs[10:]
    width, spans = sizes.width, sizes.spans
    z, core = place[0], place[1]
    stride = sizes.stride
    copies = []
    for number, (piece, (by, side, first, count)) in enumerate(zip(pieces, places)):
        span = (1 - core if side else core) * (spans // 2) + lax.rem(z + by, spans // 2)
        at = pl.ds(pl.multiple_of(span * stride + first, sizes.seg), count)
        copy = pltpu.make_async_copy(piece, grad_branch.at[at], piece_sems.at[number])
        copies.append((side, copy))
    taken = [
        pltpu.make_async_copy(source, target, in_sems.at[number])
        for number, (source, target) in enumerate(
            (
                (weights_hbm.at[:, out_at * width : (out_at + 1) * width], weights),
                (pre_hbm, branch_pre),
                (natural_hbm, natural),
                (decay_hbm, decay),
            )
        )
    ]
    taken[0].start()
    for _, copy in copies:
        copy.start()
    for copy in taken[1:]:
        copy.start()
    taken[0].wait()
    half = sizes.tokens // 2
    branch_out = []
    for side in range(2):
        for piece_side, copy in copies:
            if piece_side == side:
                copy.wait()
        at = pl.ds(pl.multiple_of((1 - core if side else core) * half, half), half)
        out = pltpu.make_async_copy(grad_branch.at[at], outs[0].at[at], branch_sems.at[side])
        out.start()
        branch_out.append(out)
        grad_mixer[at, :] = dot(grad_branch[at, :], weights[...])
    taken[1].wait()
    taken[2].wait()
    sent = Parts((grad_branch_pre, own_part, later_by), outs[1:], out_sems)
    step_rows = 32
    steps = sizes.tokens // parts // step_rows

    def part_step(part, carried):
        def gelu_step(step, carried):
            start = pl.multiple_of((part * steps + step) * step_rows, step_rows)
            at = pl.ds(start, step_rows)
            grad = grad_mixer[at, :]
            act, slope = gelu_parts(branch_pre[at, :])
            grad_branch_pre[at, :] = (grad * natural[at, :] * slope).astype(bf16)
            grad_mixer[at, :] = grad * act
            return carried

        lax.fori_loop(0, steps, gelu_step, 0, unroll=2)
        sent.start(part, (0,))
        return carried

    lax.fori_loop(0, parts, part_step, 0)
    weave(sizes, grad_mixer, grad_states)
    taken[3].wait()
    per_part = sizes.seg // parts

    def scan_part(index, carried):
        part = parts - 1 - index

        def scan_step(step, carried):
            at = sizes.pair(part * per_part + per_part - 1 - step)
            decay_now = decay[at, :]
            own = carried[1] + grad_states[at, :]
            own_part[at, :] = own
            later_by[at, :] = carried[0]
            return (carried[0] * decay_now, own * decay_now)

        carried = lax.fori_loop(0, per_part, scan_step, carried, unroll=4)
        sent.start(part, (1, 2))
        return carried

    shape = (sizes.rows * spans, width)
    first = (jnp.ones(shape, f32), jnp.zeros(shape, f32))
    found = lax.fori_loop(0, parts, scan_part, first)
    keep_ends(sizes, found, prefix, last, True)
    for part in range(parts):
        sent.wait(part)
    for out in branch_out:
        out.wait()


def gates_back_kernel(sizes, peers, index, gathered, prefix, tail, masks, table, params, *refs):
    sources, branch_hbm, refs = refs[:7], refs[7], refs[8:]
    outs, ends, head, sums, refs = refs[:2], refs[2], refs[3], refs[4], refs[5:]
    held, refs = refs[:7], refs[7:]
    grad_gates, grad_front, grad_conv, grad_conv_in, natural = refs[:5]
    in_sems, branch_sem, out_sems = refs[5:]
    own_part, later_by, direct_by, entry_by, recur_by, slope_by, woven_low = held
    seg, taps, width, spans = sizes.seg, sizes.conv_width, sizes.width, sizes.spans
    rows = sizes.rows
    taken = Parts(sources, held, in_sems)
    branch_copy = pltpu.make_async_copy(
        branch_hbm, grad_front.at[:, width : 2 * width], branch_sem
    )
    for part in range(2):
        taken.start(part, range(6))
    entering = from_others(sizes, index, gathered, peers, True)
    spans_in = entering_spans(sizes, prefix, entering)
    shape = (rows * spans, width)

    def gate_step(position, carried):
        at = sizes.pair(position)
        rate_sum, recur_sum, entry_sum = carried
        direct, entry, recur, slope = (
            ref[at, :].astype(f32) for ref in (direct_by, entry_by, recur_by, slope_by)
        )
        carried_now = own_part[at, :] + later_by[at, :] * spans_in
        rated = carried_now * recur
        recur_low = (rated * slope).astype(bf16)
        entry_low = (carried_now * entry).astype(bf16)
        grad_gates[at, :width] = recur_low
        grad_gates[at, width:] = entry_low
        grad_conv[at, :] = carried_now * direct
        return (
            rate_sum + rated,
            recur_sum + recur_low.astype(f32),
            entry_sum + entry_low.astype(f32),
        )

    empty = jnp.zeros(shape, f32)
    gate_sums = (empty,) * 3
    per_part = seg // parts
    part_rows = per_part * rows * spans
    sent = Parts((grad_gates, grad_front), outs, out_sems)
    for part in range(parts):
        taken.wait(part, range(6))
        if part + 2 < parts:
            taken.start(part + 2, range(6))
        elif part + 2 == parts:
            for later in range(parts):
                taken.start(later, (6,))
        else:
            branch_copy.start()
        gate_sums = lax.fori_loop(
            part * per_part, (part + 1) * per_part, gate_step, gate_sums, unroll=4
        )
        sent.start(part, (0,))
        at = pl.ds(part * part_rows, part_rows)
        grad_conv[at, :] = grad_conv[at, :] + dot(grad_gates[at, :], table[...], 1, 0)

    def weighted(position):
        at = sizes.pair(position)
        grad = grad_conv[at, :]
        valid = masks[at, :]
        return [grad] + [grad * valid[:, tap : tap + 1] for tap in range(1, taps)]

    tap_rows = [params[tap : tap + 1, :] for tap in range(taps)]
    ahead = [weighted(position) for position in range(taps - 1)]
    nothing_after = [jnp.zeros((1, width), f32)] * rows
    held_ahead = [
        per_row(sizes, span_after, ahead[place][tap], nothing_after)
        for tap in range(1, taps)
        for place in range(tap)
    ]

    def conv_step(index, carried):
        held_now, now_sums = carried
        at = sizes.pair(seg - 1 - index)
        tile = woven_low[at, :].astype(f32)
        now = weighted(seg - 1 - index)
        value = tap_rows[0] * now[0]
        new_held, new_sums, first = [], [now_sums[0] + tile * now[0]], 0
        for tap in range(1, taps):
            far = held_now[first + tap - 1]
            value = value + tap_rows[tap] * far
            new_sums.append(now_sums[tap] + tile * far)
            new_held += [now[tap]] + list(held_now[first : first + tap - 1])
            first += tap
        new_sums.append(now_sums[taps] + now[0])
        grad_conv_in[at, :] = value
        return tuple(new_held), tuple(new_sums)

    for part in range(parts):
        taken.wait(part, (6,))
    held_ahead, tap_sums = lax.fori_loop(
        0, seg, conv_step, (tuple(held_ahead), (empty,) * (taps + 1)), unroll=8
    )
    tap_sums = list(tap_sums)
    head[...] = jnp.zeros(head.shape, f32)
    for row in range(rows):
        for back in range(1, taps):
            value = jnp.zeros((1, width), f32)
            tail_row = tail[row * 8 + 8 - back : row * 8 + 9 - back, :]
            first = 0
            for tap in range(1, taps):
                if tap >= back:
                    first_row = held_ahead[first + tap - back][row * spans : row * spans + 1]
                    value = value + tap_rows[tap] * first_row
                    tap_sums[tap] = tap_sums[tap] + jnp.concatenate(
                        [tail_row * first_row, jnp.zeros((rows * spans - 1, width), f32)], axis=0
                    )
                first += tap
            head[row * 8 + 8 - back : row * 8 + 9 - back, :] = value
    weave(sizes, grad_conv_in, natural, True)
    branch_copy.wait()
    step_rows = 32
    steps = sizes.tokens // parts // step_rows

    def part_step(part, carried):
        def front_step(step, carried):
            start = pl.multiple_of((part * steps + step) * step_rows, step_rows)
            at = pl.ds(start, step_rows)
            grad_front[at, :width] = natural[at, :].astype(bf16)
            return carried

        lax.fori_loop(0, steps, front_step, 0, unroll=4)
        sent.start(part, (1,))
        return carried

    lax.fori_loop(0, parts, part_step, 0)
    for row in range(rows):
        end = (spans - 1) * sizes.stride + (row + 1) * seg
        ends[row * 8 : row * 8 + 8, :] = natural[end - 8 : end, :]
    for place, part_sum in enumerate(tap_sums + [gate_sums[1], gate_sums[2], gate_sums[0]]):
        sums[place : place + 1, :] = jnp.sum(part_sum, axis=0, keepdims=True)
    for part in range(parts):
        sent.wait(part)


def rows_kernel(body, inputs, *refs):
    ins, outs = refs[:inputs], refs[inputs:]
    rows, step_rows = ins[0].shape[0], 32
    for start in range(0, rows, step_rows):
        body(start, slice(start, start + step_rows), ins, outs)


def rows_call(body, ins, outs):
    vmem = pl.BlockSpec(memory_space=pltpu.VMEM)
    return pl.pallas_call(
        partial(rows_kernel, body, len(ins)),
        out_shape=[jax.ShapeDtypeStruct(shape, kind) for shape, kind in outs],
        in_specs=[vmem] * len(ins),
        out_specs=[vmem] * len(outs),
        cost_estimate=no_cost,
        compiler_params=pltpu.CompilerParams(vmem_limit_bytes=20 * 1024 * 1024),
    )(*ins)


def near_body(start, at, ins, outs):
    half = ins[2].shape[0]
    ahead, behind = ins[0][at, :], ins[1][at, :]
    if start < half:
        ahead = ahead + ins[2][at, :].astype(f32)
    else:
        behind = behind + ins[3][start - half : start - half + behind.shape[0], :].astype(f32)
    outs[0][at, :] = ahead.astype(bf16)
    outs[1][at, :] = behind.astype(bf16)


def own_sum(at, ins):
    return ins[0][at, :] + ins[1][at, :].astype(f32) + ins[2][at, :].astype(f32)


def branch_body(start, at, ins, outs):
    residual = own_sum(at, ins) + ins[3][at, :].astype(f32)
    outs[0][at, :] = residual
    outs[1][at, :] = (rms_unit(residual)[0] * ins[4][...]).astype(bf16)


def feed_back_body(start, at, ins, outs):
    grad = own_sum(at, ins)
    unit, inverse = rms_unit(ins[3][at, :])
    found = ins[4][at, :].astype(f32) + norm_back(grad, unit, inverse, ins[5][...])
    outs[0][at, :] = found
    outs[1][at, :] = found.astype(bf16)
    part = jnp.sum((grad * unit).reshape(-1, 8, grad.shape[1]), axis=0)
    outs[2][...] = part if start == 0 else outs[2][...] + part


def feed_body(start, at, ins, outs):
    outs[0][at, :] = (own_sum(at, ins) + ins[3][at, :]).astype(bf16)


def tokens_body(start, at, ins, outs):
    grad = own_sum(at, ins)
    unit, inverse = rms_unit(ins[3][at, :].astype(f32))
    outs[0][at, :] = ins[4][at, :] + norm_back(grad, unit, inverse, ins[5][...])


def call(kernel, outs, scratch, *operands, scalars=0, anywhere=(), out_anywhere=0, sems=(), takes=0):
    vmem = pl.BlockSpec(memory_space=pltpu.VMEM)
    hbm = pl.BlockSpec(memory_space=pl.ANY)
    in_specs = [pl.BlockSpec(memory_space=pltpu.SMEM)] * scalars
    in_specs += [vmem] * (len(operands) - scalars)
    for index in anywhere:
        in_specs[index] = hbm
    return pl.pallas_call(
        kernel,
        out_shape=[jax.ShapeDtypeStruct(shape, kind) for shape, kind in outs],
        in_specs=in_specs,
        out_specs=[hbm] * out_anywhere + [vmem] * (len(outs) - out_anywhere),
        scratch_shapes=[pltpu.VMEM(shape, kind) for shape, kind in scratch]
        + [pltpu.SemaphoreType.DMA(shape) for shape in sems],
        cost_estimate=cost(takes),
        compiler_params=pltpu.CompilerParams(vmem_limit_bytes=60 * 1024 * 1024),
    )(*operands)


def product_kernel(at, bys, place, x_hbm, got_hbm, own_hbm, other_hbm, *refs):
    count = (len(refs) - 5) // 2
    targets, outs = refs[:count], refs[count : 2 * count]
    x, weights, x_sem, weight_sem, out_sem = refs[2 * count :]
    depth = got_hbm.shape[1]
    span = x.shape[0] // len(bys)
    rows = got_hbm.shape[0]
    columns = 512
    steps = weights.shape[0] // columns
    halves = (slice(0, depth), slice(depth, 2 * depth))

    def weight_copies(index):
        place = slice(index * columns, (index + 1) * columns)
        return [
            pltpu.make_async_copy(
                source.at[place, at * depth : (at + 1) * depth],
                weights.at[place, half],
                weight_sem.at[2 * index + side],
            )
            for side, (source, half) in enumerate(zip((own_hbm, other_hbm), halves))
        ]

    x_copies = []
    for number, by in enumerate(bys):
        first = lax.rem(place[0] + by, rows // span) * span
        to = slice(number * span, (number + 1) * span)
        mine = pl.ds(pl.multiple_of(place[1] * rows + first, span), span)
        theirs = pl.ds(pl.multiple_of(first, span), span)
        x_copies += [
            pltpu.make_async_copy(x_hbm.at[mine], x.at[to, halves[0]], x_sem.at[2 * number]),
            pltpu.make_async_copy(
                got_hbm.at[theirs], x.at[to, halves[1]], x_sem.at[2 * number + 1]
            ),
        ]
    sent = []
    for side in range(2):
        for copy in x_copies[side::2]:
            copy.start()
        weight_copies(0)[side].start()
    for copy in weight_copies(1):
        copy.start()
    for index in range(steps):
        place_now = slice(index * columns, (index + 1) * columns)
        if index == 0:
            value = 0.0
            for side, half in enumerate(halves):
                for copy in x_copies[side::2]:
                    copy.wait()
                weight_copies(0)[side].wait()
                value = value + dot(x[:, half], weights[place_now, half], 1, 1)
        else:
            for copy in weight_copies(index):
                copy.wait()
        if index + 2 < steps:
            for copy in weight_copies(index + 2):
                copy.start()
        if index > 0:
            value = dot(x[...], weights[place_now, :], 1, 1)
        first = 0
        for number, (out, target) in enumerate(zip(outs, targets)):
            out[:, place_now] = value[first : first + out.shape[0]].astype(out.dtype)
            first += out.shape[0]
            copy = pltpu.make_async_copy(
                out.at[:, place_now], target.at[:, place_now], out_sem.at[number, index]
            )
            copy.start()
            sent.append(copy)
    for copy in sent:
        copy.wait()


def product_pieces(bys, x, got, weights, others, at, outs, takes, room=60):
    depth, model = got.shape[1], weights.shape[0]
    span = got.shape[0] // lax.axis_size("z")
    place = jnp.stack([lax.axis_index("z"), lax.axis_index("core")]).astype(jnp.int32)
    anywhere = pl.BlockSpec(memory_space=pl.ANY)
    return pl.pallas_call(
        partial(product_kernel, at, bys),
        out_shape=[jax.ShapeDtypeStruct(shape, kind) for shape, kind in outs],
        in_specs=[pl.BlockSpec(memory_space=pltpu.SMEM)] + [anywhere] * 4,
        out_specs=[anywhere] * len(outs),
        scratch_shapes=[pltpu.VMEM(shape, kind) for shape, kind in outs]
        + [
            pltpu.VMEM((len(bys) * span, 2 * depth), bf16),
            pltpu.VMEM((model, 2 * depth), bf16),
            pltpu.SemaphoreType.DMA((2 * len(bys),)),
            pltpu.SemaphoreType.DMA((2 * model // 512,)),
            pltpu.SemaphoreType.DMA((len(outs), model // 512)),
        ],
        cost_estimate=cost(takes),
        compiler_params=pltpu.CompilerParams(vmem_limit_bytes=room * 1024 * 1024),
    )(place, x, got, weights, others)


def swap_rows(x):
    rows = x.shape[0] // 2
    theirs = (1 - lax.axis_index("core")) * rows
    return swap_cores(lax.dynamic_slice_in_dim(x, theirs, rows, 0))


def feed_kernel(aliased, sends, core, x_hbm, grad_hbm, weights_hbm, *refs):
    refs = refs[aliased:]
    hidden_hbm, both_hbm, refs = refs[0], refs[1], refs[2:]
    if sends:
        send_hbm, refs = refs[0], refs[1:]
    x, grad, weights, pre, hidden, both, in_sem, weight_sem, out_sem = refs
    rows = x.shape[0]
    inner = grad.shape[1]
    mine = pl.ds(pl.multiple_of(core[0] * rows, rows), rows)
    copies = [
        pltpu.make_async_copy(x_hbm.at[mine], x, in_sem.at[0]),
        pltpu.make_async_copy(grad_hbm.at[mine], grad, in_sem.at[1]),
    ]
    columns = weights.shape[2]
    count = 2 * inner // columns

    def weight_copy(index):
        at = slice(index * columns, (index + 1) * columns)
        return pltpu.make_async_copy(
            weights_hbm.at[:, at], weights.at[index], weight_sem.at[index]
        )

    copies[0].start()
    for index in range(count):
        weight_copy(index).start()
    copies[1].start()
    copies[0].wait()
    for index in range(count):
        weight_copy(index).wait()
        pre[:, index * columns : (index + 1) * columns] = dot(x[...], weights[index])
    copies[1].wait()
    step_rows = 32
    outs = []

    def out_copies(part):
        size = rows // parts
        here = pl.ds(pl.multiple_of(part * size, size), size)
        there = pl.ds(pl.multiple_of(core[0] * rows + part * size, size), size)
        found = [
            pltpu.make_async_copy(hidden.at[here], hidden_hbm.at[there], out_sem.at[part, 0]),
            pltpu.make_async_copy(both.at[here], both_hbm.at[there], out_sem.at[part, 1]),
        ]
        if sends:
            found.append(
                pltpu.make_async_copy(both.at[here], send_hbm.at[here], out_sem.at[part, 2])
            )
        return found

    steps = rows // parts // step_rows

    def part_step(part, carried):
        def act_step(step, carried):
            start = pl.multiple_of((part * steps + step) * step_rows, step_rows)
            at = pl.ds(start, step_rows)
            act, slope = gelu_parts(pre[at, :inner])
            up = pre[at, inner:]
            grad_now = grad[at, :]
            hidden[at, :] = (act * up).astype(bf16)
            both[at, :inner] = (grad_now * up * slope).astype(bf16)
            both[at, inner:] = (grad_now * act).astype(bf16)
            return carried

        lax.fori_loop(0, steps, act_step, 0)
        for copy in out_copies(part):
            copy.start()
        return carried

    lax.fori_loop(0, parts, part_step, 0)
    for part in range(parts):
        for copy in out_copies(part):
            copy.wait()


def feed_forward(core, flat, grad_hidden, weights, sends, given):
    tokens, model = flat.shape
    inner = grad_hidden.shape[1]
    rows = tokens // 2
    columns = 512
    anywhere = pl.BlockSpec(memory_space=pl.ANY)
    outs = [(tokens, inner), (tokens, 2 * inner)] + [(rows, 2 * inner)] * sends
    return pl.pallas_call(
        partial(feed_kernel, len(given), sends),
        out_shape=[jax.ShapeDtypeStruct(shape, bf16) for shape in outs],
        in_specs=[pl.BlockSpec(memory_space=pltpu.SMEM)] + [anywhere] * (3 + len(given)),
        out_specs=[anywhere] * len(outs),
        scratch_shapes=[
            pltpu.VMEM((rows, model), bf16),
            pltpu.VMEM((rows, inner), f32),
            pltpu.VMEM((2 * inner // columns, model, columns), bf16),
            pltpu.VMEM((rows, 2 * inner), f32),
            pltpu.VMEM((rows, inner), bf16),
            pltpu.VMEM((rows, 2 * inner), bf16),
            pltpu.SemaphoreType.DMA((2,)),
            pltpu.SemaphoreType.DMA((2 * inner // columns,)),
            pltpu.SemaphoreType.DMA((parts, 3)),
        ],
        input_output_aliases={4: 0, 5: 1} if given else {},
        cost_estimate=cost(8),
        compiler_params=pltpu.CompilerParams(vmem_limit_bytes=60 * 1024 * 1024),
    )(
        jnp.reshape(core, (1,)).astype(jnp.int32),
        flat,
        grad_hidden,
        weights,
        *given,
    )


def weight_kernel(with_sums, filled, left, right, *refs):
    value = dot(left[...], right[...], 0, 0)
    if with_sums:
        weight, (out, sums) = refs[0], refs[1 + filled :]
        product = value * weight[...].astype(f32)
        sums[...] = sum(
            product[:, start : start + lanes] for start in range(0, product.shape[1], lanes)
        )
    else:
        out = refs[filled]
    out[...] = value.astype(bf16).reshape(out.shape)


def weight_grad(left, right, width, total, place=0, given=None, weight=None, weight_at=0, blocks=0, room=60, peers=0, more=0):
    depth, rows = left.shape
    block = 512 if width > 1024 else 1024
    blocks = blocks or right.shape[1] // width
    in_specs = [
        pl.BlockSpec((depth, block), lambda j, i: (0, i)),
        pl.BlockSpec((depth, width), lambda j, i: (0, j)),
    ]
    operands = [left, right]
    out_shape = [jax.ShapeDtypeStruct((rows, total), bf16)]
    out_specs = [pl.BlockSpec((block, width), lambda j, i: (i, j + place))]
    if peers:
        share = rows // peers
        out_shape = [jax.ShapeDtypeStruct((peers, share + more, total), bf16)]
        out_specs = [pl.BlockSpec((block // share, share, width), lambda j, i: (i, 0, j + place))]
    if weight is not None:
        in_specs.append(pl.BlockSpec((block, width), lambda j, i: (i, weight_at)))
        operands.append(weight)
        out_shape.append(jax.ShapeDtypeStruct((rows, lanes), f32))
        out_specs.append(pl.BlockSpec((block, lanes), lambda j, i: (i, 0)))
    aliases = {}
    if given is not None:
        aliases = {len(operands): 0}
        in_specs.append(pl.BlockSpec(memory_space=pl.ANY))
        operands.append(given)
    found = pl.pallas_call(
        partial(weight_kernel, weight is not None, given is not None),
        grid=(blocks, rows // block),
        out_shape=out_shape,
        in_specs=in_specs,
        out_specs=out_specs,
        input_output_aliases=aliases,
        cost_estimate=pl.CostEstimate(
            flops=2 * depth * rows * blocks * width,
            bytes_accessed=2 * (depth * rows + depth * blocks * width + rows * blocks * width),
            transcendentals=0,
        ),
        compiler_params=pltpu.CompilerParams(vmem_limit_bytes=room * 1024 * 1024),
    )(*operands)
    return found if weight is not None else found[0]


def shards(
    tokens,
    cotangent,
    mixer_gain,
    feedforward_gain,
    branch_weight,
    input_weight,
    output_weight,
    recurrence_gate,
    input_gate,
    conv_kernel,
    conv_bias,
    recurrence_bias,
    input_bias,
    decay_param,
    gate_weight,
    up_weight,
    down_weight,
    doc_starts,
):
    spans = lax.axis_size("z") * 2
    core = lax.axis_index("core")
    dp_index = lax.axis_index(dp)
    peers = lax.axis_size(dp)
    rows, seg, model = tokens.shape
    units = branch_weight.shape[1]
    width = up_to(units, lanes)
    hidden_width = gate_weight.shape[1]
    taps = conv_kernel.shape[0]
    block = recurrence_gate.shape[0]
    blocks = units // block
    share = units // peers
    sizes = Sizes(rows, seg, spans, width, taps)
    own, length, block_tokens = rows * seg, seg * spans, sizes.tokens
    depth = model // peers

    mine = jnp.reshape(dp_index, (1,)).astype(jnp.int32)

    unit_one = rms_unit(tokens.reshape(own, model).astype(f32))[0]
    gain_one = mixer_gain.astype(f32)
    gain_two = feedforward_gain.astype(f32)
    normed_one = (unit_one * gain_one).astype(bf16)
    one_near = ring_near(normed_one)
    one_far = ring_far(one_near)

    small = jnp.concatenate(
        tie_all(
            [
                recurrence_gate,
                input_gate,
                conv_kernel,
                conv_bias[None],
                recurrence_bias[None],
                input_bias[None],
                decay_param[None],
            ],
            normed_one,
        ),
        axis=0,
    ).T
    small_width = up_to(small.shape[1], lanes)
    small_rows = up_to(share, 8)
    small_all = gather_small(widen(widen(small, small_width, 1), small_rows, 0), dp)
    small_all = small_all[:, :share].reshape(units, small_width)
    front_weights = lax.all_gather(
        jnp.concatenate(
            [
                widen(input_weight, width, 1),
                widen(branch_weight, width, 1),
                widen(output_weight.T, width, 1),
            ],
            axis=1,
        ),
        dp,
        axis=0,
        tiled=True,
    )
    flat_one = ring_whole(one_far)
    cot_near = ring_near(tie(cotangent.reshape(own, model), one_far))
    def back_parts(weights):
        return jnp.concatenate([weights[0], weights[1], weights[2].T], axis=1)

    back_weights = lax.all_gather(
        back_parts(tie_all((gate_weight, up_weight, down_weight), one_near)),
        dp,
        axis=0,
        tiled=True,
    )
    input_matrix = front_weights[:, :width]
    branch_matrix = front_weights[:, width : 2 * width]
    down_turned = back_weights[:, 2 * hidden_width :]
    def diagonal(turned):
        lines = [
            jnp.pad(
                turned[h * block : (h + 1) * block],
                ((0, 0), (h * block, width - (h + 1) * block)),
            )
            for h in range(blocks)
        ]
        return widen(jnp.concatenate(lines, axis=0), width, 0)

    table = jnp.concatenate(
        [diagonal(small_all[:, :block]), diagonal(small_all[:, block : 2 * block])], axis=0
    )
    vectors = widen(small_all[:, 2 * block : 2 * block + taps + 4].astype(f32).T, width, 1)
    decay_values = vectors[taps + 3]
    params = widen(
        jnp.concatenate([vectors[: taps + 3], jax.nn.softplus(-decay_values)[None]], axis=0),
        up_to(taps + 4, 8),
        0,
    )

    positions = dp_index * length - (taps - 1) + jnp.arange(length + taps - 1, dtype=jnp.int32)
    starts = jnp.any(doc_starts[:, :, None] == positions[None, None, :], axis=1).astype(f32)
    columns = [starts[:, taps - 1 :]]
    valid = jnp.ones((rows, length), f32)
    for tap in range(1, taps):
        valid = valid * (1.0 - starts[:, taps - tap : taps - tap + length])
        columns.append(valid)
    masks = jnp.stack(columns + [valid] * (8 - taps), axis=-1)
    masks = masks.reshape(rows, spans, seg, 8).transpose(2, 0, 1, 3).reshape(block_tokens, 8)

    conv_in = dot(flat_one, input_matrix)
    conv_ends = conv_in.reshape(spans, rows, seg, width)[spans - 1, :, seg - 8 :, :]
    tail = lax.ppermute(
        conv_ends.reshape(rows * 8, width), dp, [(i, i + 1) for i in range(peers - 1)]
    )
    conv_in, cot_near = lax.optimization_barrier((conv_in, cot_near))
    flat = (block_tokens, width)
    prefix_kind, edge_kind = ((2 * rows * spans, width), f32), ((peers, 8, width), f32)
    kinds = [(flat, f32)] * 3 + [(flat, bf16)] * 7
    *gate_parts, prefix, last = call(
        partial(gates_kernel, sizes),
        kinds + [prefix_kind, edge_kind],
        kinds + [((block_tokens // parts, width), f32), (flat, f32)]
        + [((block_tokens // parts, 2 * width), f32)],
        conv_in,
        tail,
        masks,
        table,
        params,
        out_anywhere=10,
        sems=[(10, parts)],
    )
    product, total, decay, conv_low, woven_low, direct_by, entry_by, state_by, rest_by, slope_by = gate_parts
    front_other = swap_cores(tie(front_weights, last))
    kept = {}

    def branch_work(operand):
        kept["branch"] = dot(operand, branch_matrix)
        return kept["branch"]

    cot_far = ring_far(cot_near, (tie(flat_one, last), branch_work))
    branch_pre, _ = lax.optimization_barrier((kept["branch"], cot_far[3:5]))
    gathered = send_copies(last, dp)
    mixer_in, states_natural, entered = call(
        partial(states_kernel, sizes, peers),
        [(flat, bf16), (flat, f32), ((8, width), f32)],
        [(flat, f32)] * 3 + [(flat, bf16), (flat, f32), (flat, f32)],
        mine,
        gathered,
        prefix,
        product,
        total,
        branch_pre,
        scalars=1,
        anywhere=range(3, 6),
        out_anywhere=2,
        sems=[(2, parts), (), (2, parts)],
    )
    own_kind = ((own, model), f32)
    own_low = ((own, model), bf16)
    tokens_own, cotangent_own = (part.reshape(own, model) for part in (tokens, cotangent))
    residual, normed_two = ring_scatter(
        mixer_in,
        swap_rows(mixer_in),
        front_weights,
        front_other,
        2,
        branch_body,
        (tokens_own, gain_two[None]),
        [own_kind, own_low],
    )

    flat_two = lax.all_gather(normed_two, ("core", "z"), axis=0, tiled=True)
    back_other = swap_cores(tie(back_weights, normed_two))
    cotangent_flat = ring_whole(tie_all(cot_far, normed_two))
    grad_hidden = dot(cotangent_flat, down_turned)
    (recur_by,) = call(
        partial(recur_kernel, sizes),
        [(flat, bf16)],
        [(flat, f32), (flat, bf16), (flat, bf16), (flat, bf16), (flat, f32)],
        tie(entered, normed_two),
        states_natural,
        state_by,
        rest_by,
        anywhere=range(1, 4),
        out_anywhere=1,
        sems=[(3, parts), (1, parts)],
    )
    flat_two, back_other, recur_by = lax.optimization_barrier((flat_two, back_other, recur_by))
    hidden, grad_gate_up, gate_up_send = feed_forward(
        1 - core, flat_two, grad_hidden, back_weights, True, ()
    )
    gate_up_got = swap_cores(gate_up_send)
    hidden, grad_gate_up = feed_forward(
        core, flat_two, grad_hidden, back_weights, False, (hidden, grad_gate_up)
    )
    feed_width = 3 * hidden_width

    def gate_up_part(operand):
        kept["feed"] = weight_grad(flat_two, operand, 2 * hidden_width, feed_width)
        return kept["feed"]

    def down_part(operand):
        kept["feed"] = weight_grad(
            cotangent_flat, operand, hidden_width, feed_width, 2, kept["feed"], room=40
        )
        return kept["feed"]

    def feed_scatter(below, above):
        below, above, part = lax.optimization_barrier((below, above, kept["feed"]))
        kept["feed"] = lax.psum_scatter(part, dp, scatter_dimension=0, tiled=True)
        return below, above

    grad_residual, grad_branch_own, gain_two_rows = ring_scatter(
        grad_gate_up,
        gate_up_got,
        back_weights,
        back_other,
        0,
        feed_back_body,
        (residual, cotangent_own, gain_two[None]),
        [own_kind, own_low, ((8, model), f32)],
        (grad_gate_up, gate_up_part),
        (hidden, down_part),
        feed_scatter,
    )
    feed_grads = kept["feed"]
    gain_two_part = jnp.sum(gain_two_rows, axis=0)
    near = ring_near(grad_branch_own)
    hidden_got = swap_rows(tie(hidden, near[0]))
    feed_operands = (hidden, hidden_got, back_weights, back_other, 2)
    low, high, ahead, behind, feed_own = all_pieces(feed_operands)
    far = ring_far(tie_all(near, low, feed_own))

    places = jnp.stack([lax.axis_index("z"), core]).astype(jnp.int32)

    grad_branch, grad_branch_pre, own_part, later_by, back_prefix, back_last = call(
        partial(reverse_kernel, sizes, 2),
        [((block_tokens, model), bf16), (flat, bf16)]
        + [(flat, f32)] * 2
        + [prefix_kind, edge_kind],
        [((block_tokens, model), bf16), (flat, bf16)]
        + [(flat, f32)] * 7
        + [((model, width), bf16)],
        places,
        branch_pre,
        states_natural,
        decay,
        front_weights,
        *far,
        scalars=1,
        anywhere=range(1, 5 + len(far)),
        out_anywhere=4,
        sems=[(4,), (len(far),), (3, parts), (2,)],
        takes=24,
    )
    back_gathered = send_copies(back_last, dp)

    def output_work(operand):
        kept["middle"] = weight_grad(operand, mixer_in, width, 2 * width)
        return kept["middle"]

    from_below, from_above = ring_step(low, high, (grad_branch, output_work))
    ahead, behind = near_sums(ahead, behind, from_below, from_above)
    sum_rows = up_to(taps + 4, 8)
    wide = (block_tokens, 2 * width)

    def gates_back(operand):
        gathered, kept["middle"] = operand
        kept["gates"] = call(
            partial(gates_back_kernel, sizes, peers),
            [
                (wide, bf16),
                (wide, bf16),
                ((rows * 8, width), f32),
                ((rows * 8, width), f32),
                ((sum_rows, width), f32),
            ],
            [(flat, f32)] * 2
            + [(flat, bf16)] * 5
            + [(wide, bf16), (wide, bf16)]
            + [(flat, f32)] * 3,
            mine,
            gathered,
            back_prefix,
            tail,
            masks,
            table,
            params,
            own_part,
            later_by,
            direct_by,
            entry_by,
            recur_by,
            slope_by,
            woven_low,
            grad_branch_pre,
            scalars=1,
            anywhere=range(7, 15),
            out_anywhere=2,
            sems=[(7, parts), (), (2, parts)],
            takes=11,
        )
        return kept["gates"][-1]

    below, above = ring_step(ahead, behind, ((back_gathered, kept["middle"]), gates_back))
    kept["gates"], below, above = lax.optimization_barrier((kept["gates"], below, above))
    grad_gates, grad_front, ends, head, sums = kept["gates"]
    from_next = lax.ppermute(head, dp, [(i + 1, i) for i in range(peers - 1)])
    middle_part, branch_sums = weight_grad(
        flat_one,
        tie(grad_branch_pre, head),
        width,
        2 * width,
        1,
        kept["middle"],
        front_weights,
        1,
    )
    from_next, middle_part = lax.optimization_barrier((from_next, middle_part))
    middle_half = lax.psum_scatter(
        tie(middle_part, feed_grads), dp[0], scatter_dimension=0, tiled=True
    )
    grad_front = lax.dynamic_update_slice(
        grad_front.reshape(spans, rows, seg, 2 * width),
        (ends + from_next).astype(bf16).reshape(1, rows, 8, width),
        (spans - 1, 0, seg - 8, 0),
    ).reshape(block_tokens, 2 * width)
    normed_got = swap_rows(grad_front)
    payload, input_sums = weight_grad(
        flat_one,
        grad_front,
        width,
        width,
        0,
        None,
        front_weights,
        0,
        1,
        peers=peers,
        more=small_rows,
    )
    payload, normed_got = lax.optimization_barrier((payload, normed_got))
    gain_one_part = jnp.sum(branch_sums + input_sums, axis=1) / gain_one
    gain_parts = jnp.stack([gain_one_part, gain_two_part]).reshape(2, spans // 2, 2, -1)
    gain_parts = gain_parts.transpose(2, 1, 0, 3)
    gain_keep = lax.dynamic_index_in_dim(gain_parts, core, 0, keepdims=False)
    gain_send = lax.dynamic_index_in_dim(gain_parts, 1 - core, 0, keepdims=False)
    gain_got = swap_cores(gain_send)
    normed_operands = (grad_front, normed_got, front_weights, front_other, 0)
    low, high, ahead, behind, normed_own = all_pieces(normed_operands)
    low, high, gain_got = lax.optimization_barrier((low, high, gain_got))

    def fill_payload(operand):
        payload_now, gain_sum, gates_now = operand
        table_grads = dot(gates_now, conv_low, 0, 0)

        def diagonal_back(turned):
            block_of = (jnp.arange(units) // block)[:, None]
            kept = turned[:units, :block]
            for h in range(1, blocks):
                kept = jnp.where(block_of == h, turned[:units, h * block : (h + 1) * block], kept)
            return kept

        small_grads = jnp.concatenate(
            [
                diagonal_back(table_grads[:width]),
                diagonal_back(table_grads[width:]),
                sums[:, :units].T,
            ],
            axis=1,
        )
        gain_parts = scatter_direct(gain_sum, "z")
        gain_share = model // spans // peers
        gain_parts = gain_parts.reshape(2, peers, gain_share).transpose(1, 0, 2)

        small_now = widen(small_grads, small_width, 1).reshape(peers, share, small_width)
        small_now = jnp.concatenate([small_now, widen(gain_parts, small_width, 2)], axis=1)
        payload = lax.dynamic_update_slice(payload_now, small_now.astype(bf16), (0, depth, 0))
        kept["payload"] = payload
        return payload

    from_below, from_above = ring_step(low, high, ((payload, gain_keep + gain_got, grad_gates), fill_payload))
    from_below, from_above, middle_half, payload = lax.optimization_barrier(
        (from_below, from_above, middle_half, kept["payload"])
    )
    middle_grad = lax.psum_scatter(middle_half, dp[1], scatter_dimension=0, tiled=True)

    kept["sent"] = lax.all_to_all(payload, dp, 0, 0)
    normed_below, normed_above = ring_step(*near_sums(ahead, behind, from_below, from_above), None)
    (tokens_grad,) = rows_call(
        tokens_body,
        (normed_own, normed_below, normed_above, tokens_own, grad_residual, gain_one[None]),
        [own_kind],
    )
    below, above = tie_all((below, above), tokens_grad)
    (layer_output,) = rows_call(feed_body, (feed_own, below, above, residual), [own_low])
    feed_grads = tie(feed_grads, normed_own).astype(f32)
    summed = jnp.sum(tie(kept["sent"], tokens_grad).astype(f32), axis=0)
    input_grad, small_grads = summed[:depth], summed[depth:]
    middle_grad = tie(middle_grad, summed).astype(f32)
    gain_share = model // spans // peers
    gain_grads = small_grads[share : share + 2, :gain_share]
    small_grads = small_grads[:share].T
    rate_slope = jax.nn.sigmoid(-decay_param.astype(f32)) * decay_power
    at = 2 * block
    return (
        layer_output.reshape(rows, seg, model),
        tokens_grad.reshape(rows, seg, model),
        gain_grads[0],
        gain_grads[1],
        middle_grad[:, width : width + units],
        input_grad[:, :units],
        middle_grad[:, :units].T,
        small_grads[:block],
        small_grads[block:at],
        small_grads[at : at + taps],
        small_grads[at + taps],
        small_grads[at + taps + 1],
        small_grads[at + taps + 2],
        small_grads[at + taps + 3] * rate_slope,
        feed_grads[:, :hidden_width],
        feed_grads[:, hidden_width : 2 * hidden_width],
        feed_grads[:, 2 * hidden_width :].T,
    )


def solution(mesh):
    peers, group = mesh.devices.shape
    side = 4
    split = Mesh(
        mesh.devices.reshape(side, peers // side, group // 2, 2), dp + ("z", "core")
    )
    tokens_spec = P(None, dp + ("z", "core"), None)
    split_units = P(None, ("z", "core") + dp)
    split_vector = P(("z", "core") + dp)
    rows_first, units_first = P(dp, ("z", "core")), P(("z", "core"), dp)
    return jax.shard_map(
        shards,
        mesh=split,
        in_specs=(tokens_spec, tokens_spec, P(), P(), rows_first, rows_first, units_first)
        + (split_units,) * 3
        + (split_vector,) * 4
        + (rows_first, rows_first, units_first, P()),
        out_specs=(tokens_spec, tokens_spec, split_vector, split_vector)
        + (rows_first, rows_first, units_first)
        + (split_units,) * 3
        + (split_vector,) * 4
        + (rows_first, rows_first, units_first),
        check_vma=False,
    )
```
